32 devices in a mesh: wide: 16 (over z, y, core), narrow: 2 (over x).
Axes of the slice: x: 2, y: 2, z: 4, core: 2. Of those that a mesh axis runs over, the one named last changes fastest.
Arguments:
- state: float32 [2, 4194304], P(None, ('wide', 'narrow')), may hold values from -6 to 6
- gate_re: float32 [6, 128, 128], replicated, may hold values from -0.375 to 0.375
- gate_im: float32 [6, 128, 128], replicated, may hold values from -0.375 to 0.375
- bit_orders: int32 [6, 8], replicated, may hold values from 0 to 7, each once within a row
- phase_pairs: int32 [6, 16, 2], replicated, may hold values from 0 to 11
- phase_angles: float32 [6, 16], replicated, may hold values from -3.140625 to 3.140625
Outputs:
- final_state: float32 [2, 4194304], P(None, ('wide', 'narrow'))
The draws below stay inside these ranges and needn't reach their ends.
Inputs may be any that keep to these rules, and one draw needn't show every extreme that they name: `bit_orders`: each row is a permutation of 0 to 7. `phase_pairs`: qubit positions among the lowest 12; the two of a pair may coincide.
All inputs are finite; a program needn't handle non-finite values.
Results may differ from the reference program's by a relative error of at most 0.00012.
Values sent between devices are 32-bit elements; how exact they have to be, the bound alone decides.
No kernel may reach another device: no remote copies, remote signals or barrier semaphores. Data moves between devices by JAX's collectives and lax.ppermute only.
A program may use at most 64 MiB of HBM per device.

```python
from functools import partial
import jax
import jax.numpy as jnp
from jax import lax

LAYERS = 6
GATE = 128
PHASES = 16
PHASE_BITS = 12
AMPS = 4194304
ROWS_HIGH = 256
LOW_SPAN = 16
N_WIDE = 16
N_NARROW = 2


def touch_ends(entries, own_key, least, largest):
    dims = entries.shape
    place = [jax.random.randint(jax.random.fold_in(own_key, axis), (), 0, dims[axis]) for axis in range(len(dims))]
    entries = entries.at[tuple(place)].set(least)
    longest = dims.index(max(dims))
    place[longest] = (place[longest] + 1) % dims[longest]
    return entries.at[tuple(place)].set(largest)


def steps_of(own_key, extent, split, least, top_value):
    loudness = 1.0
    for axis_at, blocks in split:
        heights = jax.random.uniform(jax.random.fold_in(jax.random.fold_in(own_key, 6), axis_at), (blocks,), jnp.float32, least / len(split), top_value / len(split))
        loudness = loudness * jnp.repeat(jnp.exp(heights), extent[axis_at] // blocks).reshape((-1,) + (1,) * (len(extent) - 1 - axis_at))
    return loudness


def normal_values(key, dims, deviation, most, shards=(), kind=jnp.bfloat16):
    gain = steps_of(key, dims, shards, -0.22, 0.18) if shards else 1.0
    drawn = jax.random.normal(key, dims, jnp.float32) * deviation * gain
    return jnp.minimum(jnp.maximum(drawn, -most), most).astype(kind)


def setup_inputs(seed: int = 0) -> dict:
    keys = jax.random.split(jax.random.key(seed), 7)
    state = normal_values(keys[0], (2, AMPS), 1.0, 6.0, ((1, 32),), jnp.float32)
    gate_re = normal_values(keys[1], (LAYERS, GATE, GATE), (2 * GATE) ** -0.5, 0.375, (), jnp.float32)
    gate_im = normal_values(keys[2], (LAYERS, GATE, GATE), (2 * GATE) ** -0.5, 0.375, (), jnp.float32)
    bit_orders = jax.vmap(lambda own: jax.random.permutation(own, 8))(jax.random.split(keys[3], LAYERS)).reshape((LAYERS, 8)).astype(jnp.int32)
    phase_pairs = touch_ends(jax.random.randint(keys[4], (LAYERS, PHASES, 2), 0, PHASE_BITS), jax.random.fold_in(keys[4], 1), 0, PHASE_BITS - 1).astype(jnp.int32)
    phase_angles = jnp.clip(jax.random.uniform(keys[5], (LAYERS, PHASES), jnp.float32, -3.140625, 3.140625), -3.140625, 3.140625)
    return dict(state=state, gate_re=gate_re, gate_im=gate_im, bit_orders=bit_orders, phase_pairs=phase_pairs, phase_angles=phase_angles)


def source_index(bit_order):
    position = jnp.arange(256, dtype=jnp.int32)
    source = jnp.zeros((256,), jnp.int32)
    for which in range(8):
        source = source + jnp.left_shift(jnp.right_shift(position, which) & 1, bit_order[which])
    return source


def complex_rows(left_re, left_im, right_re, right_im):
    product = partial(jnp.dot, preferred_element_type=jnp.float32, precision=lax.Precision.HIGHEST)
    real = product(left_re, right_re.T) - product(left_im, right_im.T)
    imag = product(left_re, right_im.T) + product(left_im, right_re.T)
    return real, imag


def apply_gates(blocks, bit_order, matrix_re, matrix_im):
    moved = jnp.take(blocks, source_index(bit_order), axis=2)
    halves = moved.reshape(2, -1, 128)
    real, imag = complex_rows(halves[0], halves[1], matrix_re, matrix_im)
    return jnp.stack([real, imag]).reshape(blocks.shape)


def phase_factors(pair_row, angle_row):
    position = jnp.arange(2 ** PHASE_BITS, dtype=jnp.int32)
    first = jnp.right_shift(position[None, :], pair_row[:, 0:1]) & 1
    second = jnp.right_shift(position[None, :], pair_row[:, 1:2]) & 1
    phase = jnp.sum(angle_row[:, None] * (first * second).astype(jnp.float32), axis=0)
    return jnp.cos(phase), jnp.sin(phase)


def apply_phase(amps, pair_row, angle_row):
    cosine, sine = phase_factors(pair_row, angle_row)
    view = amps.reshape(2, -1, 2 ** PHASE_BITS)
    real = view[0] * cosine - view[1] * sine
    imag = view[0] * sine + view[1] * cosine
    return jnp.stack([real, imag]).reshape(amps.shape)


def reference(state, gate_re, gate_im, bit_orders, phase_pairs, phase_angles):
    amps = state
    for layer in range(LAYERS):
        view = amps.reshape(2, N_WIDE, N_NARROW, ROWS_HIGH, N_NARROW, N_WIDE, LOW_SPAN)
        amps = view.transpose(0, 5, 4, 3, 2, 1, 6).reshape(2, -1)
        blocks = amps.reshape(2, -1, 256)
        amps = apply_gates(blocks, bit_orders[layer], gate_re[layer], gate_im[layer]).reshape(2, -1)
        amps = apply_phase(amps, phase_pairs[layer], phase_angles[layer])
    return amps
```

```python
from functools import partial

import jax
import jax.numpy as jnp
from jax import lax
from jax.experimental import pallas as pl
from jax.experimental.pallas import tpu as pltpu
from jax.sharding import PartitionSpec as P

LAYERS = 6
GATE = 128
LOW = 256
LOW_BITS = 8
PHASES = 16
PHASE_BITS = 12
LANES = 128


def split(x):
    high = x.astype(jnp.bfloat16)
    low = (x - high.astype(jnp.float32)).astype(jnp.bfloat16)
    return high, low


def tables_kernel(spect, narrow, order_ref, pair_ref, angle_ref, place_ref, re_ref, im_ref, high_ref, low_ref, turn_ref):
    layer = pl.program_id(0)

    t = lax.broadcasted_iota(jnp.int32, (LOW, LOW), 1)
    source = jnp.zeros((LOW, LOW), jnp.int32)
    for bit in range(LOW_BITS):
        source = source + lax.shift_left((t >> bit) & 1, jnp.full((LOW, LOW), order_ref[layer, bit], jnp.int32))
    hot = jnp.where(lax.broadcasted_iota(jnp.int32, (LOW, LOW), 0) == source, 1.0, 0.0).astype(jnp.bfloat16)
    contract = (((1,), (1,)), ((), ()))
    for part, gate in enumerate((re_ref[0], im_ref[0])):
        for out_ref, piece in zip((high_ref, low_ref), split(gate)):
            for e in range(2):
                moved = lax.dot_general(
                    hot[:, e * GATE : (e + 1) * GATE], piece, contract, preferred_element_type=jnp.float32
                ).astype(jnp.bfloat16)
                lanes = slice(e * GATE, (e + 1) * GATE)
                shifted = slice(LOW + e * GATE, LOW + (e + 1) * GATE)
                if part == 0:
                    out_ref[0, :LOW, lanes] = moved
                    out_ref[0, LOW:, shifted] = moved
                else:
                    out_ref[0, :LOW, shifted] = moved
                    out_ref[0, LOW:, lanes] = -moved

    row = lax.broadcasted_iota(jnp.int32, (spect, LOW), 0)
    lane = lax.broadcasted_iota(jnp.int32, (spect, LOW), 1)
    r = place_ref[0] * (spect // narrow) + row // narrow
    b = jnp.where(layer % 2 == 0, jnp.full((spect, LOW), place_ref[1], jnp.int32), row % narrow)
    u = ((r * narrow + b) * LOW + lane) & (2**PHASE_BITS - 1)
    phase = jnp.zeros((spect, LOW), jnp.float32)
    for gate in range(PHASES):
        first = u >> jnp.full((spect, LOW), pair_ref[layer, 2 * gate], jnp.int32)
        second = u >> jnp.full((spect, LOW), pair_ref[layer, 2 * gate + 1], jnp.int32)
        phase = phase + jnp.where((first & second & 1) == 1, angle_ref[layer, gate], 0.0)
    turn_ref[0, 0] = jnp.cos(phase)
    turn_ref[0, 1] = jnp.sin(phase)


def exchange_modes(rows, span):
    rows = list(rows)
    lane = lax.broadcasted_iota(jnp.int32, rows[0].shape, 1)
    step = 1
    while step < len(rows):
        shift = step * span
        upper = (lane & shift) != 0
        for m in range(len(rows)):
            if m & step:
                continue
            x0, x1 = rows[m], rows[m + step]
            if 2 * shift == LANES:
                crossing = pltpu.roll(jnp.where(upper, x0, x1), shift, 1)
                rows[m] = jnp.where(upper, crossing, x0)
                rows[m + step] = jnp.where(upper, x1, crossing)
            else:
                rows[m] = jnp.where(upper, pltpu.roll(x1, shift, 1), x0)
                rows[m + step] = jnp.where(upper, x1, pltpu.roll(x0, LANES - shift, 1))
        step *= 2
    return rows


def layers_kernel(wide, spect, x_ref, high_ref, low_ref, turn_ref, out_ref, state, left_high, left_low):
    layer = pl.program_id(0)
    count = wide * spect
    span = LOW // wide
    half = wide // 2

    @pl.when(layer == 0)
    def _():
        for part in range(2):
            for lanes in range(2):
                state[part, :, lanes * LANES : (lanes + 1) * LANES] = x_ref[pl.ds(2 * lanes + part, count, stride=4), :]

    for part in range(2):
        for top in range(2):
            for lanes in range(2):
                first = top * half * spect
                block = state[part, first : first + half * spect, lanes * LANES : (lanes + 1) * LANES]
                rows = exchange_modes([block[m * spect : (m + 1) * spect] for m in range(half)], span)
                for g in range(half):
                    at = (lanes * half + g) * spect
                    column = part * LOW + top * LANES
                    high, low = split(rows[g])
                    left_high[at : at + spect, column : column + LANES] = high
                    left_low[at : at + spect, column : column + LANES] = low

    cosine = turn_ref[0, 0][None]
    sine = turn_ref[0, 1][None]
    for block in range(2):
        rows = slice(block * half * spect, (block + 1) * half * spect)
        dot = partial(jnp.dot, preferred_element_type=jnp.float32)
        gated = dot(left_high[rows], high_ref[0])
        gated = gated + dot(left_low[rows], high_ref[0])
        gated = gated + dot(left_high[rows], low_ref[0])
        real = gated[:, :LOW].reshape(half, spect, LOW)
        imag = gated[:, LOW:].reshape(half, spect, LOW)
        state[0, rows] = (real * cosine - imag * sine).reshape(half * spect, LOW)
        state[1, rows] = (real * sine + imag * cosine).reshape(half * spect, LOW)

    @pl.when(layer == LAYERS - 1)
    def _():
        for part in range(2):
            for lanes in range(2):
                out_ref[pl.ds(2 * lanes + part, count, stride=4), :] = state[part, :, lanes * LANES : (lanes + 1) * LANES]


def local(state, gate_re, gate_im, bit_orders, phase_pairs, phase_angles):
    wide = lax.axis_size("wide")
    narrow = lax.axis_size("narrow")
    amps = state.shape[1]
    spect = amps // (wide * LOW)
    count = wide * spect

    rows = state.reshape(2, amps // LANES, LANES).transpose(1, 0, 2).reshape(2 * amps // LANES, LANES)
    gathered = lax.all_to_all(rows, "wide", split_axis=0, concat_axis=0, tiled=True)

    place = jnp.stack([lax.axis_index("wide"), lax.axis_index("narrow")]).astype(jnp.int32)
    smem = pl.BlockSpec(memory_space=pltpu.SMEM)
    gate_spec = pl.BlockSpec((1, GATE, GATE), lambda l: (l, 0, 0))
    square_spec = pl.BlockSpec((1, 2 * LOW, 2 * LOW), lambda l: (l, 0, 0))
    turn_spec = pl.BlockSpec((1, 2, spect, LOW), lambda l: (l, 0, 0, 0))
    square = jax.ShapeDtypeStruct((LAYERS, 2 * LOW, 2 * LOW), jnp.bfloat16)
    high, low, turn = pl.pallas_call(
        partial(tables_kernel, spect, narrow),
        grid=(LAYERS,),
        in_specs=[smem, smem, smem, smem, gate_spec, gate_spec],
        out_specs=[square_spec, square_spec, turn_spec],
        out_shape=[square, square, jax.ShapeDtypeStruct((LAYERS, 2, spect, LOW), jnp.float32)],
        cost_estimate=pl.CostEstimate(flops=10**9, bytes_accessed=8 * 10**6, transcendentals=10**5),
        name="tables",
    )(bit_orders, phase_pairs.reshape(LAYERS, 2 * PHASES), phase_angles, place, gate_re, gate_im)

    whole = pl.BlockSpec((4 * count, LANES), lambda l: (0, 0))
    done = pl.pallas_call(
        partial(layers_kernel, wide, spect),
        grid=(LAYERS,),
        in_specs=[whole, square_spec, square_spec, turn_spec],
        out_specs=whole,
        out_shape=jax.ShapeDtypeStruct((4 * count, LANES), jnp.float32),
        scratch_shapes=[
            pltpu.VMEM((2, count, LOW), jnp.float32),
            pltpu.VMEM((count, 2 * LOW), jnp.bfloat16),
            pltpu.VMEM((count, 2 * LOW), jnp.bfloat16),
        ],
        compiler_params=pltpu.CompilerParams(vmem_limit_bytes=32 * 2**20),
        cost_estimate=pl.CostEstimate(flops=5 * 10**9, bytes_accessed=10**7, transcendentals=0),
        name="layers",
    )(gathered, high, low, turn)

    back = lax.all_to_all(done, "wide", split_axis=0, concat_axis=0, tiled=True)
    return back.reshape(amps // LANES, 2, LANES).transpose(1, 0, 2).reshape(2, amps)


def solution(mesh):
    return jax.shard_map(
        local,
        mesh=mesh,
        in_specs=(P(None, ("wide", "narrow")), P(), P(), P(), P(), P()),
        out_specs=P(None, ("wide", "narrow")),
        check_vma=False,
    )
```

```python
from functools import partial

import jax
import jax.numpy as jnp
from jax import lax
from jax.experimental import pallas as pl
from jax.experimental.layout import Layout, with_layout_constraint
from jax.experimental.pallas import tpu as pltpu
from jax.sharding import PartitionSpec as P

LAYERS = 6
GATE = 128
LOW = 256
LOW_BITS = 8
PHASES = 16
PHASE_BITS = 12
LANES = 128
PAIRED = Layout(major_to_minor=(1, 0, 2))


def split(x):
    high = x.astype(jnp.bfloat16)
    low = (x - high.astype(jnp.float32)).astype(jnp.bfloat16)
    return high, low


def tables_kernel(spect, narrow, order_ref, pair_ref, angle_ref, place_ref, re_ref, im_ref, high_ref, low_ref, turn_ref):
    layer = pl.program_id(0)

    t = lax.broadcasted_iota(jnp.int32, (LOW, LOW), 1)
    source = jnp.zeros((LOW, LOW), jnp.int32)
    for bit in range(LOW_BITS):
        source = source + lax.shift_left((t >> bit) & 1, jnp.full((LOW, LOW), order_ref[layer, bit], jnp.int32))
    hot = jnp.where(lax.broadcasted_iota(jnp.int32, (LOW, LOW), 0) == source, 1.0, 0.0).astype(jnp.bfloat16)
    contract = (((1,), (1,)), ((), ()))
    for part, gate in enumerate((re_ref[0], im_ref[0])):
        for out_ref, piece in zip((high_ref, low_ref), split(gate)):
            for e in range(2):
                moved = lax.dot_general(
                    hot[:, e * GATE : (e + 1) * GATE], piece, contract, preferred_element_type=jnp.float32
                ).astype(jnp.bfloat16)
                lanes = slice(e * GATE, (e + 1) * GATE)
                shifted = slice(LOW + e * GATE, LOW + (e + 1) * GATE)
                if part == 0:
                    out_ref[0, :LOW, lanes] = moved
                    out_ref[0, LOW:, shifted] = moved
                else:
                    out_ref[0, :LOW, shifted] = moved
                    out_ref[0, LOW:, lanes] = -moved

    row = lax.broadcasted_iota(jnp.int32, (spect, LOW), 0)
    lane = lax.broadcasted_iota(jnp.int32, (spect, LOW), 1)
    r = place_ref[0] * (spect // narrow) + row // narrow
    b = jnp.where(layer % 2 == 0, jnp.full((spect, LOW), place_ref[1], jnp.int32), row % narrow)
    u = ((r * narrow + b) * LOW + lane) & (2**PHASE_BITS - 1)
    phase = jnp.zeros((spect, LOW), jnp.float32)
    for gate in range(PHASES):
        first = u >> jnp.full((spect, LOW), pair_ref[layer, 2 * gate], jnp.int32)
        second = u >> jnp.full((spect, LOW), pair_ref[layer, 2 * gate + 1], jnp.int32)
        phase = phase + jnp.where((first & second & 1) == 1, angle_ref[layer, gate], 0.0)
    turn_ref[0, 0] = jnp.cos(phase)
    turn_ref[0, 1] = jnp.sin(phase)


def exchange_modes(rows, span):
    rows = list(rows)
    lane = lax.broadcasted_iota(jnp.int32, rows[0].shape, 1)
    step = 1
    while step < len(rows):
        shift = step * span
        upper = (lane & shift) != 0
        for m in range(len(rows)):
            if m & step:
                continue
            x0, x1 = rows[m], rows[m + step]
            if 2 * shift == LANES:
                crossing = pltpu.roll(jnp.where(upper, x0, x1), shift, 1)
                rows[m] = jnp.where(upper, crossing, x0)
                rows[m + step] = jnp.where(upper, x1, crossing)
            else:
                rows[m] = jnp.where(upper, pltpu.roll(x1, shift, 1), x0)
                rows[m + step] = jnp.where(upper, x1, pltpu.roll(x0, LANES - shift, 1))
        step *= 2
    return rows


def layers_kernel(wide, spect, x_ref, high_ref, low_ref, turn_ref, out_ref, state, left_high, left_low):
    layer = pl.program_id(0)
    count = wide * spect
    span = LOW // wide
    half = wide // 2

    @pl.when(layer == 0)
    def _():
        for part in range(2):
            for lanes in range(2):
                state[part, :, lanes * LANES : (lanes + 1) * LANES] = x_ref[pl.ds(2 * lanes + part, count, stride=4), :]

    for part in range(2):
        for top in range(2):
            for lanes in range(2):
                first = top * half * spect
                block = state[part, first : first + half * spect, lanes * LANES : (lanes + 1) * LANES]
                rows = exchange_modes([block[m * spect : (m + 1) * spect] for m in range(half)], span)
                for g in range(half):
                    at = (lanes * half + g) * spect
                    column = part * LOW + top * LANES
                    high, low = split(rows[g])
                    left_high[at : at + spect, column : column + LANES] = high
                    left_low[at : at + spect, column : column + LANES] = low

    cosine = turn_ref[0, 0][None]
    sine = turn_ref[0, 1][None]
    for block in range(2):
        rows = slice(block * half * spect, (block + 1) * half * spect)
        dot = partial(jnp.dot, preferred_element_type=jnp.float32)
        gated = dot(left_high[rows], high_ref[0])
        gated = gated + dot(left_low[rows], high_ref[0])
        gated = gated + dot(left_high[rows], low_ref[0])
        real = gated[:, :LOW].reshape(half, spect, LOW)
        imag = gated[:, LOW:].reshape(half, spect, LOW)
        state[0, rows] = (real * cosine - imag * sine).reshape(half * spect, LOW)
        state[1, rows] = (real * sine + imag * cosine).reshape(half * spect, LOW)

    @pl.when(layer == LAYERS - 1)
    def _():
        for part in range(2):
            for lanes in range(2):
                out_ref[pl.ds(2 * lanes + part, count, stride=4), :] = state[part, :, lanes * LANES : (lanes + 1) * LANES]


def local(state, gate_re, gate_im, bit_orders, phase_pairs, phase_angles):
    wide = lax.axis_size("wide")
    narrow = lax.axis_size("narrow")
    amps = state.shape[1]
    spect = amps // (wide * LOW)
    count = wide * spect

    view = with_layout_constraint(state.reshape(2, amps // LANES, LANES), PAIRED)
    rows = view.transpose(1, 0, 2).reshape(2 * amps // LANES, LANES)
    gathered = lax.all_to_all(rows, "wide", split_axis=0, concat_axis=0, tiled=True)

    place = jnp.stack([lax.axis_index("wide"), lax.axis_index("narrow")]).astype(jnp.int32)
    smem = pl.BlockSpec(memory_space=pltpu.SMEM)
    gate_spec = pl.BlockSpec((1, GATE, GATE), lambda l: (l, 0, 0))
    square_spec = pl.BlockSpec((1, 2 * LOW, 2 * LOW), lambda l: (l, 0, 0))
    turn_spec = pl.BlockSpec((1, 2, spect, LOW), lambda l: (l, 0, 0, 0))
    square = jax.ShapeDtypeStruct((LAYERS, 2 * LOW, 2 * LOW), jnp.bfloat16)
    high, low, turn = pl.pallas_call(
        partial(tables_kernel, spect, narrow),
        grid=(LAYERS,),
        in_specs=[smem, smem, smem, smem, gate_spec, gate_spec],
        out_specs=[square_spec, square_spec, turn_spec],
        out_shape=[square, square, jax.ShapeDtypeStruct((LAYERS, 2, spect, LOW), jnp.float32)],
        compiler_params=pltpu.CompilerParams(vmem_limit_bytes=16 * 2**20),
        cost_estimate=pl.CostEstimate(flops=10**9, bytes_accessed=8 * 10**6, transcendentals=10**5),
        name="tables",
    )(bit_orders, phase_pairs.reshape(LAYERS, 2 * PHASES), phase_angles, place, gate_re, gate_im)

    whole = pl.BlockSpec((4 * count, LANES), lambda l: (0, 0))
    done = pl.pallas_call(
        partial(layers_kernel, wide, spect),
        grid=(LAYERS,),
        in_specs=[whole, square_spec, square_spec, turn_spec],
        out_specs=whole,
        out_shape=jax.ShapeDtypeStruct((4 * count, LANES), jnp.float32),
        scratch_shapes=[
            pltpu.VMEM((2, count, LOW), jnp.float32),
            pltpu.VMEM((count, 2 * LOW), jnp.bfloat16),
            pltpu.VMEM((count, 2 * LOW), jnp.bfloat16),
        ],
        compiler_params=pltpu.CompilerParams(vmem_limit_bytes=32 * 2**20),
        cost_estimate=pl.CostEstimate(flops=5 * 10**9, bytes_accessed=10**7, transcendentals=0),
        name="layers",
    )(gathered, high, low, turn)

    back = lax.all_to_all(done, "wide", split_axis=0, concat_axis=0, tiled=True)
    view = with_layout_constraint(back.reshape(amps // LANES, 2, LANES).transpose(1, 0, 2), PAIRED)
    return view.reshape(2, amps)


def solution(mesh):
    return jax.shard_map(
        local,
        mesh=mesh,
        in_specs=(P(None, ("wide", "narrow")), P(), P(), P(), P(), P()),
        out_specs=P(None, ("wide", "narrow")),
        check_vma=False,
    )
```

```python
from functools import partial

import jax
import jax.numpy as jnp
from jax import lax
from jax.experimental import pallas as pl
from jax.experimental.layout import Layout, with_layout_constraint
from jax.experimental.pallas import tpu as pltpu
from jax.sharding import PartitionSpec as P

LAYERS = 6
GATE = 128
LOW = 256
LOW_BITS = 8
PHASES = 16
PHASE_BITS = 12
LANES = 128
PACKED = 16
CHUNKS = 2
PAIRED = Layout(major_to_minor=(1, 0, 2))


def split(x):
    high = x.astype(jnp.bfloat16)
    low = (x - high.astype(jnp.float32)).astype(jnp.bfloat16)
    return high, low


def tables_kernel(spect, narrow, order_ref, pair_ref, angle_ref, place_ref, re_ref, im_ref, high_ref, low_ref, turn_ref):
    layer = pl.program_id(0)

    t = lax.broadcasted_iota(jnp.int32, (LOW, LOW), 1)
    source = jnp.zeros((LOW, LOW), jnp.int32)
    for bit in range(LOW_BITS):
        source = source + lax.shift_left((t >> bit) & 1, jnp.full((LOW, LOW), order_ref[layer, bit], jnp.int32))
    hot = jnp.where(lax.broadcasted_iota(jnp.int32, (LOW, LOW), 0) == source, 1.0, 0.0).astype(jnp.bfloat16)
    contract = (((1,), (1,)), ((), ()))
    for part, gate in enumerate((re_ref[0], im_ref[0])):
        for out_ref, piece in zip((high_ref, low_ref), split(gate)):
            for e in range(2):
                moved = lax.dot_general(
                    hot[:, e * GATE : (e + 1) * GATE], piece, contract, preferred_element_type=jnp.float32
                ).astype(jnp.bfloat16)
                lanes = slice(e * GATE, (e + 1) * GATE)
                shifted = slice(LOW + e * GATE, LOW + (e + 1) * GATE)
                if part == 0:
                    out_ref[0, :LOW, lanes] = moved
                    out_ref[0, LOW:, shifted] = moved
                else:
                    out_ref[0, :LOW, shifted] = moved
                    out_ref[0, LOW:, lanes] = -moved

    row = lax.broadcasted_iota(jnp.int32, (spect, LOW), 0)
    lane = lax.broadcasted_iota(jnp.int32, (spect, LOW), 1)
    r = place_ref[0] * (spect // narrow) + row // narrow
    b = jnp.where(layer % 2 == 0, jnp.full((spect, LOW), place_ref[1], jnp.int32), row % narrow)
    u = ((r * narrow + b) * LOW + lane) & (2**PHASE_BITS - 1)
    phase = jnp.zeros((spect, LOW), jnp.float32)
    for gate in range(PHASES):
        first = u >> jnp.full((spect, LOW), pair_ref[layer, 2 * gate], jnp.int32)
        second = u >> jnp.full((spect, LOW), pair_ref[layer, 2 * gate + 1], jnp.int32)
        phase = phase + jnp.where((first & second & 1) == 1, angle_ref[layer, gate], 0.0)
    turn_ref[0, 0] = jnp.cos(phase)
    turn_ref[0, 1] = jnp.sin(phase)


def exchange_modes(rows, span):
    rows = list(rows)
    lane = lax.broadcasted_iota(jnp.int32, rows[0].shape, 1)
    step = 1
    while step < len(rows):
        shift = step * span
        upper = (lane & shift) != 0
        for m in range(len(rows)):
            if m & step:
                continue
            x0, x1 = rows[m], rows[m + step]
            if 2 * shift == LANES:
                crossing = pltpu.roll(jnp.where(upper, x0, x1), shift, 1)
                rows[m] = jnp.where(upper, crossing, x0)
                rows[m + step] = jnp.where(upper, x1, crossing)
            else:
                rows[m] = jnp.where(upper, pltpu.roll(x1, shift, 1), x0)
                rows[m + step] = jnp.where(upper, x1, pltpu.roll(x0, LANES - shift, 1))
        step *= 2
    return rows


def layers_kernel(wide, spect, x_ref, high_ref, low_ref, turn_ref, out_ref, state, left_high, left_low):
    layer = pl.program_id(0)
    count = wide * spect
    span = LOW // wide
    half = wide // 2

    @pl.when(layer == 0)
    def _():
        for part in range(2):
            for lanes in range(2):
                state[part, :, lanes * LANES : (lanes + 1) * LANES] = x_ref[pl.ds(2 * lanes + part, count, stride=4), :]

    joined = max(1, PACKED // spect)
    for part in range(2):
        for top in range(2):
            for lanes in range(2):
                first = top * half * spect
                block = state[part, first : first + half * spect, lanes * LANES : (lanes + 1) * LANES]
                rows = exchange_modes([block[m * spect : (m + 1) * spect] for m in range(half)], span)
                for g in range(0, half, joined):
                    at = (lanes * half + g) * spect
                    column = part * LOW + top * LANES
                    high, low = split(jnp.concatenate(rows[g : g + joined], axis=0))
                    left_high[at : at + joined * spect, column : column + LANES] = high
                    left_low[at : at + joined * spect, column : column + LANES] = low

    cosine = turn_ref[0, 0][None]
    sine = turn_ref[0, 1][None]
    for block in range(2):
        rows = slice(block * half * spect, (block + 1) * half * spect)
        dot = partial(jnp.dot, preferred_element_type=jnp.float32)
        gated = dot(left_high[rows], high_ref[0])
        gated = gated + dot(left_low[rows], high_ref[0])
        gated = gated + dot(left_high[rows], low_ref[0])
        real = gated[:, :LOW].reshape(half, spect, LOW)
        imag = gated[:, LOW:].reshape(half, spect, LOW)
        state[0, rows] = (real * cosine - imag * sine).reshape(half * spect, LOW)
        state[1, rows] = (real * sine + imag * cosine).reshape(half * spect, LOW)

    @pl.when(layer == LAYERS - 1)
    def _():
        for part in range(2):
            for lanes in range(2):
                out_ref[pl.ds(2 * lanes + part, count, stride=4), :] = state[part, :, lanes * LANES : (lanes + 1) * LANES]


def local(state, gate_re, gate_im, bit_orders, phase_pairs, phase_angles):
    wide = lax.axis_size("wide")
    narrow = lax.axis_size("narrow")
    amps = state.shape[1]
    spect = amps // (CHUNKS * wide * LOW)
    count = wide * spect

    view = with_layout_constraint(state.reshape(2, amps // LANES, LANES), PAIRED)
    rows = view.transpose(1, 0, 2).reshape(CHUNKS, 4 * count, LANES)
    gathered = [
        lax.all_to_all(rows[chunk], "wide", split_axis=0, concat_axis=0, tiled=True) for chunk in range(CHUNKS)
    ]

    place = jnp.stack([lax.axis_index("wide"), lax.axis_index("narrow")]).astype(jnp.int32)
    smem = pl.BlockSpec(memory_space=pltpu.SMEM)
    gate_spec = pl.BlockSpec((1, GATE, GATE), lambda l: (l, 0, 0))
    square_spec = pl.BlockSpec((1, 2 * LOW, 2 * LOW), lambda l: (l, 0, 0))
    turn_spec = pl.BlockSpec((1, 2, spect, LOW), lambda l: (l, 0, 0, 0))
    square = jax.ShapeDtypeStruct((LAYERS, 2 * LOW, 2 * LOW), jnp.bfloat16)
    high, low, turn = pl.pallas_call(
        partial(tables_kernel, spect, narrow),
        grid=(LAYERS,),
        in_specs=[smem, smem, smem, smem, gate_spec, gate_spec],
        out_specs=[square_spec, square_spec, turn_spec],
        out_shape=[square, square, jax.ShapeDtypeStruct((LAYERS, 2, spect, LOW), jnp.float32)],
        compiler_params=pltpu.CompilerParams(vmem_limit_bytes=60 * 2**20),
        cost_estimate=pl.CostEstimate(flops=10**9, bytes_accessed=8 * 10**6, transcendentals=10**5),
        name="tables",
    )(bit_orders, phase_pairs.reshape(LAYERS, 2 * PHASES), phase_angles, place, gate_re, gate_im)

    whole = pl.BlockSpec((4 * count, LANES), lambda l: (0, 0))
    layers = pl.pallas_call(
        partial(layers_kernel, wide, spect),
        grid=(LAYERS,),
        in_specs=[whole, square_spec, square_spec, turn_spec],
        out_specs=whole,
        out_shape=jax.ShapeDtypeStruct((4 * count, LANES), jnp.float32),
        scratch_shapes=[
            pltpu.VMEM((2, count, LOW), jnp.float32),
            pltpu.VMEM((count, 2 * LOW), jnp.bfloat16),
            pltpu.VMEM((count, 2 * LOW), jnp.bfloat16),
        ],
        compiler_params=pltpu.CompilerParams(vmem_limit_bytes=60 * 2**20),
        cost_estimate=pl.CostEstimate(flops=5 * 10**9, bytes_accessed=10**7, transcendentals=0),
        name="layers",
    )
    back = []
    for chunk in range(CHUNKS):
        done = layers(gathered[chunk], high, low, turn)
        back.append(lax.all_to_all(done, "wide", split_axis=0, concat_axis=0, tiled=True))
    view = jnp.concatenate(back).reshape(amps // LANES, 2, LANES).transpose(1, 0, 2)
    return with_layout_constraint(view, PAIRED).reshape(2, amps)


def solution(mesh):
    return jax.shard_map(
        local,
        mesh=mesh,
        in_specs=(P(None, ("wide", "narrow")), P(), P(), P(), P(), P()),
        out_specs=P(None, ("wide", "narrow")),
        check_vma=False,
    )
```

```python
from functools import partial

import jax
import jax.numpy as jnp
from jax import lax
from jax.experimental import pallas as pl
from jax.experimental.layout import Layout, with_layout_constraint
from jax.experimental.pallas import tpu as pltpu
from jax.sharding import PartitionSpec as P

LAYERS = 6
GATE = 128
LOW = 256
LOW_BITS = 8
PHASES = 16
PHASE_BITS = 12
LANES = 128
PACKED = 16
PAIRED = Layout(major_to_minor=(1, 0, 2))


def split(x):
    high = x.astype(jnp.bfloat16)
    low = (x - high.astype(jnp.float32)).astype(jnp.bfloat16)
    return high, low


def tables_kernel(spect, narrow, order_ref, pair_ref, angle_ref, place_ref, re_ref, im_ref, gate_ref, turn_ref):
    layer = pl.program_id(0)

    t = lax.broadcasted_iota(jnp.int32, (LOW, LOW), 1)
    source = jnp.zeros((LOW, LOW), jnp.int32)
    for bit in range(LOW_BITS):
        source = source + lax.shift_left((t >> bit) & 1, jnp.full((LOW, LOW), order_ref[layer, bit], jnp.int32))
    hot = jnp.where(lax.broadcasted_iota(jnp.int32, (LOW, LOW), 0) == source, 1.0, 0.0).astype(jnp.bfloat16)
    contract = (((1,), (1,)), ((), ()))
    for part, gate in enumerate((re_ref[0], im_ref[0])):
        for which, piece in enumerate(split(gate)):
            for e in range(2):
                moved = lax.dot_general(
                    hot[:, e * GATE : (e + 1) * GATE], piece, contract, preferred_element_type=jnp.float32
                )
                start = part * LOW + e * GATE
                gate_ref[0, which, :, start : start + GATE] = moved.astype(jnp.bfloat16)

    row = lax.broadcasted_iota(jnp.int32, (spect, LOW), 0)
    lane = lax.broadcasted_iota(jnp.int32, (spect, LOW), 1)
    r = place_ref[0] * (spect // narrow) + row // narrow
    b = jnp.where(layer % 2 == 0, jnp.full((spect, LOW), place_ref[1], jnp.int32), row % narrow)
    u = ((r * narrow + b) * LOW + lane) & (2**PHASE_BITS - 1)
    phase = jnp.zeros((spect, LOW), jnp.float32)
    for gate in range(PHASES):
        first = u >> jnp.full((spect, LOW), pair_ref[layer, 2 * gate], jnp.int32)
        second = u >> jnp.full((spect, LOW), pair_ref[layer, 2 * gate + 1], jnp.int32)
        phase = phase + jnp.where((first & second & 1) == 1, angle_ref[layer, gate], 0.0)
    turn_ref[0, 0] = jnp.cos(phase)
    turn_ref[0, 1] = jnp.sin(phase)


def exchange_modes(rows, span):
    rows = list(rows)
    lane = lax.broadcasted_iota(jnp.int32, rows[0].shape, 1)
    step = 1
    while step < len(rows):
        shift = step * span
        upper = (lane & shift) != 0
        for m in range(len(rows)):
            if m & step:
                continue
            x0, x1 = rows[m], rows[m + step]
            if 2 * shift == LANES:
                crossing = pltpu.roll(jnp.where(upper, x0, x1), shift, 1)
                rows[m] = jnp.where(upper, crossing, x0)
                rows[m + step] = jnp.where(upper, x1, crossing)
            else:
                rows[m] = jnp.where(upper, pltpu.roll(x1, shift, 1), x0)
                rows[m + step] = jnp.where(upper, x1, pltpu.roll(x0, LANES - shift, 1))
        step *= 2
    return rows


def layers_kernel(
    wide, spect, x_hbm, gate_hbm, turn_hbm, out_hbm, x, gate, turn, state, left, x_sem, gate_sem, turn_sem, out_sem
):
    count = wide * spect
    span = LOW // wide
    half = wide // 2
    joined = max(1, PACKED // spect)
    block = 4 * spect

    x_copies = [
        pltpu.make_async_copy(x_hbm.at[pl.ds(m * block, block)], x.at[pl.ds(m * block, block)], x_sem.at[m])
        for m in range(wide)
    ]
    for copy in x_copies:
        copy.start()
    for layer in range(LAYERS):
        pltpu.make_async_copy(gate_hbm.at[layer], gate.at[layer], gate_sem.at[layer]).start()
        pltpu.make_async_copy(turn_hbm.at[layer], turn.at[layer], turn_sem.at[layer]).start()
    for copy in x_copies:
        copy.wait()

    for part in range(2):
        for lanes in range(2):
            state[part, :, lanes * LANES : (lanes + 1) * LANES] = x[pl.ds(2 * lanes + part, count, stride=4), :]

    def one_layer(layer, carry):
        for part in range(2):
            for top in range(2):
                for lanes in range(2):
                    first = top * half * spect
                    piece = state[part, first : first + half * spect, lanes * LANES : (lanes + 1) * LANES]
                    rows = exchange_modes([piece[m * spect : (m + 1) * spect] for m in range(half)], span)
                    for g in range(0, half, joined):
                        at = (lanes * half + g) * spect
                        high, low = split(jnp.concatenate(rows[g : g + joined], axis=0))
                        left[0, part, at : at + joined * spect, top * LANES : (top + 1) * LANES] = high
                        left[1, part, at : at + joined * spect, top * LANES : (top + 1) * LANES] = low

        pltpu.make_async_copy(gate_hbm.at[layer], gate.at[layer], gate_sem.at[layer]).wait()
        pltpu.make_async_copy(turn_hbm.at[layer], turn.at[layer], turn_sem.at[layer]).wait()
        cosine = turn[layer, 0][None]
        sine = turn[layer, 1][None]
        dot = partial(jnp.dot, preferred_element_type=jnp.float32)
        for part in range(2):
            rows = slice(part * half * spect, (part + 1) * half * spect)
            by_re, by_im = (
                dot(left[0, which, rows], gate[layer, 0])
                + dot(left[1, which, rows], gate[layer, 0])
                + dot(left[0, which, rows], gate[layer, 1])
                for which in range(2)
            )
            real = (by_re[:, :LOW] - by_im[:, LOW:]).reshape(half, spect, LOW)
            imag = (by_re[:, LOW:] + by_im[:, :LOW]).reshape(half, spect, LOW)
            state[0, rows] = (real * cosine - imag * sine).reshape(half * spect, LOW)
            state[1, rows] = (real * sine + imag * cosine).reshape(half * spect, LOW)
        return carry

    lax.fori_loop(0, LAYERS, one_layer, 0)

    for part in range(2):
        for lanes in range(2):
            x[pl.ds(2 * lanes + part, count, stride=4), :] = state[part, :, lanes * LANES : (lanes + 1) * LANES]
    out_copies = [
        pltpu.make_async_copy(x.at[pl.ds(m * block, block)], out_hbm.at[pl.ds(m * block, block)], out_sem.at[m])
        for m in range(wide)
    ]
    for copy in out_copies:
        copy.start()
    for copy in out_copies:
        copy.wait()


def local(state, gate_re, gate_im, bit_orders, phase_pairs, phase_angles):
    wide = lax.axis_size("wide")
    narrow = lax.axis_size("narrow")
    amps = state.shape[1]
    spect = amps // (wide * LOW)
    count = wide * spect

    view = with_layout_constraint(state.reshape(2, amps // LANES, LANES), PAIRED)
    rows = view.transpose(1, 0, 2).reshape(2 * amps // LANES, LANES)
    gathered = lax.all_to_all(rows, "wide", split_axis=0, concat_axis=0, tiled=True)

    place = jnp.stack([lax.axis_index("wide"), lax.axis_index("narrow")]).astype(jnp.int32)
    smem = pl.BlockSpec(memory_space=pltpu.SMEM)
    gate_spec = pl.BlockSpec((1, GATE, GATE), lambda l: (l, 0, 0))
    gates = (LAYERS, 2, LOW, 2 * LOW)
    turns = (LAYERS, 2, spect, LOW)
    gate, turn = pl.pallas_call(
        partial(tables_kernel, spect, narrow),
        grid=(LAYERS,),
        in_specs=[smem, smem, smem, smem, gate_spec, gate_spec],
        out_specs=[
            pl.BlockSpec((1,) + gates[1:], lambda l: (l, 0, 0, 0)),
            pl.BlockSpec((1,) + turns[1:], lambda l: (l, 0, 0, 0)),
        ],
        out_shape=[jax.ShapeDtypeStruct(gates, jnp.bfloat16), jax.ShapeDtypeStruct(turns, jnp.float32)],
        compiler_params=pltpu.CompilerParams(vmem_limit_bytes=60 * 2**20),
        cost_estimate=pl.CostEstimate(flops=10**9, bytes_accessed=8 * 10**6, transcendentals=10**5),
        name="tables",
    )(bit_orders, phase_pairs.reshape(LAYERS, 2 * PHASES), phase_angles, place, gate_re, gate_im)

    anywhere = pl.BlockSpec(memory_space=pl.ANY)
    done = pl.pallas_call(
        partial(layers_kernel, wide, spect),
        in_specs=[anywhere, anywhere, anywhere],
        out_specs=anywhere,
        out_shape=jax.ShapeDtypeStruct((4 * count, LANES), jnp.float32),
        scratch_shapes=[
            pltpu.VMEM((4 * count, LANES), jnp.float32),
            pltpu.VMEM(gates, jnp.bfloat16),
            pltpu.VMEM(turns, jnp.float32),
            pltpu.VMEM((2, count, LOW), jnp.float32),
            pltpu.VMEM((2, 2, count, LOW), jnp.bfloat16),
            pltpu.SemaphoreType.DMA((wide,)),
            pltpu.SemaphoreType.DMA((LAYERS,)),
            pltpu.SemaphoreType.DMA((LAYERS,)),
            pltpu.SemaphoreType.DMA((wide,)),
        ],
        compiler_params=pltpu.CompilerParams(vmem_limit_bytes=60 * 2**20),
        cost_estimate=pl.CostEstimate(flops=5 * 10**9, bytes_accessed=10**7, transcendentals=0),
        name="layers",
    )(gathered, gate, turn)

    back = lax.all_to_all(done, "wide", split_axis=0, concat_axis=0, tiled=True)
    view = with_layout_constraint(back.reshape(amps // LANES, 2, LANES).transpose(1, 0, 2), PAIRED)
    return view.reshape(2, amps)


def solution(mesh):
    return jax.shard_map(
        local,
        mesh=mesh,
        in_specs=(P(None, ("wide", "narrow")), P(), P(), P(), P(), P()),
        out_specs=P(None, ("wide", "narrow")),
        check_vma=False,
    )
```

```python
from functools import partial

import jax
import jax.numpy as jnp
from jax import lax
from jax.experimental import pallas as pl
from jax.experimental.layout import Layout, with_layout_constraint
from jax.experimental.pallas import tpu as pltpu
from jax.sharding import PartitionSpec as P

LAYERS = 6
GATE = 128
LOW = 256
LOW_BITS = 8
PHASES = 16
PHASE_BITS = 12
LANES = 128
PACKED = 16
PAIRED = Layout(major_to_minor=(1, 0, 2))


def split(x):
    high = x.astype(jnp.bfloat16)
    low = (x - high.astype(jnp.float32)).astype(jnp.bfloat16)
    return high, low


def tables_kernel(spect, narrow, order_ref, pair_ref, angle_ref, place_ref, re_ref, im_ref, gate_ref, turn_ref):
    layer = pl.program_id(0)

    t = lax.broadcasted_iota(jnp.int32, (LOW, LOW), 1)
    source = jnp.zeros((LOW, LOW), jnp.int32)
    for bit in range(LOW_BITS):
        source = source + lax.shift_left((t >> bit) & 1, jnp.full((LOW, LOW), order_ref[layer, bit], jnp.int32))
    hot = jnp.where(lax.broadcasted_iota(jnp.int32, (LOW, LOW), 0) == source, 1.0, 0.0).astype(jnp.bfloat16)
    contract = (((1,), (1,)), ((), ()))
    for part, gate in enumerate((re_ref[0], im_ref[0])):
        for which, piece in enumerate(split(gate)):
            for e in range(2):
                moved = lax.dot_general(
                    hot[:, e * GATE : (e + 1) * GATE], piece, contract, preferred_element_type=jnp.float32
                )
                start = part * LOW + e * GATE
                gate_ref[0, which, :, start : start + GATE] = moved.astype(jnp.bfloat16)

    row = lax.broadcasted_iota(jnp.int32, (spect, LOW), 0)
    lane = lax.broadcasted_iota(jnp.int32, (spect, LOW), 1)
    r = place_ref[0] * (spect // narrow) + row // narrow
    b = jnp.where(layer % 2 == 0, jnp.full((spect, LOW), place_ref[1], jnp.int32), row % narrow)
    u = ((r * narrow + b) * LOW + lane) & (2**PHASE_BITS - 1)
    phase = jnp.zeros((spect, LOW), jnp.float32)
    for gate in range(PHASES):
        first = u >> jnp.full((spect, LOW), pair_ref[layer, 2 * gate], jnp.int32)
        second = u >> jnp.full((spect, LOW), pair_ref[layer, 2 * gate + 1], jnp.int32)
        phase = phase + jnp.where((first & second & 1) == 1, angle_ref[layer, gate], 0.0)
    turn_ref[0, 0] = jnp.cos(phase)
    turn_ref[0, 1] = jnp.sin(phase)


def exchange_modes(rows, span):
    rows = list(rows)
    lane = lax.broadcasted_iota(jnp.int32, rows[0].shape, 1)
    step = 1
    while step < len(rows):
        shift = step * span
        upper = (lane & shift) != 0
        for m in range(len(rows)):
            if m & step:
                continue
            x0, x1 = rows[m], rows[m + step]
            if 2 * shift == LANES:
                crossing = pltpu.roll(jnp.where(upper, x0, x1), shift, 1)
                rows[m] = jnp.where(upper, crossing, x0)
                rows[m + step] = jnp.where(upper, x1, crossing)
            else:
                rows[m] = jnp.where(upper, pltpu.roll(x1, shift, 1), x0)
                rows[m + step] = jnp.where(upper, x1, pltpu.roll(x0, LANES - shift, 1))
        step *= 2
    return rows


def pick_kernel(wide, x_hbm, *rest):
    sends, sem = rest[:-1], rest[-1]
    me = lax.axis_index("wide")
    block = x_hbm.shape[0] // wide
    copies = [
        pltpu.make_async_copy(x_hbm.at[pl.ds((me ^ k) * block, block)], sends[k - 1], sem.at[k]) for k in range(1, wide)
    ]
    for copy in copies:
        copy.start()
    for copy in copies:
        copy.wait()


def place_kernel(wide, *rest):
    blocks, out_hbm, sem = rest[:wide], rest[wide], rest[wide + 1]
    me = lax.axis_index("wide")
    block = blocks[0].shape[0]
    copies = [
        pltpu.make_async_copy(blocks[k], out_hbm.at[pl.ds((me ^ k) * block, block)], sem.at[k]) for k in range(wide)
    ]
    for copy in copies:
        copy.start()
    for copy in copies:
        copy.wait()


def layers_kernel(wide, spect, x_hbm, *rest):
    received = rest[: wide - 1]
    gate_hbm, turn_hbm = rest[wide - 1 : wide + 1]
    outs = rest[wide + 1 : 2 * wide + 1]
    x, gate, turn, state, left, x_sem, gate_sem, turn_sem, out_sem = rest[2 * wide + 1 :]
    me = lax.axis_index("wide")
    count = wide * spect
    span = LOW // wide
    half = wide // 2
    joined = max(1, PACKED // spect)
    block = 4 * spect

    def rows_of(ref, k):
        return ref.at[pl.ds((me ^ k) * block, block)]

    x_copies = [
        pltpu.make_async_copy(received[k - 1] if k else rows_of(x_hbm, 0), rows_of(x, k), x_sem.at[k]) for k in range(wide)
    ]
    for copy in x_copies:
        copy.start()
    for layer in range(LAYERS):
        pltpu.make_async_copy(gate_hbm.at[layer], gate.at[layer], gate_sem.at[layer]).start()
        pltpu.make_async_copy(turn_hbm.at[layer], turn.at[layer], turn_sem.at[layer]).start()
    for copy in x_copies:
        copy.wait()

    for part in range(2):
        for lanes in range(2):
            state[part, :, lanes * LANES : (lanes + 1) * LANES] = x[pl.ds(2 * lanes + part, count, stride=4), :]

    def one_layer(layer, carry):
        for part in range(2):
            for top in range(2):
                for lanes in range(2):
                    first = top * half * spect
                    piece = state[part, first : first + half * spect, lanes * LANES : (lanes + 1) * LANES]
                    rows = exchange_modes([piece[m * spect : (m + 1) * spect] for m in range(half)], span)
                    for g in range(0, half, joined):
                        at = (lanes * half + g) * spect
                        high, low = split(jnp.concatenate(rows[g : g + joined], axis=0))
                        left[0, part, at : at + joined * spect, top * LANES : (top + 1) * LANES] = high
                        left[1, part, at : at + joined * spect, top * LANES : (top + 1) * LANES] = low

        pltpu.make_async_copy(gate_hbm.at[layer], gate.at[layer], gate_sem.at[layer]).wait()
        pltpu.make_async_copy(turn_hbm.at[layer], turn.at[layer], turn_sem.at[layer]).wait()
        cosine = turn[layer, 0][None]
        sine = turn[layer, 1][None]
        both = []
        for which in range(2):
            real, imag = gate[layer, which, :, :LOW], gate[layer, which, :, LOW:]
            both.append(jnp.concatenate([gate[layer, which], jnp.concatenate([-imag, real], axis=1)], axis=0))
        factors = jnp.concatenate([left[0, 0], left[0, 1], left[1, 0], left[1, 1], left[0, 0], left[0, 1]], axis=1)
        gated = jnp.dot(
            factors, jnp.concatenate([both[0], both[0], both[1]], axis=0), preferred_element_type=jnp.float32
        )
        real = gated[:, :LOW].reshape(wide, spect, LOW)
        imag = gated[:, LOW:].reshape(wide, spect, LOW)
        state[0] = (real * cosine - imag * sine).reshape(count, LOW)
        state[1] = (real * sine + imag * cosine).reshape(count, LOW)
        return carry

    lax.fori_loop(0, LAYERS, one_layer, 0)

    for part in range(2):
        for lanes in range(2):
            x[pl.ds(2 * lanes + part, count, stride=4), :] = state[part, :, lanes * LANES : (lanes + 1) * LANES]
    out_copies = [pltpu.make_async_copy(rows_of(x, k), outs[k], out_sem.at[k]) for k in range(wide)]
    for copy in out_copies:
        copy.start()
    for copy in out_copies:
        copy.wait()


def local(state, gate_re, gate_im, bit_orders, phase_pairs, phase_angles):
    wide = lax.axis_size("wide")
    narrow = lax.axis_size("narrow")
    amps = state.shape[1]
    spect = amps // (wide * LOW)
    count = wide * spect

    view = with_layout_constraint(state.reshape(2, amps // LANES, LANES), PAIRED)
    rows = view.transpose(1, 0, 2).reshape(2 * amps // LANES, LANES)
    anywhere = pl.BlockSpec(memory_space=pl.ANY)
    piece = jax.ShapeDtypeStruct((4 * spect, LANES), jnp.float32)
    part_of_vmem = pltpu.CompilerParams(vmem_limit_bytes=24 * 2**20)

    def swap(blocks):
        return [
            lax.ppermute(blocks[k - 1], "wide", [(i, i ^ k) for i in range(wide)]) for k in range(1, wide)
        ]

    sends = pl.pallas_call(
        partial(pick_kernel, wide),
        in_specs=[anywhere],
        out_specs=[anywhere] * (wide - 1),
        out_shape=[piece] * (wide - 1),
        scratch_shapes=[pltpu.SemaphoreType.DMA((wide,))],
        compiler_params=part_of_vmem,
        name="pick",
    )(rows)
    received = swap(sends)

    place = jnp.stack([lax.axis_index("wide"), lax.axis_index("narrow")]).astype(jnp.int32)
    smem = pl.BlockSpec(memory_space=pltpu.SMEM)
    gate_spec = pl.BlockSpec((1, GATE, GATE), lambda l: (l, 0, 0))
    gates = (LAYERS, 2, LOW, 2 * LOW)
    turns = (LAYERS, 2, spect, LOW)
    gate, turn = pl.pallas_call(
        partial(tables_kernel, spect, narrow),
        grid=(LAYERS,),
        in_specs=[smem, smem, smem, smem, gate_spec, gate_spec],
        out_specs=[
            pl.BlockSpec((1,) + gates[1:], lambda l: (l, 0, 0, 0)),
            pl.BlockSpec((1,) + turns[1:], lambda l: (l, 0, 0, 0)),
        ],
        out_shape=[jax.ShapeDtypeStruct(gates, jnp.bfloat16), jax.ShapeDtypeStruct(turns, jnp.float32)],
        compiler_params=part_of_vmem,
        cost_estimate=pl.CostEstimate(flops=10**9, bytes_accessed=8 * 10**6, transcendentals=10**5),
        name="tables",
    )(bit_orders, phase_pairs.reshape(LAYERS, 2 * PHASES), phase_angles, place, gate_re, gate_im)

    done = pl.pallas_call(
        partial(layers_kernel, wide, spect),
        in_specs=[anywhere] * (wide + 2),
        out_specs=[anywhere] * wide,
        out_shape=[piece] * wide,
        scratch_shapes=[
            pltpu.VMEM((4 * count, LANES), jnp.float32),
            pltpu.VMEM(gates, jnp.bfloat16),
            pltpu.VMEM(turns, jnp.float32),
            pltpu.VMEM((2, count, LOW), jnp.float32),
            pltpu.VMEM((2, 2, count, LOW), jnp.bfloat16),
            pltpu.SemaphoreType.DMA((wide,)),
            pltpu.SemaphoreType.DMA((LAYERS,)),
            pltpu.SemaphoreType.DMA((LAYERS,)),
            pltpu.SemaphoreType.DMA((wide,)),
        ],
        compiler_params=part_of_vmem,
        cost_estimate=pl.CostEstimate(flops=5 * 10**9, bytes_accessed=10**7, transcendentals=0),
        name="layers",
    )(rows, *received, gate, turn)

    back = pl.pallas_call(
        partial(place_kernel, wide),
        in_specs=[anywhere] * wide,
        out_specs=anywhere,
        out_shape=jax.ShapeDtypeStruct(rows.shape, jnp.float32),
        scratch_shapes=[pltpu.SemaphoreType.DMA((wide,))],
        compiler_params=part_of_vmem,
        name="place",
    )(done[0], *swap(done[1:]))
    view = with_layout_constraint(back.reshape(amps // LANES, 2, LANES).transpose(1, 0, 2), PAIRED)
    return view.reshape(2, amps)


def solution(mesh):
    return jax.shard_map(
        local,
        mesh=mesh,
        in_specs=(P(None, ("wide", "narrow")), P(), P(), P(), P(), P()),
        out_specs=P(None, ("wide", "narrow")),
        check_vma=False,
    )
```

```python
from functools import partial

import jax
import jax.numpy as jnp
from jax import lax
from jax.experimental import pallas as pl
from jax.experimental.layout import Layout, with_layout_constraint
from jax.experimental.pallas import tpu as pltpu
from jax.sharding import PartitionSpec as P

LAYERS = 6
GATE = 128
LOW = 256
LOW_BITS = 8
PHASES = 16
PHASE_BITS = 12
LANES = 128
PACKED = 16
PAIRED = Layout(major_to_minor=(1, 0, 2))


def split(x):
    high = x.astype(jnp.bfloat16)
    low = (x - high.astype(jnp.float32)).astype(jnp.bfloat16)
    return high, low


def tables_kernel(spect, narrow, order_ref, pair_ref, angle_ref, place_ref, re_ref, im_ref, high_ref, low_ref, turn_ref):
    layer = pl.program_id(0)

    t = lax.broadcasted_iota(jnp.int32, (LOW, LOW), 1)
    source = jnp.zeros((LOW, LOW), jnp.int32)
    for bit in range(LOW_BITS):
        source = source + lax.shift_left((t >> bit) & 1, jnp.full((LOW, LOW), order_ref[layer, bit], jnp.int32))
    hot = jnp.where(lax.broadcasted_iota(jnp.int32, (LOW, LOW), 0) == source, 1.0, 0.0).astype(jnp.bfloat16)
    contract = (((1,), (1,)), ((), ()))
    for part, gate in enumerate((re_ref[0], im_ref[0])):
        for out_ref, piece in zip((high_ref, low_ref), split(gate)):
            for e in range(2):
                moved = lax.dot_general(
                    hot[:, e * GATE : (e + 1) * GATE], piece, contract, preferred_element_type=jnp.float32
                ).astype(jnp.bfloat16)
                lanes = slice(e * GATE, (e + 1) * GATE)
                shifted = slice(LOW + e * GATE, LOW + (e + 1) * GATE)
                if part == 0:
                    out_ref[0, :LOW, lanes] = moved
                    out_ref[0, LOW:, shifted] = moved
                else:
                    out_ref[0, :LOW, shifted] = moved
                    out_ref[0, LOW:, lanes] = -moved

    row = lax.broadcasted_iota(jnp.int32, (spect, LOW), 0)
    lane = lax.broadcasted_iota(jnp.int32, (spect, LOW), 1)
    r = place_ref[0] * (spect // narrow) + row // narrow
    b = jnp.where(layer % 2 == 0, jnp.full((spect, LOW), place_ref[1], jnp.int32), row % narrow)
    u = ((r * narrow + b) * LOW + lane) & (2**PHASE_BITS - 1)
    phase = jnp.zeros((spect, LOW), jnp.float32)
    for gate in range(PHASES):
        first = u >> jnp.full((spect, LOW), pair_ref[layer, 2 * gate], jnp.int32)
        second = u >> jnp.full((spect, LOW), pair_ref[layer, 2 * gate + 1], jnp.int32)
        phase = phase + jnp.where((first & second & 1) == 1, angle_ref[layer, gate], 0.0)
    turn_ref[0, 0] = jnp.cos(phase)
    turn_ref[0, 1] = jnp.sin(phase)


def exchange_modes(rows, span):
    rows = list(rows)
    lane = lax.broadcasted_iota(jnp.int32, rows[0].shape, 1)
    step = 1
    while step < len(rows):
        shift = step * span
        upper = (lane & shift) != 0
        for m in range(len(rows)):
            if m & step:
                continue
            x0, x1 = rows[m], rows[m + step]
            if 2 * shift == LANES:
                crossing = pltpu.roll(jnp.where(upper, x0, x1), shift, 1)
                rows[m] = jnp.where(upper, crossing, x0)
                rows[m + step] = jnp.where(upper, x1, crossing)
            else:
                rows[m] = jnp.where(upper, pltpu.roll(x1, shift, 1), x0)
                rows[m + step] = jnp.where(upper, x1, pltpu.roll(x0, LANES - shift, 1))
        step *= 2
    return rows


def exchange_order(wide):
    order = [0]
    for far, near in zip(range(wide // 2, wide), list(range(wide // 2 - 1, 0, -1)) + [None]):
        order += [far] if near is None else [far, near]
    return order


def pick_kernel(wide, x_hbm, *rest):
    sends, sem = rest[:-1], rest[-1]
    me = lax.axis_index("wide")
    block = x_hbm.shape[0] // wide
    copies = [
        pltpu.make_async_copy(x_hbm.at[pl.ds((me ^ k) * block, block)], sends[i], sem.at[i])
        for i, k in enumerate(exchange_order(wide))
    ]
    for copy in copies:
        copy.start()
    for copy in copies:
        copy.wait()


def place_kernel(wide, *rest):
    blocks, out_hbm, sem = rest[:wide], rest[wide], rest[wide + 1]
    me = lax.axis_index("wide")
    block = blocks[0].shape[0]
    copies = [
        pltpu.make_async_copy(blocks[i], out_hbm.at[pl.ds((me ^ k) * block, block)], sem.at[i])
        for i, k in enumerate(exchange_order(wide))
    ]
    for copy in copies:
        copy.start()
    for copy in copies:
        copy.wait()


def layers_kernel(wide, spect, *rest):
    received = rest[:wide]
    high_ref, low_ref, turn_ref = rest[wide : wide + 3]
    outs = rest[wide + 3 : 2 * wide + 3]
    state, left_high, left_low = rest[2 * wide + 3 :]
    me = lax.axis_index("wide")
    span = LOW // wide
    half = wide // 2
    joined = max(1, PACKED // spect)

    for i, k in enumerate(exchange_order(wide)):
        rows = pl.ds(pl.multiple_of((me ^ k) * spect, spect), spect)
        for part in range(2):
            for lanes in range(2):
                state[part, rows, lanes * LANES : (lanes + 1) * LANES] = received[i][
                    pl.ds(2 * lanes + part, spect, stride=4), :
                ]

    def one_layer(layer, carry):
        for part in range(2):
            for top in range(2):
                for lanes in range(2):
                    first = top * half * spect
                    piece = state[part, first : first + half * spect, lanes * LANES : (lanes + 1) * LANES]
                    rows = exchange_modes([piece[m * spect : (m + 1) * spect] for m in range(half)], span)
                    for g in range(0, half, joined):
                        at = (lanes * half + g) * spect
                        column = part * LOW + top * LANES
                        high, low = split(jnp.concatenate(rows[g : g + joined], axis=0))
                        left_high[at : at + joined * spect, column : column + LANES] = high
                        left_low[at : at + joined * spect, column : column + LANES] = low

        cosine = turn_ref[layer, 0][None]
        sine = turn_ref[layer, 1][None]
        for block in range(2):
            rows = slice(block * half * spect, (block + 1) * half * spect)
            dot = partial(jnp.dot, preferred_element_type=jnp.float32)
            gated = dot(left_high[rows], high_ref[layer])
            gated = gated + dot(left_low[rows], high_ref[layer])
            gated = gated + dot(left_high[rows], low_ref[layer])
            real = gated[:, :LOW].reshape(half, spect, LOW)
            imag = gated[:, LOW:].reshape(half, spect, LOW)
            state[0, rows] = (real * cosine - imag * sine).reshape(half * spect, LOW)
            state[1, rows] = (real * sine + imag * cosine).reshape(half * spect, LOW)
        return carry

    lax.fori_loop(0, LAYERS, one_layer, 0)

    for i, k in enumerate(exchange_order(wide)):
        rows = pl.ds(pl.multiple_of((me ^ k) * spect, spect), spect)
        for part in range(2):
            for lanes in range(2):
                outs[i][pl.ds(2 * lanes + part, spect, stride=4), :] = state[
                    part, rows, lanes * LANES : (lanes + 1) * LANES
                ]


def local(state, gate_re, gate_im, bit_orders, phase_pairs, phase_angles):
    wide = lax.axis_size("wide")
    narrow = lax.axis_size("narrow")
    amps = state.shape[1]
    spect = amps // (wide * LOW)
    count = wide * spect

    view = with_layout_constraint(state.reshape(2, amps // LANES, LANES), PAIRED)
    rows = view.transpose(1, 0, 2).reshape(2 * amps // LANES, LANES)
    anywhere = pl.BlockSpec(memory_space=pl.ANY)
    piece = jax.ShapeDtypeStruct((4 * spect, LANES), jnp.float32)
    part_of_vmem = pltpu.CompilerParams(vmem_limit_bytes=24 * 2**20)

    def swap(blocks):
        arrived = [
            lax.ppermute(block, "wide", [(i, i ^ k) for i in range(wide)])
            for block, k in zip(blocks[1:], exchange_order(wide)[1:])
        ]
        return [blocks[0]] + arrived

    sends = pl.pallas_call(
        partial(pick_kernel, wide),
        in_specs=[anywhere],
        out_specs=[anywhere] * wide,
        out_shape=[piece] * wide,
        scratch_shapes=[pltpu.SemaphoreType.DMA((wide,))],
        compiler_params=pltpu.CompilerParams(vmem_limit_bytes=60 * 2**20),
        name="pick",
    )(rows)
    received = swap(sends)

    place = jnp.stack([lax.axis_index("wide"), lax.axis_index("narrow")]).astype(jnp.int32)
    smem = pl.BlockSpec(memory_space=pltpu.SMEM)
    gate_spec = pl.BlockSpec((1, GATE, GATE), lambda l: (l, 0, 0))
    square_spec = pl.BlockSpec((1, 2 * LOW, 2 * LOW), lambda l: (l, 0, 0))
    turn_spec = pl.BlockSpec((1, 2, spect, LOW), lambda l: (l, 0, 0, 0))
    square = jax.ShapeDtypeStruct((LAYERS, 2 * LOW, 2 * LOW), jnp.bfloat16)
    high, low, turn = pl.pallas_call(
        partial(tables_kernel, spect, narrow),
        grid=(LAYERS,),
        in_specs=[smem, smem, smem, smem, gate_spec, gate_spec],
        out_specs=[square_spec, square_spec, turn_spec],
        out_shape=[square, square, jax.ShapeDtypeStruct((LAYERS, 2, spect, LOW), jnp.float32)],
        compiler_params=part_of_vmem,
        cost_estimate=pl.CostEstimate(flops=10**9, bytes_accessed=8 * 10**6, transcendentals=10**5),
        name="tables",
    )(bit_orders, phase_pairs.reshape(LAYERS, 2 * PHASES), phase_angles, place, gate_re, gate_im)

    in_vmem = pl.BlockSpec(memory_space=pltpu.VMEM)
    done = pl.pallas_call(
        partial(layers_kernel, wide, spect),
        in_specs=[in_vmem] * (wide + 3),
        out_specs=[in_vmem] * wide,
        out_shape=[piece] * wide,
        scratch_shapes=[
            pltpu.VMEM((2, count, LOW), jnp.float32),
            pltpu.VMEM((count, 2 * LOW), jnp.bfloat16),
            pltpu.VMEM((count, 2 * LOW), jnp.bfloat16),
        ],
        compiler_params=part_of_vmem,
        cost_estimate=pl.CostEstimate(flops=5 * 10**9, bytes_accessed=10**7, transcendentals=0),
        name="layers",
    )(*received, high, low, turn)

    back = pl.pallas_call(
        partial(place_kernel, wide),
        in_specs=[anywhere] * wide,
        out_specs=anywhere,
        out_shape=jax.ShapeDtypeStruct(rows.shape, jnp.float32),
        scratch_shapes=[pltpu.SemaphoreType.DMA((wide,))],
        compiler_params=part_of_vmem,
        name="place",
    )(*swap(done))
    view = with_layout_constraint(back.reshape(amps // LANES, 2, LANES).transpose(1, 0, 2), PAIRED)
    return view.reshape(2, amps)


def solution(mesh):
    return jax.shard_map(
        local,
        mesh=mesh,
        in_specs=(P(None, ("wide", "narrow")), P(), P(), P(), P(), P()),
        out_specs=P(None, ("wide", "narrow")),
        check_vma=False,
    )
```

```python
from functools import partial

import jax
import jax.numpy as jnp
from jax import lax
from jax.experimental import pallas as pl
from jax.experimental.layout import Layout, with_layout_constraint
from jax.experimental.pallas import tpu as pltpu
from jax.sharding import PartitionSpec as P

LAYERS = 6
GATE = 128
LOW = 256
LOW_BITS = 8
PHASES = 16
PHASE_BITS = 12
LANES = 128
PACKED = 16
EARLY = 5
PAIRED = Layout(major_to_minor=(1, 0, 2))


def split(x):
    high = x.astype(jnp.bfloat16)
    low = (x - high.astype(jnp.float32)).astype(jnp.bfloat16)
    return high, low


def exchange_order(wide):
    far = list(range(wide // 2, wide, 2))
    near = [k for top in (wide // 4, wide // 8) for k in range(top, 2 * top, 2) if top > 1]
    near += [k for k in range(wide // 2 - 2, 0, -2) if k not in near]
    pairs = []
    for i, k in enumerate(far):
        pairs += [k] + near[i : i + 1] * (i < len(near) - 1)
    pairs += near[-1:]
    return [0] + [k + j for k in pairs for j in range(2)] + [1]


def block_of(ref, k, wide):
    rows = ref.shape[0] // wide
    start = (lax.axis_index("wide") ^ k) * rows
    return ref.at[pl.ds(pl.multiple_of(start, rows), rows)]


def pick_kernel(wide, ks, x_hbm, *rest):
    sends, sem = rest[:-1], rest[-1]
    copies = [pltpu.make_async_copy(block_of(x_hbm, k, wide), sends[i], sem.at[i]) for i, k in enumerate(ks)]
    for copy in copies:
        copy.start()
    for copy in copies:
        copy.wait()


def tables_kernel(wide, ks, spect, narrow, x_hbm, re_hbm, im_hbm, order_ref, pair_ref, angle_ref, *rest):
    sends = rest[: len(ks)]
    high_ref, low_ref, turn_ref, gates, block_sem, gate_sem = rest[len(ks) :]
    copies = [pltpu.make_async_copy(block_of(x_hbm, k, wide), sends[i], block_sem.at[i]) for i, k in enumerate(ks)]
    gate_copies = [
        pltpu.make_async_copy(hbm, gates.at[part], gate_sem.at[part]) for part, hbm in enumerate((re_hbm, im_hbm))
    ]
    for copy in gate_copies + copies:
        copy.start()

    row = lax.broadcasted_iota(jnp.int32, (spect, LOW), 0)
    lane = lax.broadcasted_iota(jnp.int32, (spect, LOW), 1)
    r = lax.axis_index("wide") * (spect // narrow) + row // narrow
    for layer in range(LAYERS):
        b = lax.axis_index("narrow") if layer % 2 == 0 else row % narrow
        u = ((r * narrow + b) * LOW + lane) & (2**PHASE_BITS - 1)
        phase = jnp.zeros((spect, LOW), jnp.float32)
        for gate in range(PHASES):
            first = u >> jnp.full((spect, LOW), pair_ref[layer, 0, gate], jnp.int32)
            second = u >> jnp.full((spect, LOW), pair_ref[layer, 1, gate], jnp.int32)
            phase = phase + jnp.where((first & second & 1) == 1, angle_ref[layer, gate], 0.0)
        turn_ref[layer, 0] = jnp.cos(phase)
        turn_ref[layer, 1] = jnp.sin(phase)

    for copy in gate_copies:
        copy.wait()
    t = lax.broadcasted_iota(jnp.int32, (8, LOW), 1)
    position = lax.broadcasted_iota(jnp.int32, (LOW // 8, 8, LOW), 0) * 8
    position = position + lax.broadcasted_iota(jnp.int32, (LOW // 8, 8, LOW), 1)
    contract = (((1,), (1,)), ((), ()))
    for layer in range(LAYERS):
        source = jnp.zeros((8, LOW), jnp.int32)
        for bit in range(LOW_BITS):
            source = source + (((t >> bit) & 1) << jnp.full((8, LOW), order_ref[layer, bit], jnp.int32))
        hot = jnp.where(position == source[None], 1.0, 0.0).reshape(LOW, LOW).astype(jnp.bfloat16)
        for part in range(2):
            for out_ref, piece in zip((high_ref, low_ref), split(gates[part, layer])):
                for e in range(2):
                    moved = lax.dot_general(
                        hot[:, e * GATE : (e + 1) * GATE], piece, contract, preferred_element_type=jnp.float32
                    ).astype(jnp.bfloat16)
                    lanes = slice(e * GATE, (e + 1) * GATE)
                    shifted = slice(LOW + e * GATE, LOW + (e + 1) * GATE)
                    if part == 0:
                        out_ref[layer, :LOW, lanes] = moved
                        out_ref[layer, LOW:, shifted] = moved
                    else:
                        out_ref[layer, :LOW, shifted] = moved
                        out_ref[layer, LOW:, lanes] = -moved
    for copy in copies:
        copy.wait()


def exchange_modes(rows, span):
    rows = list(rows)
    lane = lax.broadcasted_iota(jnp.int32, rows[0].shape, 1)
    step = 1
    while step < len(rows):
        shift = step * span
        upper = (lane & shift) != 0
        for m in range(len(rows)):
            if m & step:
                continue
            x0, x1 = rows[m], rows[m + step]
            if 2 * shift == LANES:
                crossing = pltpu.roll(jnp.where(upper, x0, x1), shift, 1)
                rows[m] = jnp.where(upper, crossing, x0)
                rows[m + step] = jnp.where(upper, x1, crossing)
            else:
                rows[m] = jnp.where(upper, pltpu.roll(x1, shift, 1), x0)
                rows[m + step] = jnp.where(upper, x1, pltpu.roll(x0, LANES - shift, 1))
        step *= 2
    return rows


def place_kernel(wide, *rest):
    blocks, out_hbm, sem = rest[:wide], rest[wide], rest[wide + 1]
    copies = [
        pltpu.make_async_copy(blocks[i], block_of(out_hbm, k, wide), sem.at[i])
        for i, k in enumerate(exchange_order(wide))
    ]
    for copy in copies:
        copy.start()
    for copy in copies:
        copy.wait()


def layers_kernel(wide, spect, *rest):
    received = rest[:wide]
    high_ref, low_ref, turn_ref = rest[wide : wide + 3]
    outs = rest[wide + 3 : 2 * wide + 3]
    state, left_high, left_low = rest[2 * wide + 3 :]
    me = lax.axis_index("wide")
    span = LOW // wide
    half = wide // 2
    joined = max(1, PACKED // spect)

    for i, k in enumerate(exchange_order(wide)):
        rows = pl.ds(pl.multiple_of((me ^ k) * spect, spect), spect)
        for part in range(2):
            for lanes in range(2):
                state[part, rows, lanes * LANES : (lanes + 1) * LANES] = received[i][
                    pl.ds(2 * lanes + part, spect, stride=4), :
                ]

    def one_layer(layer, carry):
        for part in range(2):
            for top in range(2):
                for lanes in range(2):
                    first = top * half * spect
                    piece = state[part, first : first + half * spect, lanes * LANES : (lanes + 1) * LANES]
                    rows = exchange_modes([piece[m * spect : (m + 1) * spect] for m in range(half)], span)
                    for g in range(0, half, joined):
                        at = (lanes * half + g) * spect
                        column = part * LOW + top * LANES
                        high, low = split(jnp.concatenate(rows[g : g + joined], axis=0))
                        left_high[at : at + joined * spect, column : column + LANES] = high
                        left_low[at : at + joined * spect, column : column + LANES] = low

        cosine = turn_ref[layer, 0][None]
        sine = turn_ref[layer, 1][None]
        for block in range(2):
            rows = slice(block * half * spect, (block + 1) * half * spect)
            dot = partial(jnp.dot, preferred_element_type=jnp.float32)
            gated = dot(left_high[rows], high_ref[layer])
            gated = gated + dot(left_low[rows], high_ref[layer])
            gated = gated + dot(left_high[rows], low_ref[layer])
            real = gated[:, :LOW].reshape(half, spect, LOW)
            imag = gated[:, LOW:].reshape(half, spect, LOW)
            state[0, rows] = (real * cosine - imag * sine).reshape(half * spect, LOW)
            state[1, rows] = (real * sine + imag * cosine).reshape(half * spect, LOW)
        return carry

    lax.fori_loop(0, LAYERS, one_layer, 0)

    for i, k in enumerate(exchange_order(wide)):
        rows = pl.ds(pl.multiple_of((me ^ k) * spect, spect), spect)
        for part in range(2):
            for lanes in range(2):
                outs[i][pl.ds(2 * lanes + part, spect, stride=4), :] = state[
                    part, rows, lanes * LANES : (lanes + 1) * LANES
                ]


def local(state, gate_re, gate_im, bit_orders, phase_pairs, phase_angles):
    wide = lax.axis_size("wide")
    narrow = lax.axis_size("narrow")
    amps = state.shape[1]
    spect = amps // (wide * LOW)
    count = wide * spect

    view = with_layout_constraint(state.reshape(2, amps // LANES, LANES), PAIRED)
    rows = view.transpose(1, 0, 2).reshape(2 * amps // LANES, LANES)
    in_hbm = pl.BlockSpec(memory_space=pltpu.HBM)
    in_vmem = pl.BlockSpec(memory_space=pltpu.VMEM)
    in_smem = pl.BlockSpec(memory_space=pltpu.SMEM)
    piece = jax.ShapeDtypeStruct((4 * spect, LANES), jnp.float32)
    part_of_vmem = pltpu.CompilerParams(vmem_limit_bytes=24 * 2**20)
    order = exchange_order(wide)
    early, late = order[1 : 1 + EARLY], order[1 + EARLY :] + order[:1]

    def swap(blocks, ks):
        return [
            lax.ppermute(block, "wide", [(i, i ^ k) for i in range(wide)]) if k else block
            for block, k in zip(blocks, ks)
        ]

    sends = pl.pallas_call(
        partial(pick_kernel, wide, early),
        in_specs=[in_hbm],
        out_specs=[in_vmem] * len(early),
        out_shape=[piece] * len(early),
        scratch_shapes=[pltpu.SemaphoreType.DMA((len(early),))],
        compiler_params=part_of_vmem,
        name="pick",
    )(rows)
    received = swap(sends, early)

    square = jax.ShapeDtypeStruct((LAYERS, 2 * LOW, 2 * LOW), jnp.bfloat16)
    *sends, high, low, turn = pl.pallas_call(
        partial(tables_kernel, wide, late, spect, narrow),
        in_specs=[in_hbm, in_hbm, in_hbm, in_smem, in_smem, in_smem],
        out_specs=[in_vmem] * (len(late) + 3),
        out_shape=[piece] * len(late)
        + [square, square, jax.ShapeDtypeStruct((LAYERS, 2, spect, LOW), jnp.float32)],
        scratch_shapes=[
            pltpu.VMEM((2,) + gate_re.shape, jnp.float32),
            pltpu.SemaphoreType.DMA((len(late),)),
            pltpu.SemaphoreType.DMA((2,)),
        ],
        compiler_params=part_of_vmem,
        cost_estimate=pl.CostEstimate(flops=10**9, bytes_accessed=8 * 10**6, transcendentals=10**5),
        name="tables",
    )(rows, gate_re, gate_im, bit_orders, phase_pairs.transpose(0, 2, 1), phase_angles)
    received = received + swap(sends, late)
    received = received[-1:] + received[:-1]

    done = pl.pallas_call(
        partial(layers_kernel, wide, spect),
        in_specs=[in_vmem] * (wide + 3),
        out_specs=[in_vmem] * wide,
        out_shape=[piece] * wide,
        scratch_shapes=[
            pltpu.VMEM((2, count, LOW), jnp.float32),
            pltpu.VMEM((count, 2 * LOW), jnp.bfloat16),
            pltpu.VMEM((count, 2 * LOW), jnp.bfloat16),
        ],
        compiler_params=part_of_vmem,
        cost_estimate=pl.CostEstimate(flops=5 * 10**9, bytes_accessed=10**7, transcendentals=0),
        name="layers",
    )(*received, high, low, turn)

    back = pl.pallas_call(
        partial(place_kernel, wide),
        in_specs=[in_vmem] * wide,
        out_specs=in_hbm,
        out_shape=jax.ShapeDtypeStruct(rows.shape, jnp.float32),
        scratch_shapes=[pltpu.SemaphoreType.DMA((wide,))],
        compiler_params=part_of_vmem,
        name="place",
    )(*swap(done, order))
    view = with_layout_constraint(back.reshape(amps // LANES, 2, LANES).transpose(1, 0, 2), PAIRED)
    return view.reshape(2, amps)


def solution(mesh):
    return jax.shard_map(
        local,
        mesh=mesh,
        in_specs=(P(None, ("wide", "narrow")), P(), P(), P(), P(), P()),
        out_specs=P(None, ("wide", "narrow")),
        check_vma=False,
    )
```

```python
from functools import partial

import jax
import jax.numpy as jnp
from jax import lax
from jax.experimental import pallas as pl
from jax.experimental.layout import Layout, with_layout_constraint
from jax.experimental.pallas import tpu as pltpu
from jax.sharding import PartitionSpec as P

LAYERS = 6
GATE = 128
LOW = 256
LOW_BITS = 8
PHASES = 16
PHASE_BITS = 12
LANES = 128
PACKED = 16
TILE = 128
PAIRED = Layout(major_to_minor=(1, 0, 2))


def split(x):
    high = x.astype(jnp.bfloat16)
    low = (x - high.astype(jnp.float32)).astype(jnp.bfloat16)
    return high, low


def exchange_order(wide):
    far = list(range(wide // 2, wide, 2))
    near = [k for top in (wide // 4, wide // 8) for k in range(top, 2 * top, 2) if top > 1]
    near += [k for k in range(wide // 2 - 2, 0, -2) if k not in near]
    pairs = []
    for i, k in enumerate(far):
        pairs += [k] + near[i : i + 1] * (i < len(near) - 1)
    pairs += near[-1:]
    return [0] + [k + j for k in pairs for j in range(2)] + [1]


def block_of(ref, k, wide):
    rows = ref.shape[0] // wide
    start = (lax.axis_index("wide") ^ k) * rows
    return ref.at[pl.ds(pl.multiple_of(start, rows), rows)]


def tables_kernel(spect, narrow, re_ref, im_ref, order_ref, pair_ref, angle_ref, gate_ref, turn_ref):
    row = lax.broadcasted_iota(jnp.int32, (spect, LOW), 0)
    lane = lax.broadcasted_iota(jnp.int32, (spect, LOW), 1)
    r = lax.axis_index("wide") * (spect // narrow) + row // narrow
    turn_ref[0, 0] = jnp.ones((spect, LOW), jnp.float32)
    turn_ref[0, 1] = jnp.zeros((spect, LOW), jnp.float32)
    for layer in range(LAYERS):
        b = lax.axis_index("narrow") if layer % 2 == 0 else row % narrow
        u = ((r * narrow + b) * LOW + lane) & (2**PHASE_BITS - 1)
        phase = jnp.zeros((spect, LOW), jnp.float32)
        for gate in range(PHASES):
            first = u >> jnp.full((spect, LOW), pair_ref[layer, 0, gate], jnp.int32)
            second = u >> jnp.full((spect, LOW), pair_ref[layer, 1, gate], jnp.int32)
            phase = phase + jnp.where((first & second & 1) == 1, angle_ref[layer, gate], 0.0)
        turn_ref[layer + 1, 0] = jnp.cos(phase)
        turn_ref[layer + 1, 1] = jnp.sin(phase)

    t = lax.broadcasted_iota(jnp.int32, (8, LOW), 1)
    position = lax.broadcasted_iota(jnp.int32, (LOW // 8, 8, LOW), 0) * 8
    position = position + lax.broadcasted_iota(jnp.int32, (LOW // 8, 8, LOW), 1)
    contract = (((1,), (1,)), ((), ()))
    for layer in range(LAYERS):
        source = jnp.zeros((8, LOW), jnp.int32)
        for bit in range(LOW_BITS):
            source = source + (((t >> bit) & 1) << jnp.full((8, LOW), order_ref[layer, bit], jnp.int32))
        hot = jnp.where(position == source[None], 1.0, 0.0).reshape(LOW, LOW).astype(jnp.bfloat16)
        for part, ref in enumerate((re_ref, im_ref)):
            for which, piece in enumerate(split(ref[layer])):
                for e in range(2):
                    moved = lax.dot_general(
                        hot[:, e * GATE : (e + 1) * GATE], piece, contract, preferred_element_type=jnp.float32
                    )
                    start = part * LOW + e * GATE
                    gate_ref[layer, which, :, start : start + GATE] = moved.astype(jnp.bfloat16)


def exchange_modes(rows, span):
    rows = list(rows)
    lane = lax.broadcasted_iota(jnp.int32, rows[0].shape, 1)
    step = 1
    while step < len(rows):
        shift = step * span
        upper = (lane & shift) != 0
        for m in range(len(rows)):
            if m & step:
                continue
            x0, x1 = rows[m], rows[m + step]
            if 2 * shift == LANES:
                crossing = pltpu.roll(jnp.where(upper, x0, x1), shift, 1)
                rows[m] = jnp.where(upper, crossing, x0)
                rows[m + step] = jnp.where(upper, x1, crossing)
            else:
                rows[m] = jnp.where(upper, pltpu.roll(x1, shift, 1), x0)
                rows[m + step] = jnp.where(upper, x1, pltpu.roll(x0, LANES - shift, 1))
        step *= 2
    return rows


def place_kernel(wide, *rest):
    blocks, out_hbm, sem = rest[:wide], rest[wide], rest[wide + 1]
    copies = [
        pltpu.make_async_copy(blocks[i], block_of(out_hbm, k, wide), sem.at[i])
        for i, k in enumerate(exchange_order(wide))
    ]
    for copy in copies:
        copy.start()
    for copy in copies:
        copy.wait()


def layers_kernel(wide, spect, x_hbm, gate_hbm, turn_hbm, *rest):
    outs = rest[:wide]
    x, gate, turn, state, left_high, left_low, minus_imag, x_sem, gate_sem, turn_sem, out_sem = rest[wide:]
    me = lax.axis_index("wide")
    count = wide * spect
    span = LOW // wide
    half = wide // 2
    rows_at_once = min(spect, PACKED)
    joined = PACKED // rows_at_once
    block = 4 * spect

    def gate_copy(layer):
        return pltpu.make_async_copy(gate_hbm.at[layer], gate.at[layer], gate_sem.at[layer])

    x_copies = [
        pltpu.make_async_copy(x_hbm.at[pl.ds(m * block, block)], x.at[pl.ds(m * block, block)], x_sem.at[m])
        for m in range(wide)
    ]
    turn_copy = pltpu.make_async_copy(turn_hbm, turn, turn_sem.at[0])
    for copy in x_copies:
        copy.start()
    turn_copy.start()
    for layer in range(LAYERS):
        gate_copy(layer).start()
    for m in range(wide):
        x_copies[m].wait()
        for part in range(2):
            for lanes in range(2):
                state[0, part, m * spect : (m + 1) * spect, lanes * LANES : (lanes + 1) * LANES] = x[
                    pl.ds(m * block + 2 * lanes + part, spect, stride=4), :
                ]
    turn_copy.wait()

    def turned(slot, entry, first, size, offset, lanes):
        rows, lanes = pl.ds(first + offset, size), slice(lanes * LANES, (lanes + 1) * LANES)
        real, imag = state[slot, 0, rows, lanes], state[slot, 1, rows, lanes]
        cosine, sine = turn[entry, 0, offset : offset + size, lanes], turn[entry, 1, offset : offset + size, lanes]
        return real * cosine - imag * sine, real * sine + imag * cosine

    def one_layer(layer, slot):
        gate_copy(layer).wait()
        for which in range(2):
            minus_imag[which] = -gate[layer, which, :, LOW:]

        for lanes in range(2):
            for top in range(2):
                for offset in range(0, spect, rows_at_once):
                    pieces = [
                        turned(slot, layer, (top * half + m) * spect, rows_at_once, offset, lanes) for m in range(half)
                    ]
                    for part in range(2):
                        rows = exchange_modes([piece[part] for piece in pieces], span)
                        column = part * LOW + top * LANES
                        for g in range(0, half, joined):
                            at = (lanes * half + g) * spect + offset
                            high, low = split(jnp.concatenate(rows[g : g + joined], axis=0))
                            left_high[at : at + PACKED, column : column + LANES] = high
                            left_low[at : at + PACKED, column : column + LANES] = low

        dot = partial(jnp.dot, preferred_element_type=jnp.float32)
        factors = []
        for which in range(2):
            real, imag = gate[layer, which, :, :LOW], gate[layer, which, :, LOW:]
            factors.append([[real, minus_imag[which]], [imag, real]])
        for first in range(0, count, TILE):
            rows = slice(first, first + TILE)
            for part in range(2):
                high = jnp.concatenate(factors[0][part], axis=0)
                low = jnp.concatenate(factors[1][part], axis=0)
                gated = dot(left_high[rows], high) + dot(left_low[rows], high) + dot(left_high[rows], low)
                state[1 - slot, part, rows] = gated

    def two_layers(step, carry):
        one_layer(2 * step, 0)
        one_layer(2 * step + 1, 1)
        return carry

    lax.fori_loop(0, LAYERS // 2, two_layers, 0)

    out_copies = []
    for i, k in enumerate(exchange_order(wide)):
        first = pl.multiple_of((me ^ k) * spect, spect)
        for lanes in range(2):
            for part, piece in enumerate(turned(0, LAYERS, first, spect, 0, lanes)):
                x[pl.ds(i * block + 2 * lanes + part, spect, stride=4), :] = piece
        out_copies.append(pltpu.make_async_copy(x.at[pl.ds(i * block, block)], outs[i], out_sem.at[i]))
        out_copies[-1].start()
    for copy in out_copies:
        copy.wait()


def local(state, gate_re, gate_im, bit_orders, phase_pairs, phase_angles):
    wide = lax.axis_size("wide")
    narrow = lax.axis_size("narrow")
    amps = state.shape[1]
    spect = amps // (wide * LOW)
    count = wide * spect

    view = with_layout_constraint(state.reshape(2, amps // LANES, LANES), PAIRED)
    rows = view.transpose(1, 0, 2).reshape(2 * amps // LANES, LANES)
    gathered = lax.all_to_all(rows, "wide", split_axis=0, concat_axis=0, tiled=True)

    in_hbm = pl.BlockSpec(memory_space=pltpu.HBM)
    in_vmem = pl.BlockSpec(memory_space=pltpu.VMEM)
    in_smem = pl.BlockSpec(memory_space=pltpu.SMEM)
    piece = jax.ShapeDtypeStruct((4 * spect, LANES), jnp.float32)
    all_of_vmem = pltpu.CompilerParams(vmem_limit_bytes=60 * 2**20)
    order = exchange_order(wide)

    gates = (LAYERS, 2, LOW, 2 * LOW)
    turns = (LAYERS + 1, 2, spect, LOW)
    gate, turn = pl.pallas_call(
        partial(tables_kernel, spect, narrow),
        in_specs=[in_vmem, in_vmem, in_smem, in_smem, in_smem],
        out_specs=[in_vmem, in_vmem],
        out_shape=[jax.ShapeDtypeStruct(gates, jnp.bfloat16), jax.ShapeDtypeStruct(turns, jnp.float32)],
        compiler_params=all_of_vmem,
        cost_estimate=pl.CostEstimate(flops=10**9, bytes_accessed=8 * 10**6, transcendentals=10**5),
        name="tables",
    )(gate_re, gate_im, bit_orders, phase_pairs.transpose(0, 2, 1), phase_angles)

    done = pl.pallas_call(
        partial(layers_kernel, wide, spect),
        in_specs=[in_hbm] * 3,
        out_specs=[in_hbm] * wide,
        out_shape=[piece] * wide,
        scratch_shapes=[
            pltpu.VMEM((4 * count, LANES), jnp.float32),
            pltpu.VMEM(gates, jnp.bfloat16),
            pltpu.VMEM(turns, jnp.float32),
            pltpu.VMEM((2, 2, count, LOW), jnp.float32),
            pltpu.VMEM((count, 2 * LOW), jnp.bfloat16),
            pltpu.VMEM((count, 2 * LOW), jnp.bfloat16),
            pltpu.VMEM((2, LOW, LOW), jnp.bfloat16),
            pltpu.SemaphoreType.DMA((wide,)),
            pltpu.SemaphoreType.DMA((LAYERS,)),
            pltpu.SemaphoreType.DMA((1,)),
            pltpu.SemaphoreType.DMA((wide,)),
        ],
        compiler_params=all_of_vmem,
        cost_estimate=pl.CostEstimate(flops=5 * 10**9, bytes_accessed=10**7, transcendentals=0),
        name="layers",
    )(gathered, gate, turn)

    def swap(blocks, ks):
        return [
            lax.ppermute(block, "wide", [(i, i ^ k) for i in range(wide)]) if k else block
            for block, k in zip(blocks, ks)
        ]

    back = pl.pallas_call(
        partial(place_kernel, wide),
        in_specs=[in_vmem] * wide,
        out_specs=in_hbm,
        out_shape=jax.ShapeDtypeStruct(rows.shape, jnp.float32),
        scratch_shapes=[pltpu.SemaphoreType.DMA((wide,))],
        compiler_params=pltpu.CompilerParams(vmem_limit_bytes=24 * 2**20),
        name="place",
    )(*swap(done, order))
    view = with_layout_constraint(back.reshape(amps // LANES, 2, LANES).transpose(1, 0, 2), PAIRED)
    return view.reshape(2, amps)


def solution(mesh):
    return jax.shard_map(
        local,
        mesh=mesh,
        in_specs=(P(None, ("wide", "narrow")), P(), P(), P(), P(), P()),
        out_specs=P(None, ("wide", "narrow")),
        check_vma=False,
    )
```

```python
from functools import partial

import jax
import jax.numpy as jnp
from jax import lax
from jax.experimental import pallas as pl
from jax.experimental.layout import Layout, with_layout_constraint
from jax.experimental.pallas import tpu as pltpu
from jax.sharding import PartitionSpec as P

LAYERS = 6
GATE = 128
LOW = 256
LOW_BITS = 8
PHASES = 16
PHASE_BITS = 12
LANES = 128
PACKED = 16
TILE = 128
PAIRED = Layout(major_to_minor=(1, 0, 2))


def split(x):
    high = x.astype(jnp.bfloat16)
    low = (x - high.astype(jnp.float32)).astype(jnp.bfloat16)
    return high, low


def exchange_order(wide):
    far = range(wide // 2, wide, 2)
    near = list(range(wide // 4, wide // 2, 2))
    near = [k for pair in zip(near, list(range(2, wide // 4, 2)) + [None]) for k in pair if k]
    pairs = [k for pair in zip(far, near) for k in pair]
    return [0] + [k + j for k in pairs for j in range(2)] + [1, wide - 2, wide - 1]


def block_of(ref, k, wide):
    rows = ref.shape[0] // wide
    start = (lax.axis_index("wide") ^ k) * rows
    return ref.at[pl.ds(pl.multiple_of(start, rows), rows)]


def tables_kernel(spect, narrow, re_ref, im_ref, order_ref, pair_ref, angle_ref, gate_ref, turn_ref):
    row = lax.broadcasted_iota(jnp.int32, (spect, LOW), 0)
    lane = lax.broadcasted_iota(jnp.int32, (spect, LOW), 1)
    r = lax.axis_index("wide") * (spect // narrow) + row // narrow
    for layer in range(LAYERS):
        b = lax.axis_index("narrow") if layer % 2 == 0 else row % narrow
        u = ((r * narrow + b) * LOW + lane) & (2**PHASE_BITS - 1)
        phase = jnp.zeros((spect, LOW), jnp.float32)
        for gate in range(PHASES):
            first = u >> jnp.full((spect, LOW), pair_ref[layer, 0, gate], jnp.int32)
            second = u >> jnp.full((spect, LOW), pair_ref[layer, 1, gate], jnp.int32)
            phase = phase + jnp.where((first & second & 1) == 1, angle_ref[layer, gate], 0.0)
        turn_ref[layer, 0] = jnp.cos(phase)
        turn_ref[layer, 1] = jnp.sin(phase)

    j = lax.broadcasted_iota(jnp.int32, (8, GATE), 1)
    position = lax.broadcasted_iota(jnp.int32, (GATE // 8, 8, GATE), 0) * 8
    position = position + lax.broadcasted_iota(jnp.int32, (GATE // 8, 8, GATE), 1)
    contract = (((1,), (1,)), ((), ()))
    top = LOW_BITS - 1
    for layer in range(LAYERS):
        source = jnp.zeros((8, GATE), jnp.int32)
        for bit in range(top):
            place = order_ref[layer, bit]
            place = jnp.where(place == top, order_ref[layer, top], place)
            source = source + (((j >> bit) & 1) << jnp.full((8, GATE), place, jnp.int32))
        hot = jnp.where(position == source[None], 1.0, 0.0).reshape(GATE, GATE).astype(jnp.bfloat16)
        for part, ref in enumerate((re_ref, im_ref)):
            for which, piece in enumerate(split(ref[layer])):
                moved = lax.dot_general(hot, piece, contract, preferred_element_type=jnp.float32)
                gate_ref[layer, which, :, part * GATE : (part + 1) * GATE] = moved.astype(jnp.bfloat16)


def exchange_modes(rows, span):
    rows = list(rows)
    lane = lax.broadcasted_iota(jnp.int32, rows[0].shape, 1)
    step = 1
    while step < len(rows):
        shift = step * span
        upper = (lane & shift) != 0
        for m in range(len(rows)):
            if m & step:
                continue
            x0, x1 = rows[m], rows[m + step]
            if 2 * shift == LANES:
                crossing = pltpu.roll(jnp.where(upper, x0, x1), shift, 1)
                rows[m] = jnp.where(upper, crossing, x0)
                rows[m + step] = jnp.where(upper, x1, crossing)
            else:
                rows[m] = jnp.where(upper, pltpu.roll(x1, shift, 1), x0)
                rows[m + step] = jnp.where(upper, x1, pltpu.roll(x0, LANES - shift, 1))
        step *= 2
    return rows


def place_kernel(wide, *rest):
    blocks, out_hbm, sem = rest[:wide], rest[wide], rest[wide + 1]
    copies = [
        pltpu.make_async_copy(blocks[i], block_of(out_hbm, k, wide), sem.at[i])
        for i, k in enumerate(exchange_order(wide))
    ]
    for copy in copies:
        copy.start()
    for copy in copies:
        copy.wait()


def exchange_top(x0, x1, shift):
    at = lax.broadcasted_iota(jnp.int32, x0.shape, 1) & shift
    back = (LANES - shift) & (LANES - 1)
    forth = shift & (LANES - 1)
    return jnp.where(at != 0, pltpu.roll(x1, forth, 1), x0), jnp.where(at == forth, x1, pltpu.roll(x0, back, 1))


def layers_kernel(wide, spect, order_ref, x, gate, turn, *rest):
    outs = rest[:wide]
    state, left_high, left_low, factor = rest[wide:]
    me = lax.axis_index("wide")
    count = wide * spect
    span = LOW // wide
    half = wide // 2
    rows_at_once = min(spect, PACKED)
    joined = PACKED // rows_at_once
    tile = min(TILE, count)

    for part in range(2):
        for lanes in range(2):
            state[0, part, :, lanes * LANES : (lanes + 1) * LANES] = x[pl.ds(2 * lanes + part, count, stride=4), :]

    def one_layer(layer, slot):
        for which in range(2):
            factor[which, :GATE] = gate[layer, which]
            factor[which, GATE:, :GATE] = -gate[layer, which, :, GATE:]
            factor[which, GATE:, GATE:] = gate[layer, which, :, :GATE]

        shift = jnp.int32(1) << order_ref[layer, LOW_BITS - 1]
        for lanes in range(2):
            for part in range(2):
                for offset in range(0, spect, rows_at_once):
                    tops = []
                    for top in range(2):
                        first = top * half * spect + offset
                        pieces = [
                            state[
                                slot,
                                part,
                                first + m * spect : first + m * spect + rows_at_once,
                                lanes * LANES : (lanes + 1) * LANES,
                            ]
                            for m in range(half)
                        ]
                        tops.append(exchange_modes(pieces, span))
                    for g in range(0, half, joined):
                        at = (lanes * half + g) * spect + offset
                        ends = [jnp.concatenate(rows[g : g + joined], axis=0) for rows in tops]
                        for e, piece in enumerate(exchange_top(*ends, shift)):
                            high, low = split(piece)
                            left_high[e, at : at + PACKED, part * LANES : (part + 1) * LANES] = high
                            left_low[e, at : at + PACKED, part * LANES : (part + 1) * LANES] = low

        dot = partial(jnp.dot, preferred_element_type=jnp.float32)
        for first in range(0, count, tile):
            rows = slice(first, first + tile)
            for e in range(2):
                gated = dot(left_high[e, rows], factor[0])
                gated = gated + dot(left_low[e, rows], factor[0])
                gated = gated + dot(left_high[e, rows], factor[1])
                real = gated[:, :LANES].reshape(tile // spect, spect, LANES)
                imag = gated[:, LANES:].reshape(tile // spect, spect, LANES)
                lanes = slice(e * LANES, (e + 1) * LANES)
                cosine, sine = turn[layer, 0, :, lanes][None], turn[layer, 1, :, lanes][None]
                state[1 - slot, 0, rows, lanes] = (real * cosine - imag * sine).reshape(tile, LANES)
                state[1 - slot, 1, rows, lanes] = (real * sine + imag * cosine).reshape(tile, LANES)

    def two_layers(step, carry):
        one_layer(2 * step, 0)
        one_layer(2 * step + 1, 1)
        return carry

    lax.fori_loop(0, LAYERS // 2, two_layers, 0)

    for i, k in enumerate(exchange_order(wide)):
        rows = pl.ds(pl.multiple_of((me ^ k) * spect, spect), spect)
        for part in range(2):
            for lanes in range(2):
                outs[i][pl.ds(2 * lanes + part, spect, stride=4), :] = state[
                    0, part, rows, lanes * LANES : (lanes + 1) * LANES
                ]


def local(state, gate_re, gate_im, bit_orders, phase_pairs, phase_angles):
    wide = lax.axis_size("wide")
    narrow = lax.axis_size("narrow")
    amps = state.shape[1]
    spect = amps // (wide * LOW)
    count = wide * spect

    view = with_layout_constraint(state.reshape(2, amps // LANES, LANES), PAIRED)
    rows = view.transpose(1, 0, 2).reshape(2 * amps // LANES, LANES)
    gathered = lax.all_to_all(rows, "wide", split_axis=0, concat_axis=0, tiled=True)

    in_hbm = pl.BlockSpec(memory_space=pltpu.HBM)
    in_vmem = pl.BlockSpec(memory_space=pltpu.VMEM)
    in_smem = pl.BlockSpec(memory_space=pltpu.SMEM)
    piece = jax.ShapeDtypeStruct((4 * spect, LANES), jnp.float32)
    part_of_vmem = pltpu.CompilerParams(vmem_limit_bytes=24 * 2**20)
    order = exchange_order(wide)

    gates = (LAYERS, 2, GATE, 2 * GATE)
    turns = (LAYERS, 2, spect, LOW)
    gate, turn = pl.pallas_call(
        partial(tables_kernel, spect, narrow),
        in_specs=[in_vmem, in_vmem, in_smem, in_smem, in_smem],
        out_specs=[in_vmem, in_vmem],
        out_shape=[jax.ShapeDtypeStruct(gates, jnp.bfloat16), jax.ShapeDtypeStruct(turns, jnp.float32)],
        compiler_params=part_of_vmem,
        cost_estimate=pl.CostEstimate(flops=10**9, bytes_accessed=8 * 10**6, transcendentals=10**5),
        name="tables",
    )(gate_re, gate_im, bit_orders, phase_pairs.transpose(0, 2, 1), phase_angles)

    done = pl.pallas_call(
        partial(layers_kernel, wide, spect),
        in_specs=[in_smem] + [in_vmem] * 3,
        out_specs=[in_vmem] * wide,
        out_shape=[piece] * wide,
        scratch_shapes=[
            pltpu.VMEM((2, 2, count, LOW), jnp.float32),
            pltpu.VMEM((2, count, 2 * LANES), jnp.bfloat16),
            pltpu.VMEM((2, count, 2 * LANES), jnp.bfloat16),
            pltpu.VMEM((2, 2 * GATE, 2 * GATE), jnp.bfloat16),
        ],
        compiler_params=part_of_vmem,
        cost_estimate=pl.CostEstimate(flops=5 * 10**9, bytes_accessed=10**7, transcendentals=0),
        name="layers",
    )(bit_orders, gathered, gate, turn)

    def swap(blocks, ks):
        return [
            lax.ppermute(block, "wide", [(i, i ^ k) for i in range(wide)]) if k else block
            for block, k in zip(blocks, ks)
        ]

    back = pl.pallas_call(
        partial(place_kernel, wide),
        in_specs=[in_vmem] * wide,
        out_specs=in_hbm,
        out_shape=jax.ShapeDtypeStruct(rows.shape, jnp.float32),
        scratch_shapes=[pltpu.SemaphoreType.DMA((wide,))],
        compiler_params=part_of_vmem,
        name="place",
    )(*swap(done, order))
    view = with_layout_constraint(back.reshape(amps // LANES, 2, LANES).transpose(1, 0, 2), PAIRED)
    return view.reshape(2, amps)


def solution(mesh):
    return jax.shard_map(
        local,
        mesh=mesh,
        in_specs=(P(None, ("wide", "narrow")), P(), P(), P(), P(), P()),
        out_specs=P(None, ("wide", "narrow")),
        check_vma=False,
    )
```

```python
from functools import partial

import jax
import jax.numpy as jnp
from jax import lax
from jax.experimental import pallas as pl
from jax.experimental.layout import Layout, with_layout_constraint
from jax.experimental.pallas import tpu as pltpu
from jax.sharding import PartitionSpec as P

LAYERS = 6
GATE = 128
LOW = 256
LOW_BITS = 8
PHASES = 16
PHASE_BITS = 12
LANES = 128
PACKED = 16
EARLY = 5
PAIRED = Layout(major_to_minor=(1, 0, 2))


def split(x):
    high = x.astype(jnp.bfloat16)
    low = (x - high.astype(jnp.float32)).astype(jnp.bfloat16)
    return high, low


def exchange_order(wide):
    far = list(range(wide // 2, wide))
    near = [k for low in (wide // 4, wide // 8, wide // 16) for k in range(low, 2 * low) if k]
    near += [k for k in range(wide // 2 - 1, 0, -1) if k not in near]
    order = [0] + far[:4]
    for i, k in enumerate(near):
        order += [k] + far[4 + i : 5 + i]
    return order + far[4 + len(near) :]


def block_of(ref, k, wide):
    rows = ref.shape[0] // wide
    start = (lax.axis_index("wide") ^ k) * rows
    return ref.at[pl.ds(pl.multiple_of(start, rows), rows)]


def pick_kernel(wide, ks, x_hbm, *rest):
    sends, sem = rest[:-1], rest[-1]
    copies = [pltpu.make_async_copy(block_of(x_hbm, k, wide), sends[i], sem.at[i]) for i, k in enumerate(ks)]
    for copy in copies:
        copy.start()
    for copy in copies:
        copy.wait()


def tables_kernel(wide, ks, spect, narrow, x_hbm, re_hbm, im_hbm, order_ref, pair_ref, angle_ref, *rest):
    sends = rest[: len(ks)]
    high_ref, low_ref, turn_ref, gates, block_sem, gate_sem = rest[len(ks) :]
    copies = [pltpu.make_async_copy(block_of(x_hbm, k, wide), sends[i], block_sem.at[i]) for i, k in enumerate(ks)]
    gate_copies = [
        pltpu.make_async_copy(hbm, gates.at[part], gate_sem.at[part]) for part, hbm in enumerate((re_hbm, im_hbm))
    ]
    for copy in gate_copies + copies:
        copy.start()

    row = lax.broadcasted_iota(jnp.int32, (spect, LOW), 0)
    lane = lax.broadcasted_iota(jnp.int32, (spect, LOW), 1)
    r = lax.axis_index("wide") * (spect // narrow) + row // narrow
    for layer in range(LAYERS):
        b = lax.axis_index("narrow") if layer % 2 == 0 else row % narrow
        u = ((r * narrow + b) * LOW + lane) & (2**PHASE_BITS - 1)
        phase = jnp.zeros((spect, LOW), jnp.float32)
        for gate in range(PHASES):
            first = u >> jnp.full((spect, LOW), pair_ref[layer, 0, gate], jnp.int32)
            second = u >> jnp.full((spect, LOW), pair_ref[layer, 1, gate], jnp.int32)
            phase = phase + jnp.where((first & second & 1) == 1, angle_ref[layer, gate], 0.0)
        turn_ref[layer, 0] = jnp.cos(phase)
        turn_ref[layer, 1] = jnp.sin(phase)

    for copy in gate_copies:
        copy.wait()
    t = lax.broadcasted_iota(jnp.int32, (8, LOW), 1)
    position = lax.broadcasted_iota(jnp.int32, (LOW // 8, 8, LOW), 0) * 8
    position = position + lax.broadcasted_iota(jnp.int32, (LOW // 8, 8, LOW), 1)
    contract = (((1,), (1,)), ((), ()))
    for layer in range(LAYERS):
        source = jnp.zeros((8, LOW), jnp.int32)
        for bit in range(LOW_BITS):
            source = source + (((t >> bit) & 1) << jnp.full((8, LOW), order_ref[layer, bit], jnp.int32))
        hot = jnp.where(position == source[None], 1.0, 0.0).reshape(LOW, LOW).astype(jnp.bfloat16)
        for part in range(2):
            for out_ref, piece in zip((high_ref, low_ref), split(gates[part, layer])):
                for e in range(2):
                    moved = lax.dot_general(
                        hot[:, e * GATE : (e + 1) * GATE], piece, contract, preferred_element_type=jnp.float32
                    ).astype(jnp.bfloat16)
                    lanes = slice(e * GATE, (e + 1) * GATE)
                    shifted = slice(LOW + e * GATE, LOW + (e + 1) * GATE)
                    if part == 0:
                        out_ref[layer, :LOW, lanes] = moved
                        out_ref[layer, LOW:, shifted] = moved
                    else:
                        out_ref[layer, :LOW, shifted] = moved
                        out_ref[layer, LOW:, lanes] = -moved
    for copy in copies:
        copy.wait()


def exchange_modes(rows, span):
    rows = list(rows)
    lane = lax.broadcasted_iota(jnp.int32, rows[0].shape, 1)
    step = 1
    while step < len(rows):
        shift = step * span
        upper = (lane & shift) != 0
        for m in range(len(rows)):
            if m & step:
                continue
            x0, x1 = rows[m], rows[m + step]
            if 2 * shift == LANES:
                crossing = pltpu.roll(jnp.where(upper, x0, x1), shift, 1)
                rows[m] = jnp.where(upper, crossing, x0)
                rows[m + step] = jnp.where(upper, x1, crossing)
            else:
                rows[m] = jnp.where(upper, pltpu.roll(x1, shift, 1), x0)
                rows[m + step] = jnp.where(upper, x1, pltpu.roll(x0, LANES - shift, 1))
        step *= 2
    return rows


def place_kernel(wide, *rest):
    blocks, out_hbm, sem = rest[:wide], rest[wide], rest[wide + 1]
    copies = [
        pltpu.make_async_copy(blocks[i], block_of(out_hbm, k, wide), sem.at[i])
        for i, k in enumerate(exchange_order(wide))
    ]
    for copy in copies:
        copy.start()
    for copy in copies:
        copy.wait()


def layers_kernel(wide, spect, *rest):
    received = rest[:wide]
    high_ref, low_ref, turn_ref = rest[wide : wide + 3]
    outs = rest[wide + 3 : 2 * wide + 3]
    state, left_high, left_low = rest[2 * wide + 3 :]
    me = lax.axis_index("wide")
    span = LOW // wide
    half = wide // 2
    joined = max(1, PACKED // spect)

    for i, k in enumerate(exchange_order(wide)):
        rows = pl.ds(pl.multiple_of((me ^ k) * spect, spect), spect)
        for part in range(2):
            for lanes in range(2):
                state[part, rows, lanes * LANES : (lanes + 1) * LANES] = received[i][
                    pl.ds(2 * lanes + part, spect, stride=4), :
                ]

    def one_layer(layer, carry):
        for part in range(2):
            for top in range(2):
                for lanes in range(2):
                    first = top * half * spect
                    piece = state[part, first : first + half * spect, lanes * LANES : (lanes + 1) * LANES]
                    rows = exchange_modes([piece[m * spect : (m + 1) * spect] for m in range(half)], span)
                    for g in range(0, half, joined):
                        at = (lanes * half + g) * spect
                        column = part * LOW + top * LANES
                        high, low = split(jnp.concatenate(rows[g : g + joined], axis=0))
                        left_high[at : at + joined * spect, column : column + LANES] = high
                        left_low[at : at + joined * spect, column : column + LANES] = low

        cosine = turn_ref[layer, 0][None]
        sine = turn_ref[layer, 1][None]
        for block in range(2):
            rows = slice(block * half * spect, (block + 1) * half * spect)
            dot = partial(jnp.dot, preferred_element_type=jnp.float32)
            gated = dot(left_high[rows], high_ref[layer])
            gated = gated + dot(left_low[rows], high_ref[layer])
            gated = gated + dot(left_high[rows], low_ref[layer])
            real = gated[:, :LOW].reshape(half, spect, LOW)
            imag = gated[:, LOW:].reshape(half, spect, LOW)
            state[0, rows] = (real * cosine - imag * sine).reshape(half * spect, LOW)
            state[1, rows] = (real * sine + imag * cosine).reshape(half * spect, LOW)
        return carry

    lax.fori_loop(0, LAYERS, one_layer, 0)

    for i, k in enumerate(exchange_order(wide)):
        rows = pl.ds(pl.multiple_of((me ^ k) * spect, spect), spect)
        for part in range(2):
            for lanes in range(2):
                outs[i][pl.ds(2 * lanes + part, spect, stride=4), :] = state[
                    part, rows, lanes * LANES : (lanes + 1) * LANES
                ]


def local(state, gate_re, gate_im, bit_orders, phase_pairs, phase_angles):
    wide = lax.axis_size("wide")
    narrow = lax.axis_size("narrow")
    amps = state.shape[1]
    spect = amps // (wide * LOW)
    count = wide * spect

    view = with_layout_constraint(state.reshape(2, amps // LANES, LANES), PAIRED)
    rows = view.transpose(1, 0, 2).reshape(2 * amps // LANES, LANES)
    in_hbm = pl.BlockSpec(memory_space=pltpu.HBM)
    in_vmem = pl.BlockSpec(memory_space=pltpu.VMEM)
    in_smem = pl.BlockSpec(memory_space=pltpu.SMEM)
    piece = jax.ShapeDtypeStruct((4 * spect, LANES), jnp.float32)
    part_of_vmem = pltpu.CompilerParams(vmem_limit_bytes=24 * 2**20)
    order = exchange_order(wide)
    early, late = order[1 : 1 + EARLY], order[1 + EARLY :] + order[:1]

    def swap(blocks, ks):
        return [
            lax.ppermute(block, "wide", [(i, i ^ k) for i in range(wide)]) if k else block
            for block, k in zip(blocks, ks)
        ]

    sends = pl.pallas_call(
        partial(pick_kernel, wide, early),
        in_specs=[in_hbm],
        out_specs=[in_vmem] * len(early),
        out_shape=[piece] * len(early),
        scratch_shapes=[pltpu.SemaphoreType.DMA((len(early),))],
        compiler_params=part_of_vmem,
        name="pick",
    )(rows)
    received = swap(sends, early)

    square = jax.ShapeDtypeStruct((LAYERS, 2 * LOW, 2 * LOW), jnp.bfloat16)
    *sends, high, low, turn = pl.pallas_call(
        partial(tables_kernel, wide, late, spect, narrow),
        in_specs=[in_hbm, in_hbm, in_hbm, in_smem, in_smem, in_smem],
        out_specs=[in_vmem] * (len(late) + 3),
        out_shape=[piece] * len(late)
        + [square, square, jax.ShapeDtypeStruct((LAYERS, 2, spect, LOW), jnp.float32)],
        scratch_shapes=[
            pltpu.VMEM((2,) + gate_re.shape, jnp.float32),
            pltpu.SemaphoreType.DMA((len(late),)),
            pltpu.SemaphoreType.DMA((2,)),
        ],
        compiler_params=part_of_vmem,
        cost_estimate=pl.CostEstimate(flops=10**9, bytes_accessed=8 * 10**6, transcendentals=10**5),
        name="tables",
    )(rows, gate_re, gate_im, bit_orders, phase_pairs.transpose(0, 2, 1), phase_angles)
    received = received + swap(sends, late)
    received = received[-1:] + received[:-1]

    done = pl.pallas_call(
        partial(layers_kernel, wide, spect),
        in_specs=[in_vmem] * (wide + 3),
        out_specs=[in_vmem] * wide,
        out_shape=[piece] * wide,
        scratch_shapes=[
            pltpu.VMEM((2, count, LOW), jnp.float32),
            pltpu.VMEM((count, 2 * LOW), jnp.bfloat16),
            pltpu.VMEM((count, 2 * LOW), jnp.bfloat16),
        ],
        compiler_params=part_of_vmem,
        cost_estimate=pl.CostEstimate(flops=5 * 10**9, bytes_accessed=10**7, transcendentals=0),
        name="layers",
    )(*received, high, low, turn)

    back = pl.pallas_call(
        partial(place_kernel, wide),
        in_specs=[in_vmem] * wide,
        out_specs=in_hbm,
        out_shape=jax.ShapeDtypeStruct(rows.shape, jnp.float32),
        scratch_shapes=[pltpu.SemaphoreType.DMA((wide,))],
        compiler_params=part_of_vmem,
        name="place",
    )(*swap(done, order))
    view = with_layout_constraint(back.reshape(amps // LANES, 2, LANES).transpose(1, 0, 2), PAIRED)
    return view.reshape(2, amps)


def solution(mesh):
    return jax.shard_map(
        local,
        mesh=mesh,
        in_specs=(P(None, ("wide", "narrow")), P(), P(), P(), P(), P()),
        out_specs=P(None, ("wide", "narrow")),
        check_vma=False,
    )
```

```python
from functools import partial

import jax
import jax.numpy as jnp
from jax import lax
from jax.experimental import pallas as pl
from jax.experimental.layout import Layout, with_layout_constraint
from jax.experimental.pallas import tpu as pltpu
from jax.sharding import PartitionSpec as P

LAYERS = 6
GATE = 128
LOW = 256
LOW_BITS = 8
PHASES = 16
PHASE_BITS = 12
LANES = 128
PACKED = 16
EARLY = 5
TILE = 128
PAIRED = Layout(major_to_minor=(1, 0, 2))


def split(x):
    high = x.astype(jnp.bfloat16)
    low = (x - high.astype(jnp.float32)).astype(jnp.bfloat16)
    return high, low


def exchange_order(wide):
    far = list(range(wide // 2, wide, 2))
    near = [k for top in (wide // 4, wide // 8) for k in range(top, 2 * top, 2) if top > 1]
    near += [k for k in range(wide // 2 - 2, 0, -2) if k not in near]
    pairs = []
    for i, k in enumerate(far):
        pairs += [k] + near[i : i + 1] * (i < len(near) - 1)
    pairs += near[-1:]
    return [0] + [k + j for k in pairs for j in range(2)] + [1]


def block_of(ref, k, wide):
    rows = ref.shape[0] // wide
    start = (lax.axis_index("wide") ^ k) * rows
    return ref.at[pl.ds(pl.multiple_of(start, rows), rows)]


def pick_kernel(wide, ks, x_hbm, *rest):
    sends, sem = rest[:-1], rest[-1]
    copies = [pltpu.make_async_copy(block_of(x_hbm, k, wide), sends[i], sem.at[i]) for i, k in enumerate(ks)]
    for copy in copies:
        copy.start()
    for copy in copies:
        copy.wait()


def tables_kernel(wide, ks, spect, narrow, x_hbm, re_hbm, im_hbm, order_ref, pair_ref, angle_ref, *rest):
    sends = rest[: len(ks)]
    gate_ref, turn_ref, gates, block_sem, gate_sem = rest[len(ks) :]
    copies = [pltpu.make_async_copy(block_of(x_hbm, k, wide), sends[i], block_sem.at[i]) for i, k in enumerate(ks)]
    gate_copies = [
        pltpu.make_async_copy(hbm, gates.at[part], gate_sem.at[part]) for part, hbm in enumerate((re_hbm, im_hbm))
    ]
    for copy in gate_copies + copies:
        copy.start()

    row = lax.broadcasted_iota(jnp.int32, (spect, LOW), 0)
    lane = lax.broadcasted_iota(jnp.int32, (spect, LOW), 1)
    r = lax.axis_index("wide") * (spect // narrow) + row // narrow
    turn_ref[0, 0] = jnp.ones((spect, LOW), jnp.float32)
    turn_ref[0, 1] = jnp.zeros((spect, LOW), jnp.float32)
    for layer in range(LAYERS):
        b = lax.axis_index("narrow") if layer % 2 == 0 else row % narrow
        u = ((r * narrow + b) * LOW + lane) & (2**PHASE_BITS - 1)
        phase = jnp.zeros((spect, LOW), jnp.float32)
        for gate in range(PHASES):
            first = u >> jnp.full((spect, LOW), pair_ref[layer, 0, gate], jnp.int32)
            second = u >> jnp.full((spect, LOW), pair_ref[layer, 1, gate], jnp.int32)
            phase = phase + jnp.where((first & second & 1) == 1, angle_ref[layer, gate], 0.0)
        turn_ref[layer + 1, 0] = jnp.cos(phase)
        turn_ref[layer + 1, 1] = jnp.sin(phase)

    for copy in gate_copies:
        copy.wait()
    t = lax.broadcasted_iota(jnp.int32, (8, LOW), 1)
    position = lax.broadcasted_iota(jnp.int32, (LOW // 8, 8, LOW), 0) * 8
    position = position + lax.broadcasted_iota(jnp.int32, (LOW // 8, 8, LOW), 1)
    contract = (((1,), (1,)), ((), ()))
    for layer in range(LAYERS):
        source = jnp.zeros((8, LOW), jnp.int32)
        for bit in range(LOW_BITS):
            source = source + (((t >> bit) & 1) << jnp.full((8, LOW), order_ref[layer, bit], jnp.int32))
        hot = jnp.where(position == source[None], 1.0, 0.0).reshape(LOW, LOW).astype(jnp.bfloat16)
        for part in range(2):
            for which, piece in enumerate(split(gates[part, layer])):
                for e in range(2):
                    moved = lax.dot_general(
                        hot[:, e * GATE : (e + 1) * GATE], piece, contract, preferred_element_type=jnp.float32
                    )
                    start = part * LOW + e * GATE
                    gate_ref[layer, which, :, start : start + GATE] = moved.astype(jnp.bfloat16)
    for copy in copies:
        copy.wait()


def exchange_modes(rows, span):
    count = len(rows)
    group = lax.broadcasted_iota(jnp.int32, rows[0].shape, 1) // span
    rows = [pltpu.roll(row, m * span, 1) if m else row for m, row in enumerate(rows)]
    step = 1
    while step < count:
        taken = (group & step) != 0
        rows = [jnp.where(taken, rows[(y + step) % count], rows[y]) for y in range(count)]
        step *= 2
    return [pltpu.roll(rows[-r % count], LANES - r * span, 1) if r else rows[0] for r in range(count)]


def place_kernel(wide, *rest):
    blocks, out_hbm, sem = rest[:wide], rest[wide], rest[wide + 1]
    copies = [
        pltpu.make_async_copy(blocks[i], block_of(out_hbm, k, wide), sem.at[i])
        for i, k in enumerate(exchange_order(wide))
    ]
    for copy in copies:
        copy.start()
    for copy in copies:
        copy.wait()


def layers_kernel(wide, spect, *rest):
    received = rest[:wide]
    gate, turn = rest[wide : wide + 2]
    outs = rest[wide + 2 : 2 * wide + 2]
    state, left_high, left_low, minus_imag = rest[2 * wide + 2 :]
    me = lax.axis_index("wide")
    count = wide * spect
    span = LOW // wide
    half = wide // 2
    rows_at_once = min(spect, PACKED)
    joined = PACKED // rows_at_once
    tile = min(TILE, count)

    for i, k in enumerate(exchange_order(wide)):
        rows = pl.ds(pl.multiple_of((me ^ k) * spect, spect), spect)
        for part in range(2):
            for lanes in range(2):
                state[0, part, rows, lanes * LANES : (lanes + 1) * LANES] = received[i][
                    pl.ds(2 * lanes + part, spect, stride=4), :
                ]

    def turned(slot, entry, first, size, offset, lanes):
        rows, lanes = pl.ds(first + offset, size), slice(lanes * LANES, (lanes + 1) * LANES)
        real, imag = state[slot, 0, rows, lanes], state[slot, 1, rows, lanes]
        cosine, sine = turn[entry, 0, offset : offset + size, lanes], turn[entry, 1, offset : offset + size, lanes]
        return real * cosine - imag * sine, real * sine + imag * cosine

    def one_layer(layer, slot):
        for which in range(2):
            minus_imag[which] = -gate[layer, which, :, LOW:]

        for lanes in range(2):
            for top in range(2):
                for offset in range(0, spect, rows_at_once):
                    pieces = [
                        turned(slot, layer, (top * half + m) * spect, rows_at_once, offset, lanes) for m in range(half)
                    ]
                    for part in range(2):
                        rows = exchange_modes([piece[part] for piece in pieces], span)
                        column = part * LOW + top * LANES
                        for g in range(0, half, joined):
                            at = (lanes * half + g) * spect + offset
                            high, low = split(jnp.concatenate(rows[g : g + joined], axis=0))
                            left_high[at : at + PACKED, column : column + LANES] = high
                            left_low[at : at + PACKED, column : column + LANES] = low

        factors = []
        for which in range(2):
            real, imag = gate[layer, which, :, :LOW], gate[layer, which, :, LOW:]
            factors.append([[real, minus_imag[which]], [imag, real]])
        for first in range(0, count, tile):
            rows = slice(first, first + tile)
            terms = jnp.concatenate([left_high[rows], left_low[rows], left_high[rows]], axis=1)
            for part in range(2):
                square = jnp.concatenate(factors[0][part] + factors[0][part] + factors[1][part], axis=0)
                state[1 - slot, part, rows] = jnp.dot(terms, square, preferred_element_type=jnp.float32)

    def two_layers(step, carry):
        one_layer(2 * step, 0)
        one_layer(2 * step + 1, 1)
        return carry

    lax.fori_loop(0, LAYERS // 2, two_layers, 0)

    for i, k in enumerate(exchange_order(wide)):
        first = pl.multiple_of((me ^ k) * spect, spect)
        for lanes in range(2):
            for part, piece in enumerate(turned(0, LAYERS, first, spect, 0, lanes)):
                outs[i][pl.ds(2 * lanes + part, spect, stride=4), :] = piece


def local(state, gate_re, gate_im, bit_orders, phase_pairs, phase_angles):
    wide = lax.axis_size("wide")
    narrow = lax.axis_size("narrow")
    amps = state.shape[1]
    spect = amps // (wide * LOW)
    count = wide * spect

    view = with_layout_constraint(state.reshape(2, amps // LANES, LANES), PAIRED)
    rows = view.transpose(1, 0, 2).reshape(2 * amps // LANES, LANES)
    in_hbm = pl.BlockSpec(memory_space=pltpu.HBM)
    in_vmem = pl.BlockSpec(memory_space=pltpu.VMEM)
    in_smem = pl.BlockSpec(memory_space=pltpu.SMEM)
    piece = jax.ShapeDtypeStruct((4 * spect, LANES), jnp.float32)
    part_of_vmem = pltpu.CompilerParams(vmem_limit_bytes=24 * 2**20)
    order = exchange_order(wide)
    early, late = order[1 : 1 + EARLY], order[1 + EARLY :] + order[:1]

    def swap(blocks, ks):
        return [
            lax.ppermute(block, "wide", [(i, i ^ k) for i in range(wide)]) if k else block
            for block, k in zip(blocks, ks)
        ]

    sends = pl.pallas_call(
        partial(pick_kernel, wide, early),
        in_specs=[in_hbm],
        out_specs=[in_vmem] * len(early),
        out_shape=[piece] * len(early),
        scratch_shapes=[pltpu.SemaphoreType.DMA((len(early),))],
        compiler_params=part_of_vmem,
        name="pick",
    )(rows)
    received = swap(sends, early)

    gates = jax.ShapeDtypeStruct((LAYERS, 2, LOW, 2 * LOW), jnp.bfloat16)
    turns = jax.ShapeDtypeStruct((LAYERS + 1, 2, spect, LOW), jnp.float32)
    *sends, gate, turn = pl.pallas_call(
        partial(tables_kernel, wide, late, spect, narrow),
        in_specs=[in_hbm, in_hbm, in_hbm, in_smem, in_smem, in_smem],
        out_specs=[in_vmem] * (len(late) + 2),
        out_shape=[piece] * len(late) + [gates, turns],
        scratch_shapes=[
            pltpu.VMEM((2,) + gate_re.shape, jnp.float32),
            pltpu.SemaphoreType.DMA((len(late),)),
            pltpu.SemaphoreType.DMA((2,)),
        ],
        compiler_params=part_of_vmem,
        cost_estimate=pl.CostEstimate(flops=10**9, bytes_accessed=8 * 10**6, transcendentals=10**5),
        name="tables",
    )(rows, gate_re, gate_im, bit_orders, phase_pairs.transpose(0, 2, 1), phase_angles)
    received = received + swap(sends, late)
    received = received[-1:] + received[:-1]

    done = pl.pallas_call(
        partial(layers_kernel, wide, spect),
        in_specs=[in_vmem] * (wide + 2),
        out_specs=[in_vmem] * wide,
        out_shape=[piece] * wide,
        scratch_shapes=[
            pltpu.VMEM((2, 2, count, LOW), jnp.float32),
            pltpu.VMEM((count, 2 * LOW), jnp.bfloat16),
            pltpu.VMEM((count, 2 * LOW), jnp.bfloat16),
            pltpu.VMEM((2, LOW, LOW), jnp.bfloat16),
        ],
        compiler_params=part_of_vmem,
        cost_estimate=pl.CostEstimate(flops=5 * 10**9, bytes_accessed=10**7, transcendentals=0),
        name="layers",
    )(*received, gate, turn)

    back = pl.pallas_call(
        partial(place_kernel, wide),
        in_specs=[in_vmem] * wide,
        out_specs=in_hbm,
        out_shape=jax.ShapeDtypeStruct(rows.shape, jnp.float32),
        scratch_shapes=[pltpu.SemaphoreType.DMA((wide,))],
        compiler_params=part_of_vmem,
        name="place",
    )(*swap(done, order))
    view = with_layout_constraint(back.reshape(amps // LANES, 2, LANES).transpose(1, 0, 2), PAIRED)
    return view.reshape(2, amps)


def solution(mesh):
    return jax.shard_map(
        local,
        mesh=mesh,
        in_specs=(P(None, ("wide", "narrow")), P(), P(), P(), P(), P()),
        out_specs=P(None, ("wide", "narrow")),
        check_vma=False,
    )
```

```python
from functools import partial

import jax
import jax.numpy as jnp
from jax import lax
from jax.experimental import pallas as pl
from jax.experimental.layout import Layout, with_layout_constraint
from jax.experimental.pallas import tpu as pltpu
from jax.sharding import PartitionSpec as P

LAYERS = 6
GATE = 128
LOW = 256
LOW_BITS = 8
PHASES = 16
PHASE_BITS = 12
LANES = 128
PACKED = 16
GROUP = 5
TILE = 128
PAIRED = Layout(major_to_minor=(1, 0, 2))


def split(x):
    high = x.astype(jnp.bfloat16)
    low = (x - high.astype(jnp.float32)).astype(jnp.bfloat16)
    return high, low


def exchange_order(wide):
    far = list(range(wide // 2, wide, 2))
    near = [k for top in (wide // 4, wide // 8) for k in range(top, 2 * top, 2) if top > 1]
    near += [k for k in range(wide // 2 - 2, 0, -2) if k not in near]
    pairs = []
    for i, k in enumerate(far):
        pairs += [k] + near[i : i + 1] * (i < len(near) - 1)
    pairs += near[-1:]
    return [0] + [k + j for k in pairs for j in range(2)] + [1]


def block_of(ref, k, wide):
    rows = ref.shape[0] // wide
    start = (lax.axis_index("wide") ^ k) * rows
    return ref.at[pl.ds(pl.multiple_of(start, rows), rows)]


def pick_kernel(wide, ks, x_hbm, *rest):
    sends, sem = rest[:-1], rest[-1]
    copies = [pltpu.make_async_copy(block_of(x_hbm, k, wide), sends[i], sem.at[i]) for i, k in enumerate(ks)]
    for copy in copies:
        copy.start()
    for copy in copies:
        copy.wait()


def gates_kernel(wide, ks, x_hbm, re_hbm, im_hbm, order_ref, *rest):
    sends = rest[: len(ks)]
    gate_ref, gates, block_sem, gate_sem = rest[len(ks) :]
    copies = [pltpu.make_async_copy(block_of(x_hbm, k, wide), sends[i], block_sem.at[i]) for i, k in enumerate(ks)]
    gate_copies = [
        pltpu.make_async_copy(hbm, gates.at[part], gate_sem.at[part]) for part, hbm in enumerate((re_hbm, im_hbm))
    ]
    for copy in gate_copies + copies:
        copy.start()
    for copy in gate_copies:
        copy.wait()
    t = lax.broadcasted_iota(jnp.int32, (8, LOW), 1)
    position = lax.broadcasted_iota(jnp.int32, (LOW // 8, 8, LOW), 0) * 8
    position = position + lax.broadcasted_iota(jnp.int32, (LOW // 8, 8, LOW), 1)
    contract = (((1,), (1,)), ((), ()))
    for layer in range(LAYERS):
        source = jnp.zeros((8, LOW), jnp.int32)
        for bit in range(LOW_BITS):
            source = source + (((t >> bit) & 1) << jnp.full((8, LOW), order_ref[layer, bit], jnp.int32))
        hot = jnp.where(position == source[None], 1.0, 0.0).reshape(LOW, LOW).astype(jnp.bfloat16)
        for part in range(2):
            for which, piece in enumerate(split(gates[part, layer])):
                for e in range(2):
                    moved = lax.dot_general(
                        hot[:, e * GATE : (e + 1) * GATE], piece, contract, preferred_element_type=jnp.float32
                    )
                    start = part * LOW + e * GATE
                    gate_ref[layer, which, :, start : start + GATE] = moved.astype(jnp.bfloat16)
    for copy in copies:
        copy.wait()


def phases_kernel(wide, ks, spect, narrow, x_hbm, pair_ref, angle_ref, arrived_hbm, *rest):
    sends = rest[: len(ks)]
    turn_ref, block_sem = rest[len(ks) :]
    copies = [pltpu.make_async_copy(block_of(x_hbm, k, wide), sends[i], block_sem.at[i]) for i, k in enumerate(ks)]
    for copy in copies:
        copy.start()
    size = turn_ref.shape[2]
    row = lax.broadcasted_iota(jnp.int32, (size, LOW), 0)
    lane = lax.broadcasted_iota(jnp.int32, (size, LOW), 1)
    r = lax.axis_index("wide") * (spect // narrow) + row // narrow
    turn_ref[0, 0] = jnp.ones((size, LOW), jnp.float32)
    turn_ref[0, 1] = jnp.zeros((size, LOW), jnp.float32)
    for layer in range(LAYERS):
        b = lax.axis_index("narrow") if layer % 2 == 0 else row % narrow
        u = ((r * narrow + b) * LOW + lane) & (2**PHASE_BITS - 1)
        phase = jnp.zeros((size, LOW), jnp.float32)
        for gate in range(PHASES):
            first = u >> jnp.full((size, LOW), pair_ref[layer, 0, gate], jnp.int32)
            second = u >> jnp.full((size, LOW), pair_ref[layer, 1, gate], jnp.int32)
            phase = phase + jnp.where((first & second & 1) == 1, angle_ref[layer, gate], 0.0)
        turn_ref[layer + 1, 0] = jnp.cos(phase)
        turn_ref[layer + 1, 1] = jnp.sin(phase)

    for copy in copies:
        copy.wait()


def exchange_modes(rows, span):
    count = len(rows)
    group = lax.broadcasted_iota(jnp.int32, rows[0].shape, 1) // span
    rows = [pltpu.roll(row, m * span, 1) if m else row for m, row in enumerate(rows)]
    step = 1
    while step < count:
        taken = (group & step) != 0
        rows = [jnp.where(taken, rows[(y + step) % count], rows[y]) for y in range(count)]
        step *= 2
    return [pltpu.roll(rows[-r % count], LANES - r * span, 1) if r else rows[0] for r in range(count)]


def place_kernel(wide, *rest):
    blocks, out_hbm, sem = rest[:wide], rest[wide], rest[wide + 1]
    copies = [
        pltpu.make_async_copy(blocks[i], block_of(out_hbm, k, wide), sem.at[i])
        for i, k in enumerate(exchange_order(wide))
    ]
    for copy in copies:
        copy.start()
    for copy in copies:
        copy.wait()


def layers_kernel(wide, spect, *rest):
    received = rest[:wide]
    gate, turn = rest[wide : wide + 2]
    outs = rest[wide + 2 : 2 * wide + 2]
    state, left_high, left_low, minus_imag = rest[2 * wide + 2 :]
    me = lax.axis_index("wide")
    count = wide * spect
    span = LOW // wide
    half = wide // 2
    rows_at_once = min(spect, PACKED)
    joined = PACKED // rows_at_once
    tile = min(TILE, count)

    for i, k in enumerate(exchange_order(wide)):
        rows = pl.ds(pl.multiple_of((me ^ k) * spect, spect), spect)
        for part in range(2):
            for lanes in range(2):
                state[0, part, rows, lanes * LANES : (lanes + 1) * LANES] = received[i][
                    pl.ds(2 * lanes + part, spect, stride=4), :
                ]

    def turned(slot, entry, first, size, offset, lanes):
        rows, lanes = pl.ds(first + offset, size), slice(lanes * LANES, (lanes + 1) * LANES)
        real, imag = state[slot, 0, rows, lanes], state[slot, 1, rows, lanes]
        cosine, sine = turn[entry, 0, :, lanes], turn[entry, 1, :, lanes]
        return real * cosine - imag * sine, real * sine + imag * cosine

    def one_layer(layer, slot):
        for which in range(2):
            minus_imag[which] = -gate[layer, which, :, LOW:]

        for lanes in range(2):
            for top in range(2):
                for offset in range(0, spect, rows_at_once):
                    pieces = [
                        turned(slot, layer, (top * half + m) * spect, rows_at_once, offset, lanes) for m in range(half)
                    ]
                    for part in range(2):
                        rows = exchange_modes([piece[part] for piece in pieces], span)
                        column = part * LOW + top * LANES
                        for g in range(0, half, joined):
                            at = (lanes * half + g) * spect + offset
                            high, low = split(jnp.concatenate(rows[g : g + joined], axis=0))
                            left_high[at : at + PACKED, column : column + LANES] = high
                            left_low[at : at + PACKED, column : column + LANES] = low

        factors = []
        for which in range(2):
            real, imag = gate[layer, which, :, :LOW], gate[layer, which, :, LOW:]
            factors.append([[real, minus_imag[which]], [imag, real]])
        for first in range(0, count, tile):
            rows = slice(first, first + tile)
            terms = jnp.concatenate([left_high[rows], left_low[rows], left_high[rows]], axis=1)
            for part in range(2):
                square = jnp.concatenate(factors[0][part] + factors[0][part] + factors[1][part], axis=0)
                state[1 - slot, part, rows] = jnp.dot(terms, square, preferred_element_type=jnp.float32)

    def two_layers(step, carry):
        one_layer(2 * step, 0)
        one_layer(2 * step + 1, 1)
        return carry

    lax.fori_loop(0, LAYERS // 2, two_layers, 0)

    for i, k in enumerate(exchange_order(wide)):
        first = pl.multiple_of((me ^ k) * spect, spect)
        for offset in range(0, spect, rows_at_once):
            for lanes in range(2):
                for part, piece in enumerate(turned(0, LAYERS, first, rows_at_once, offset, lanes)):
                    outs[i][pl.ds(4 * offset + 2 * lanes + part, rows_at_once, stride=4), :] = piece


def local(state, gate_re, gate_im, bit_orders, phase_pairs, phase_angles):
    wide = lax.axis_size("wide")
    narrow = lax.axis_size("narrow")
    amps = state.shape[1]
    spect = amps // (wide * LOW)
    count = wide * spect

    view = with_layout_constraint(state.reshape(2, amps // LANES, LANES), PAIRED)
    rows = view.transpose(1, 0, 2).reshape(2 * amps // LANES, LANES)
    in_hbm = pl.BlockSpec(memory_space=pltpu.HBM)
    in_vmem = pl.BlockSpec(memory_space=pltpu.VMEM)
    in_smem = pl.BlockSpec(memory_space=pltpu.SMEM)
    piece = jax.ShapeDtypeStruct((4 * spect, LANES), jnp.float32)
    part_of_vmem = pltpu.CompilerParams(vmem_limit_bytes=24 * 2**20)
    order = exchange_order(wide)
    early, middle, late = order[1 : 1 + GROUP], order[1 + GROUP : 1 + 2 * GROUP], order[1 + 2 * GROUP :] + order[:1]

    def swap(blocks, ks):
        return [
            lax.ppermute(block, "wide", [(i, i ^ k) for i in range(wide)]) if k else block
            for block, k in zip(blocks, ks)
        ]

    sends = pl.pallas_call(
        partial(pick_kernel, wide, early),
        in_specs=[in_hbm],
        out_specs=[in_vmem] * len(early),
        out_shape=[piece] * len(early),
        scratch_shapes=[pltpu.SemaphoreType.DMA((len(early),))],
        compiler_params=part_of_vmem,
        name="pick",
    )(rows)
    received = swap(sends, early)

    *sends, gate = pl.pallas_call(
        partial(gates_kernel, wide, middle),
        in_specs=[in_hbm, in_hbm, in_hbm, in_smem],
        out_specs=[in_vmem] * (len(middle) + 1),
        out_shape=[piece] * len(middle) + [jax.ShapeDtypeStruct((LAYERS, 2, LOW, 2 * LOW), jnp.bfloat16)],
        scratch_shapes=[
            pltpu.VMEM((2,) + gate_re.shape, jnp.float32),
            pltpu.SemaphoreType.DMA((len(middle),)),
            pltpu.SemaphoreType.DMA((2,)),
        ],
        compiler_params=part_of_vmem,
        cost_estimate=pl.CostEstimate(flops=10**9, bytes_accessed=4 * 10**6, transcendentals=0),
        name="gates",
    )(rows, gate_re, gate_im, bit_orders)
    received = received + swap(sends, middle)

    distinct = min(spect, 2 ** (PHASE_BITS - LOW_BITS))
    *sends, turn = pl.pallas_call(
        partial(phases_kernel, wide, late, spect, narrow),
        in_specs=[in_hbm, in_smem, in_smem, in_hbm],
        out_specs=[in_vmem] * (len(late) + 1),
        out_shape=[piece] * len(late) + [jax.ShapeDtypeStruct((LAYERS + 1, 2, distinct, LOW), jnp.float32)],
        scratch_shapes=[pltpu.SemaphoreType.DMA((len(late),))],
        compiler_params=part_of_vmem,
        cost_estimate=pl.CostEstimate(flops=10**8, bytes_accessed=4 * 10**6, transcendentals=10**5),
        name="phases",
    )(rows, phase_pairs.transpose(0, 2, 1), phase_angles, received[0])
    received = received + swap(sends, late)
    received = received[-1:] + received[:-1]

    done = pl.pallas_call(
        partial(layers_kernel, wide, spect),
        in_specs=[in_vmem] * (wide + 2),
        out_specs=[in_vmem] * wide,
        out_shape=[piece] * wide,
        scratch_shapes=[
            pltpu.VMEM((2, 2, count, LOW), jnp.float32),
            pltpu.VMEM((count, 2 * LOW), jnp.bfloat16),
            pltpu.VMEM((count, 2 * LOW), jnp.bfloat16),
            pltpu.VMEM((2, LOW, LOW), jnp.bfloat16),
        ],
        compiler_params=part_of_vmem,
        cost_estimate=pl.CostEstimate(flops=5 * 10**9, bytes_accessed=10**7, transcendentals=0),
        name="layers",
    )(*received, gate, turn)

    back = pl.pallas_call(
        partial(place_kernel, wide),
        in_specs=[in_vmem] * wide,
        out_specs=in_hbm,
        out_shape=jax.ShapeDtypeStruct(rows.shape, jnp.float32),
        scratch_shapes=[pltpu.SemaphoreType.DMA((wide,))],
        compiler_params=part_of_vmem,
        name="place",
    )(*swap(done, order))
    view = with_layout_constraint(back.reshape(amps // LANES, 2, LANES).transpose(1, 0, 2), PAIRED)
    return view.reshape(2, amps)


def solution(mesh):
    return jax.shard_map(
        local,
        mesh=mesh,
        in_specs=(P(None, ("wide", "narrow")), P(), P(), P(), P(), P()),
        out_specs=P(None, ("wide", "narrow")),
        check_vma=False,
    )
```

```python
from functools import partial

import jax
import jax.numpy as jnp
from jax import lax
from jax.experimental import pallas as pl
from jax.experimental.layout import Layout, with_layout_constraint
from jax.experimental.pallas import tpu as pltpu
from jax.sharding import PartitionSpec as P

LAYERS = 6
GATE = 128
LOW = 256
LOW_BITS = 8
PHASES = 16
PHASE_BITS = 12
LANES = 128
PACKED = 16
SPARE = 34
TILE = 128
PAIRED = Layout(major_to_minor=(1, 0, 2))


def split(x):
    high = x.astype(jnp.bfloat16)
    low = (x - high.astype(jnp.float32)).astype(jnp.bfloat16)
    return high, low


def exchange_order(wide):
    far = list(range(wide // 2, wide, 2))
    near = [k for top in (wide // 4, wide // 8) for k in range(top, 2 * top, 2) if top > 1]
    near += [k for k in range(wide // 2 - 2, 0, -2) if k not in near]
    pairs = []
    for i, k in enumerate(far):
        pairs += [k] + near[i : i + 1] * (i < len(near) - 1)
    pairs += near[-1:]
    return [0] + [k + j for k in pairs for j in range(2)] + [1]


def block_of(ref, k, wide):
    rows = ref.shape[0] // wide
    start = (lax.axis_index("wide") ^ k) * rows
    return ref.at[pl.ds(pl.multiple_of(start, rows), rows)]


def tables_kernel(
    spect, narrow, re_hbm, im_hbm, order_ref, pair_ref, angle_ref, gate_hbm, turn_hbm, gate_ref, turn_ref, gates, sem
):
    copies = [pltpu.make_async_copy(hbm, gates.at[part], sem.at[part]) for part, hbm in enumerate((re_hbm, im_hbm))]
    for copy in copies:
        copy.start()
    size = turn_ref.shape[2]
    row = lax.broadcasted_iota(jnp.int32, (size, LOW), 0)
    lane = lax.broadcasted_iota(jnp.int32, (size, LOW), 1)
    r = lax.axis_index("wide") * (spect // narrow) + row // narrow
    turn_ref[0, 0] = jnp.ones((size, LOW), jnp.float32)
    turn_ref[0, 1] = jnp.zeros((size, LOW), jnp.float32)
    for layer in range(LAYERS):
        b = lax.axis_index("narrow") if layer % 2 == 0 else row % narrow
        u = ((r * narrow + b) * LOW + lane) & (2**PHASE_BITS - 1)
        phase = jnp.zeros((size, LOW), jnp.float32)
        for gate in range(PHASES):
            first = u >> jnp.full((size, LOW), pair_ref[layer, 0, gate], jnp.int32)
            second = u >> jnp.full((size, LOW), pair_ref[layer, 1, gate], jnp.int32)
            phase = phase + jnp.where((first & second & 1) == 1, angle_ref[layer, gate], 0.0)
        turn_ref[layer + 1, 0] = jnp.cos(phase)
        turn_ref[layer + 1, 1] = jnp.sin(phase)

    turn_copy = pltpu.make_async_copy(turn_ref, turn_hbm, sem.at[2])
    turn_copy.start()

    for copy in copies:
        copy.wait()
    t = lax.broadcasted_iota(jnp.int32, (8, LOW), 1)
    position = lax.broadcasted_iota(jnp.int32, (LOW // 8, 8, LOW), 0) * 8
    position = position + lax.broadcasted_iota(jnp.int32, (LOW // 8, 8, LOW), 1)
    contract = (((1,), (1,)), ((), ()))
    for layer in range(LAYERS):
        source = jnp.zeros((8, LOW), jnp.int32)
        for bit in range(LOW_BITS):
            source = source + (((t >> bit) & 1) << jnp.full((8, LOW), order_ref[layer, bit], jnp.int32))
        hot = jnp.where(position == source[None], 1.0, 0.0).reshape(LOW, LOW).astype(jnp.bfloat16)
        for part in range(2):
            for which, piece in enumerate(split(gates[part, layer])):
                for e in range(2):
                    moved = lax.dot_general(
                        hot[:, e * GATE : (e + 1) * GATE], piece, contract, preferred_element_type=jnp.float32
                    )
                    start = part * LOW + e * GATE
                    gate_ref[layer, which, :, start : start + GATE] = moved.astype(jnp.bfloat16)
    gate_copy = pltpu.make_async_copy(gate_ref, gate_hbm.at[pl.ds(0, LAYERS)], sem.at[3])
    gate_copy.start()
    turn_copy.wait()
    gate_copy.wait()


def exchange_modes(rows, span):
    count = len(rows)
    group = lax.broadcasted_iota(jnp.int32, rows[0].shape, 1) // span
    rows = [pltpu.roll(row, m * span, 1) if m else row for m, row in enumerate(rows)]
    step = 1
    while step < count:
        taken = (group & step) != 0
        rows = [jnp.where(taken, rows[(y + step) % count], rows[y]) for y in range(count)]
        step *= 2
    return [pltpu.roll(rows[-r % count], LANES - r * span, 1) if r else rows[0] for r in range(count)]


def place_kernel(wide, *rest):
    blocks, out_hbm, sem = rest[:wide], rest[wide], rest[wide + 1]
    copies = [
        pltpu.make_async_copy(blocks[i], block_of(out_hbm, k, wide), sem.at[i])
        for i, k in enumerate(exchange_order(wide))
    ]
    for copy in copies:
        copy.start()
    for copy in copies:
        copy.wait()


def layers_kernel(wide, spect, x, gate_hbm, turn_hbm, *rest):
    outs = rest[:wide]
    gate, turn, state, left_high, left_low, minus_imag, gate_sem, turn_sem = rest[wide:]
    me = lax.axis_index("wide")
    count = wide * spect
    span = LOW // wide
    half = wide // 2
    rows_at_once = min(spect, PACKED)
    joined = PACKED // rows_at_once
    tile = min(TILE, count)

    def gate_copy(layer):
        return pltpu.make_async_copy(gate_hbm.at[layer], gate.at[layer], gate_sem.at[layer])

    turn_copy = pltpu.make_async_copy(turn_hbm, turn, turn_sem.at[0])
    turn_copy.start()
    for layer in range(LAYERS):
        gate_copy(layer).start()
    for part in range(2):
        for lanes in range(2):
            state[0, part, :, lanes * LANES : (lanes + 1) * LANES] = x[pl.ds(2 * lanes + part, count, stride=4), :]
    turn_copy.wait()

    def turned(slot, entry, first, size, offset, lanes):
        rows, lanes = pl.ds(first + offset, size), slice(lanes * LANES, (lanes + 1) * LANES)
        real, imag = state[slot, 0, rows, lanes], state[slot, 1, rows, lanes]
        cosine, sine = turn[entry, 0, :, lanes], turn[entry, 1, :, lanes]
        return real * cosine - imag * sine, real * sine + imag * cosine

    def one_layer(layer, slot):
        for lanes in range(2):
            for top in range(2):
                for offset in range(0, spect, rows_at_once):
                    pieces = [
                        turned(slot, layer, (top * half + m) * spect, rows_at_once, offset, lanes) for m in range(half)
                    ]
                    for part in range(2):
                        rows = exchange_modes([piece[part] for piece in pieces], span)
                        column = part * LOW + top * LANES
                        for g in range(0, half, joined):
                            at = (lanes * half + g) * spect + offset
                            high, low = split(jnp.concatenate(rows[g : g + joined], axis=0))
                            left_high[at : at + PACKED, column : column + LANES] = high
                            left_low[at : at + PACKED, column : column + LANES] = low

        gate_copy(layer).wait()
        for which in range(2):
            minus_imag[which] = -gate[layer, which, :, LOW:]

        factors = []
        for which in range(2):
            real, imag = gate[layer, which, :, :LOW], gate[layer, which, :, LOW:]
            factors.append([[real, minus_imag[which]], [imag, real]])
        for first in range(0, count, tile):
            rows = slice(first, first + tile)
            terms = jnp.concatenate([left_high[rows], left_low[rows], left_high[rows]], axis=1)
            for part in range(2):
                square = jnp.concatenate(factors[0][part] + factors[0][part] + factors[1][part], axis=0)
                state[1 - slot, part, rows] = jnp.dot(terms, square, preferred_element_type=jnp.float32)

    def two_layers(step, carry):
        one_layer(2 * step, 0)
        one_layer(2 * step + 1, 1)
        return carry

    lax.fori_loop(0, LAYERS // 2, two_layers, 0)

    for i, k in enumerate(exchange_order(wide)):
        first = pl.multiple_of((me ^ k) * spect, spect)
        for offset in range(0, spect, rows_at_once):
            for lanes in range(2):
                for part, piece in enumerate(turned(0, LAYERS, first, rows_at_once, offset, lanes)):
                    outs[i][pl.ds(4 * offset + 2 * lanes + part, rows_at_once, stride=4), :] = piece


def local(state, gate_re, gate_im, bit_orders, phase_pairs, phase_angles):
    wide = lax.axis_size("wide")
    narrow = lax.axis_size("narrow")
    amps = state.shape[1]
    spect = amps // (wide * LOW)
    count = wide * spect

    view = with_layout_constraint(state.reshape(2, amps // LANES, LANES), PAIRED)
    rows = view.transpose(1, 0, 2).reshape(2 * amps // LANES, LANES)
    gathered = lax.all_to_all(rows, "wide", split_axis=0, concat_axis=0, tiled=True)

    in_hbm = pl.BlockSpec(memory_space=pltpu.HBM)
    in_vmem = pl.BlockSpec(memory_space=pltpu.VMEM)
    in_smem = pl.BlockSpec(memory_space=pltpu.SMEM)
    piece = jax.ShapeDtypeStruct((4 * spect, LANES), jnp.float32)
    part_of_vmem = pltpu.CompilerParams(vmem_limit_bytes=24 * 2**20)
    most_of_vmem = pltpu.CompilerParams(vmem_limit_bytes=52 * 2**20)
    order = exchange_order(wide)

    gates = (LAYERS, 2, LOW, 2 * LOW)
    turns = (LAYERS + 1, 2, min(spect, 2 ** (PHASE_BITS - LOW_BITS)), LOW)
    gate, turn = pl.pallas_call(
        partial(tables_kernel, spect, narrow),
        in_specs=[in_hbm, in_hbm, in_smem, in_smem, in_smem],
        out_specs=[in_hbm, in_hbm],
        out_shape=[
            jax.ShapeDtypeStruct((LAYERS + SPARE,) + gates[1:], jnp.bfloat16),
            jax.ShapeDtypeStruct(turns, jnp.float32),
        ],
        scratch_shapes=[
            pltpu.VMEM(gates, jnp.bfloat16),
            pltpu.VMEM(turns, jnp.float32),
            pltpu.VMEM((2,) + gate_re.shape, jnp.float32),
            pltpu.SemaphoreType.DMA((4,)),
        ],
        compiler_params=most_of_vmem,
        cost_estimate=pl.CostEstimate(flops=10**9, bytes_accessed=8 * 10**6, transcendentals=10**5),
        name="tables",
    )(gate_re, gate_im, bit_orders, phase_pairs.transpose(0, 2, 1), phase_angles)

    def swap(blocks, ks):
        return [
            lax.ppermute(block, "wide", [(i, i ^ k) for i in range(wide)]) if k else block
            for block, k in zip(blocks, ks)
        ]

    done = pl.pallas_call(
        partial(layers_kernel, wide, spect),
        in_specs=[in_vmem, in_hbm, in_hbm],
        out_specs=[in_vmem] * wide,
        out_shape=[piece] * wide,
        scratch_shapes=[
            pltpu.VMEM(gates, jnp.bfloat16),
            pltpu.VMEM(turns, jnp.float32),
            pltpu.VMEM((2, 2, count, LOW), jnp.float32),
            pltpu.VMEM((count, 2 * LOW), jnp.bfloat16),
            pltpu.VMEM((count, 2 * LOW), jnp.bfloat16),
            pltpu.VMEM((2, LOW, LOW), jnp.bfloat16),
            pltpu.SemaphoreType.DMA((LAYERS,)),
            pltpu.SemaphoreType.DMA((1,)),
        ],
        compiler_params=most_of_vmem,
        cost_estimate=pl.CostEstimate(flops=5 * 10**9, bytes_accessed=10**7, transcendentals=0),
        name="layers",
    )(gathered, gate, turn)

    back = pl.pallas_call(
        partial(place_kernel, wide),
        in_specs=[in_vmem] * wide,
        out_specs=in_hbm,
        out_shape=jax.ShapeDtypeStruct(rows.shape, jnp.float32),
        scratch_shapes=[pltpu.SemaphoreType.DMA((wide,))],
        compiler_params=part_of_vmem,
        name="place",
    )(*swap(done, order))
    view = with_layout_constraint(back.reshape(amps // LANES, 2, LANES).transpose(1, 0, 2), PAIRED)
    return view.reshape(2, amps)


def solution(mesh):
    return jax.shard_map(
        local,
        mesh=mesh,
        in_specs=(P(None, ("wide", "narrow")), P(), P(), P(), P(), P()),
        out_specs=P(None, ("wide", "narrow")),
        check_vma=False,
    )
```

```python
from functools import partial

import jax
import jax.numpy as jnp
from jax import lax
from jax.experimental import pallas as pl
from jax.experimental.layout import Layout, with_layout_constraint
from jax.experimental.pallas import tpu as pltpu
from jax.sharding import PartitionSpec as P

LAYERS = 6
GATE = 128
LOW = 256
LOW_BITS = 8
PHASES = 16
PHASE_BITS = 12
LANES = 128
PACKED = 16
TILE = 128
PAIRED = Layout(major_to_minor=(1, 0, 2))


def split(x):
    high = x.astype(jnp.bfloat16)
    low = (x - high.astype(jnp.float32)).astype(jnp.bfloat16)
    return high, low


def exchange_order(wide):
    far = list(range(wide // 2, wide, 2))
    near = [k for top in (wide // 4, wide // 8) for k in range(top, 2 * top, 2) if top > 1]
    near += [k for k in range(wide // 2 - 2, 0, -2) if k not in near]
    pairs = []
    for i, k in enumerate(far):
        pairs += [k] + near[i : i + 1] * (i < len(near) - 1)
    pairs += near[-1:]
    return [0] + [k + j for k in pairs for j in range(2)] + [1]


def block_of(ref, k, wide):
    rows = ref.shape[0] // wide
    start = (lax.axis_index("wide") ^ k) * rows
    return ref.at[pl.ds(pl.multiple_of(start, rows), rows)]


def tables_kernel(spect, narrow, re_ref, im_ref, order_ref, pair_ref, angle_ref, gate_ref, half_ref, turn_ref):
    size = turn_ref.shape[2]
    row = lax.broadcasted_iota(jnp.int32, (size, LOW), 0)
    lane = lax.broadcasted_iota(jnp.int32, (size, LOW), 1)
    r = lax.axis_index("wide") * (spect // narrow) + row // narrow
    turn_ref[0, 0] = jnp.ones((size, LOW), jnp.float32)
    turn_ref[0, 1] = jnp.zeros((size, LOW), jnp.float32)
    for layer in range(LAYERS):
        b = lax.axis_index("narrow") if layer % 2 == 0 else row % narrow
        u = ((r * narrow + b) * LOW + lane) & (2**PHASE_BITS - 1)
        phase = jnp.zeros((size, LOW), jnp.float32)
        for gate in range(PHASES):
            first = u >> jnp.full((size, LOW), pair_ref[layer, 0, gate], jnp.int32)
            second = u >> jnp.full((size, LOW), pair_ref[layer, 1, gate], jnp.int32)
            phase = phase + jnp.where((first & second & 1) == 1, angle_ref[layer, gate], 0.0)
        turn_ref[layer + 1, 0] = jnp.cos(phase)
        turn_ref[layer + 1, 1] = jnp.sin(phase)

    t = lax.broadcasted_iota(jnp.int32, (8, GATE), 1)
    position = lax.broadcasted_iota(jnp.int32, (LOW // 8, 8, GATE), 0) * 8
    position = position + lax.broadcasted_iota(jnp.int32, (LOW // 8, 8, GATE), 1)
    contract = (((1,), (1,)), ((), ()))
    for layer in range(LAYERS):
        source = jnp.zeros((8, GATE), jnp.int32)
        for bit in range(LOW_BITS - 1):
            source = source + (((t >> bit) & 1) << jnp.full((8, GATE), order_ref[layer, bit], jnp.int32))
        half = jnp.int32(1) << order_ref[layer, LOW_BITS - 1]
        hot = jnp.where((position & ~half) == source[None], 1.0, 0.0).reshape(LOW, GATE).astype(jnp.bfloat16)
        half_ref[layer] = jnp.where((position & half) == 0, 1.0, 0.0).reshape(LOW, GATE).astype(jnp.bfloat16)
        for part, ref in enumerate((re_ref, im_ref)):
            for which, piece in enumerate(split(ref[layer])):
                moved = lax.dot_general(hot, piece, contract, preferred_element_type=jnp.float32)
                gate_ref[layer, which, :, part * GATE : (part + 1) * GATE] = moved.astype(jnp.bfloat16)


def exchange_modes(rows, span):
    count = len(rows)
    group = lax.broadcasted_iota(jnp.int32, rows[0].shape, 1) // span
    rows = [pltpu.roll(row, m * span, 1) if m else row for m, row in enumerate(rows)]
    step = 1
    while step < count:
        taken = (group & step) != 0
        rows = [jnp.where(taken, rows[(y + step) % count], rows[y]) for y in range(count)]
        step *= 2
    return [pltpu.roll(rows[-r % count], LANES - r * span, 1) if r else rows[0] for r in range(count)]


def place_kernel(wide, *rest):
    blocks, out_hbm, sem = rest[:wide], rest[wide], rest[wide + 1]
    copies = [
        pltpu.make_async_copy(blocks[i], block_of(out_hbm, k, wide), sem.at[i])
        for i, k in enumerate(exchange_order(wide))
    ]
    for copy in copies:
        copy.start()
    for copy in copies:
        copy.wait()


def layers_kernel(wide, spect, x, gate, first_half, turn, *rest):
    outs = rest[:wide]
    state, left_high, left_low, spread = rest[wide:]
    me = lax.axis_index("wide")
    count = wide * spect
    span = LOW // wide
    half = wide // 2
    rows_at_once = min(spect, PACKED)
    joined = PACKED // rows_at_once
    tile = min(TILE, count)

    for part in range(2):
        for lanes in range(2):
            state[0, part, :, lanes * LANES : (lanes + 1) * LANES] = x[pl.ds(2 * lanes + part, count, stride=4), :]
    def turned(slot, entry, first, size, offset, lanes):
        rows, lanes = pl.ds(first + offset, size), slice(lanes * LANES, (lanes + 1) * LANES)
        real, imag = state[slot, 0, rows, lanes], state[slot, 1, rows, lanes]
        cosine, sine = turn[entry, 0, :, lanes], turn[entry, 1, :, lanes]
        return real * cosine - imag * sine, real * sine + imag * cosine

    def one_layer(layer, slot):
        for lanes in range(2):
            for top in range(2):
                for offset in range(0, spect, rows_at_once):
                    pieces = [
                        turned(slot, layer, (top * half + m) * spect, rows_at_once, offset, lanes) for m in range(half)
                    ]
                    for part in range(2):
                        rows = exchange_modes([piece[part] for piece in pieces], span)
                        column = part * LOW + top * LANES
                        for g in range(0, half, joined):
                            at = (lanes * half + g) * spect + offset
                            high, low = split(jnp.concatenate(rows[g : g + joined], axis=0))
                            left_high[at : at + PACKED, column : column + LANES] = high
                            left_low[at : at + PACKED, column : column + LANES] = low

        kept = first_half[layer]
        for which in range(2):
            for part in range(2):
                piece = gate[layer, which, :, part * GATE : (part + 1) * GATE]
                first = piece * kept
                both = jnp.concatenate([first, piece - first], axis=1)
                spread[which, part] = both
                if part:
                    spread[which, 2] = -both
        factors = [[[spread[which, 0], spread[which, 2]], [spread[which, 1], spread[which, 0]]] for which in range(2)]

        for first in range(0, count, tile):
            rows = slice(first, first + tile)
            terms = jnp.concatenate([left_high[rows], left_low[rows], left_high[rows]], axis=1)
            for part in range(2):
                square = jnp.concatenate(factors[0][part] + factors[0][part] + factors[1][part], axis=0)
                state[1 - slot, part, rows] = jnp.dot(terms, square, preferred_element_type=jnp.float32)

    def two_layers(step, carry):
        one_layer(2 * step, 0)
        one_layer(2 * step + 1, 1)
        return carry

    lax.fori_loop(0, LAYERS // 2, two_layers, 0)

    for i, k in enumerate(exchange_order(wide)):
        first = pl.multiple_of((me ^ k) * spect, spect)
        for offset in range(0, spect, rows_at_once):
            for lanes in range(2):
                for part, piece in enumerate(turned(0, LAYERS, first, rows_at_once, offset, lanes)):
                    outs[i][pl.ds(4 * offset + 2 * lanes + part, rows_at_once, stride=4), :] = piece


def local(state, gate_re, gate_im, bit_orders, phase_pairs, phase_angles):
    wide = lax.axis_size("wide")
    narrow = lax.axis_size("narrow")
    amps = state.shape[1]
    spect = amps // (wide * LOW)
    count = wide * spect

    view = with_layout_constraint(state.reshape(2, amps // LANES, LANES), PAIRED)
    rows = view.transpose(1, 0, 2).reshape(2 * amps // LANES, LANES)
    gathered = lax.all_to_all(rows, "wide", split_axis=0, concat_axis=0, tiled=True)

    in_hbm = pl.BlockSpec(memory_space=pltpu.HBM)
    in_vmem = pl.BlockSpec(memory_space=pltpu.VMEM)
    in_smem = pl.BlockSpec(memory_space=pltpu.SMEM)
    piece = jax.ShapeDtypeStruct((4 * spect, LANES), jnp.float32)
    part_of_vmem = pltpu.CompilerParams(vmem_limit_bytes=24 * 2**20)
    order = exchange_order(wide)

    turns = (LAYERS + 1, 2, min(spect, 2 ** (PHASE_BITS - LOW_BITS)), LOW)
    tables = pl.pallas_call(
        partial(tables_kernel, spect, narrow),
        in_specs=[in_vmem, in_vmem, in_smem, in_smem, in_smem],
        out_specs=[in_vmem] * 3,
        out_shape=[
            jax.ShapeDtypeStruct((LAYERS, 2, LOW, 2 * GATE), jnp.bfloat16),
            jax.ShapeDtypeStruct((LAYERS, LOW, GATE), jnp.bfloat16),
            jax.ShapeDtypeStruct(turns, jnp.float32),
        ],
        compiler_params=part_of_vmem,
        cost_estimate=pl.CostEstimate(flops=10**9, bytes_accessed=8 * 10**6, transcendentals=10**5),
        name="tables",
    )(gate_re, gate_im, bit_orders, phase_pairs.transpose(0, 2, 1), phase_angles)

    def swap(blocks, ks):
        return [
            lax.ppermute(block, "wide", [(i, i ^ k) for i in range(wide)]) if k else block
            for block, k in zip(blocks, ks)
        ]

    done = pl.pallas_call(
        partial(layers_kernel, wide, spect),
        in_specs=[in_vmem] * 4,
        out_specs=[in_vmem] * wide,
        out_shape=[piece] * wide,
        scratch_shapes=[
            pltpu.VMEM((2, 2, count, LOW), jnp.float32),
            pltpu.VMEM((count, 2 * LOW), jnp.bfloat16),
            pltpu.VMEM((count, 2 * LOW), jnp.bfloat16),
            pltpu.VMEM((2, 3, LOW, LOW), jnp.bfloat16),
        ],
        compiler_params=part_of_vmem,
        cost_estimate=pl.CostEstimate(flops=5 * 10**9, bytes_accessed=10**7, transcendentals=0),
        name="layers",
    )(gathered, *tables)

    back = pl.pallas_call(
        partial(place_kernel, wide),
        in_specs=[in_vmem] * wide,
        out_specs=in_hbm,
        out_shape=jax.ShapeDtypeStruct(rows.shape, jnp.float32),
        scratch_shapes=[pltpu.SemaphoreType.DMA((wide,))],
        compiler_params=part_of_vmem,
        name="place",
    )(*swap(done, order))
    view = with_layout_constraint(back.reshape(amps // LANES, 2, LANES).transpose(1, 0, 2), PAIRED)
    return view.reshape(2, amps)


def solution(mesh):
    return jax.shard_map(
        local,
        mesh=mesh,
        in_specs=(P(None, ("wide", "narrow")), P(), P(), P(), P(), P()),
        out_specs=P(None, ("wide", "narrow")),
        check_vma=False,
    )
```

```python
from functools import partial

import jax
import jax.numpy as jnp
from jax import lax
from jax.experimental import pallas as pl
from jax.experimental.layout import Layout, with_layout_constraint
from jax.experimental.pallas import tpu as pltpu
from jax.sharding import PartitionSpec as P

LAYERS = 6
GATE = 128
LOW = 256
LOW_BITS = 8
PHASES = 16
PHASE_BITS = 12
LANES = 128
PACKED = 16
TILE = 256
PAIRED = Layout(major_to_minor=(1, 0, 2))


def split(x):
    high = x.astype(jnp.bfloat16)
    low = (x - high.astype(jnp.float32)).astype(jnp.bfloat16)
    return high, low


def exchange_order(wide):
    far = list(range(wide // 2, wide, 2))
    near = [k for top in (wide // 4, wide // 8) for k in range(top, 2 * top, 2) if top > 1]
    near += [k for k in range(wide // 2 - 2, 0, -2) if k not in near]
    pairs = []
    for i, k in enumerate(far):
        pairs += [k] + near[i : i + 1] * (i < len(near) - 1)
    pairs += near[-1:]
    return [0] + [k + j for k in pairs for j in range(2)] + [1]


def block_of(ref, k, wide):
    rows = ref.shape[0] // wide
    start = (lax.axis_index("wide") ^ k) * rows
    return ref.at[pl.ds(pl.multiple_of(start, rows), rows)]


def tables_kernel(spect, narrow, re_ref, im_ref, order_ref, pair_ref, angle_ref, gate_ref, turn_ref):
    size = turn_ref.shape[2]
    row = lax.broadcasted_iota(jnp.int32, (size, LOW), 0)
    lane = lax.broadcasted_iota(jnp.int32, (size, LOW), 1)
    r = lax.axis_index("wide") * (spect // narrow) + row // narrow
    turn_ref[0, 0] = jnp.ones((size, LOW), jnp.float32)
    turn_ref[0, 1] = jnp.zeros((size, LOW), jnp.float32)
    for layer in range(LAYERS):
        b = lax.axis_index("narrow") if layer % 2 == 0 else row % narrow
        u = ((r * narrow + b) * LOW + lane) & (2**PHASE_BITS - 1)
        phase = jnp.zeros((size, LOW), jnp.float32)
        for gate in range(PHASES):
            first = u >> jnp.full((size, LOW), pair_ref[layer, 0, gate], jnp.int32)
            second = u >> jnp.full((size, LOW), pair_ref[layer, 1, gate], jnp.int32)
            phase = phase + jnp.where((first & second & 1) == 1, angle_ref[layer, gate], 0.0)
        turn_ref[layer + 1, 0] = jnp.cos(phase)
        turn_ref[layer + 1, 1] = jnp.sin(phase)

    t = lax.broadcasted_iota(jnp.int32, (8, GATE), 1)
    position = lax.broadcasted_iota(jnp.int32, (LOW // 8, 8, GATE), 0) * 8
    position = position + lax.broadcasted_iota(jnp.int32, (LOW // 8, 8, GATE), 1)
    contract = (((1,), (1,)), ((), ()))
    for layer in range(LAYERS):
        source = jnp.zeros((8, GATE), jnp.int32)
        for bit in range(LOW_BITS - 1):
            source = source + (((t >> bit) & 1) << jnp.full((8, GATE), order_ref[layer, bit], jnp.int32))
        half = jnp.int32(1) << order_ref[layer, LOW_BITS - 1]
        hot = jnp.where((position & ~half) == source[None], 1.0, 0.0).reshape(LOW, GATE).astype(jnp.bfloat16)
        for part, ref in enumerate((re_ref, im_ref)):
            for which, piece in enumerate(split(ref[layer])):
                moved = lax.dot_general(hot, piece, contract, preferred_element_type=jnp.float32)
                gate_ref[layer, which, :, part * GATE : (part + 1) * GATE] = moved.astype(jnp.bfloat16)


def exchange_modes(rows, span):
    count = len(rows)
    group = lax.broadcasted_iota(jnp.int32, rows[0].shape, 1) // span
    rows = [pltpu.roll(row, m * span, 1) if m else row for m, row in enumerate(rows)]
    step = 1
    while step < count:
        taken = (group & step) != 0
        rows = [jnp.where(taken, rows[(y + step) % count], rows[y]) for y in range(count)]
        step *= 2
    return [pltpu.roll(rows[-r % count], LANES - r * span, 1) if r else rows[0] for r in range(count)]


def place_kernel(wide, *rest):
    blocks, out_hbm, sem = rest[:wide], rest[wide], rest[wide + 1]
    copies = [
        pltpu.make_async_copy(blocks[i], block_of(out_hbm, k, wide), sem.at[i])
        for i, k in enumerate(exchange_order(wide))
    ]
    for copy in copies:
        copy.start()
    for copy in copies:
        copy.wait()


def layers_kernel(wide, spect, order_ref, x, gate, turn, *rest):
    outs = rest[:wide]
    state, left_high, left_low, spread = rest[wide:]
    me = lax.axis_index("wide")
    count = wide * spect
    span = LOW // wide
    half = wide // 2
    rows_at_once = min(spect, PACKED)
    joined = PACKED // rows_at_once
    tile = min(TILE, count)

    for part in range(2):
        for lanes in range(2):
            state[0, part, :, lanes * LANES : (lanes + 1) * LANES] = x[pl.ds(2 * lanes + part, count, stride=4), :]
    def turned(slot, entry, first, size, offset, lanes):
        rows, lanes = pl.ds(first + offset, size), slice(lanes * LANES, (lanes + 1) * LANES)
        real, imag = state[slot, 0, rows, lanes], state[slot, 1, rows, lanes]
        cosine, sine = turn[entry, 0, :, lanes], turn[entry, 1, :, lanes]
        return real * cosine - imag * sine, real * sine + imag * cosine

    def one_layer(layer, slot):
        for lanes in range(2):
            for top in range(2):
                for offset in range(0, spect, rows_at_once):
                    pieces = [
                        turned(slot, layer, (top * half + m) * spect, rows_at_once, offset, lanes) for m in range(half)
                    ]
                    for part in range(2):
                        rows = exchange_modes([piece[part] for piece in pieces], span)
                        column = part * LOW + top * LANES
                        for g in range(0, half, joined):
                            at = (lanes * half + g) * spect + offset
                            high, low = split(jnp.concatenate(rows[g : g + joined], axis=0))
                            left_high[at : at + PACKED, column : column + LANES] = high
                            left_low[at : at + PACKED, column : column + LANES] = low

        half_bit = jnp.int32(1) << order_ref[layer, LOW_BITS - 1]
        position = lax.broadcasted_iota(jnp.int32, (LOW, GATE), 0)
        kept = jnp.where((position & half_bit) == 0, 1.0, 0.0).astype(jnp.bfloat16)
        for which in range(2):
            for part in range(2):
                piece = gate[layer, which, :, part * GATE : (part + 1) * GATE]
                first = piece * kept
                both = jnp.concatenate([first, piece - first], axis=1)
                spread[which, part] = both
                if part:
                    spread[which, 2] = -both
        factors = [[[spread[which, 0], spread[which, 2]], [spread[which, 1], spread[which, 0]]] for which in range(2)]

        for first in range(0, count, tile):
            rows = slice(first, first + tile)
            terms = jnp.concatenate([left_high[rows], left_low[rows], left_high[rows]], axis=1)
            for part in range(2):
                square = jnp.concatenate(factors[0][part] + factors[0][part] + factors[1][part], axis=0)
                state[1 - slot, part, rows] = jnp.dot(terms, square, preferred_element_type=jnp.float32)

    def two_layers(step, carry):
        one_layer(2 * step, 0)
        one_layer(2 * step + 1, 1)
        return carry

    lax.fori_loop(0, LAYERS // 2, two_layers, 0)

    for i, k in enumerate(exchange_order(wide)):
        first = pl.multiple_of((me ^ k) * spect, spect)
        for offset in range(0, spect, rows_at_once):
            for lanes in range(2):
                for part, piece in enumerate(turned(0, LAYERS, first, rows_at_once, offset, lanes)):
                    outs[i][pl.ds(4 * offset + 2 * lanes + part, rows_at_once, stride=4), :] = piece


def local(state, gate_re, gate_im, bit_orders, phase_pairs, phase_angles):
    wide = lax.axis_size("wide")
    narrow = lax.axis_size("narrow")
    amps = state.shape[1]
    spect = amps // (wide * LOW)
    count = wide * spect

    view = with_layout_constraint(state.reshape(2, amps // LANES, LANES), PAIRED)
    rows = view.transpose(1, 0, 2).reshape(2 * amps // LANES, LANES)
    gathered = lax.all_to_all(rows, "wide", split_axis=0, concat_axis=0, tiled=True)

    in_hbm = pl.BlockSpec(memory_space=pltpu.HBM)
    in_vmem = pl.BlockSpec(memory_space=pltpu.VMEM)
    in_smem = pl.BlockSpec(memory_space=pltpu.SMEM)
    piece = jax.ShapeDtypeStruct((4 * spect, LANES), jnp.float32)
    part_of_vmem = pltpu.CompilerParams(vmem_limit_bytes=24 * 2**20)
    order = exchange_order(wide)

    turns = (LAYERS + 1, 2, min(spect, 2 ** (PHASE_BITS - LOW_BITS)), LOW)
    tables = pl.pallas_call(
        partial(tables_kernel, spect, narrow),
        in_specs=[in_vmem, in_vmem, in_smem, in_smem, in_smem],
        out_specs=[in_vmem] * 2,
        out_shape=[
            jax.ShapeDtypeStruct((LAYERS, 2, LOW, 2 * GATE), jnp.bfloat16),
            jax.ShapeDtypeStruct(turns, jnp.float32),
        ],
        compiler_params=part_of_vmem,
        cost_estimate=pl.CostEstimate(flops=10**9, bytes_accessed=8 * 10**6, transcendentals=10**5),
        name="tables",
    )(gate_re, gate_im, bit_orders, phase_pairs.transpose(0, 2, 1), phase_angles)

    def swap(blocks, ks):
        return [
            lax.ppermute(block, "wide", [(i, i ^ k) for i in range(wide)]) if k else block
            for block, k in zip(blocks, ks)
        ]

    done = pl.pallas_call(
        partial(layers_kernel, wide, spect),
        in_specs=[in_smem] + [in_vmem] * 3,
        out_specs=[in_vmem] * wide,
        out_shape=[piece] * wide,
        scratch_shapes=[
            pltpu.VMEM((2, 2, count, LOW), jnp.float32),
            pltpu.VMEM((count, 2 * LOW), jnp.bfloat16),
            pltpu.VMEM((count, 2 * LOW), jnp.bfloat16),
            pltpu.VMEM((2, 3, LOW, LOW), jnp.bfloat16),
        ],
        compiler_params=part_of_vmem,
        cost_estimate=pl.CostEstimate(flops=5 * 10**9, bytes_accessed=10**7, transcendentals=0),
        name="layers",
    )(bit_orders, gathered, *tables)

    back = pl.pallas_call(
        partial(place_kernel, wide),
        in_specs=[in_vmem] * wide,
        out_specs=in_hbm,
        out_shape=jax.ShapeDtypeStruct(rows.shape, jnp.float32),
        scratch_shapes=[pltpu.SemaphoreType.DMA((wide,))],
        compiler_params=part_of_vmem,
        name="place",
    )(*swap(done, order))
    view = with_layout_constraint(back.reshape(amps // LANES, 2, LANES).transpose(1, 0, 2), PAIRED)
    return view.reshape(2, amps)


def solution(mesh):
    return jax.shard_map(
        local,
        mesh=mesh,
        in_specs=(P(None, ("wide", "narrow")), P(), P(), P(), P(), P()),
        out_specs=P(None, ("wide", "narrow")),
        check_vma=False,
    )
```

```python
from functools import partial

import jax
import jax.numpy as jnp
from jax import lax
from jax.experimental import pallas as pl
from jax.experimental.layout import Layout, with_layout_constraint
from jax.experimental.pallas import tpu as pltpu
from jax.sharding import PartitionSpec as P

LAYERS = 6
GATE = 128
LOW = 256
LOW_BITS = 8
PHASES = 16
PHASE_BITS = 12
LANES = 128
PACKED = 16
TILE = 128
PAIRED = Layout(major_to_minor=(1, 0, 2))


def split(x):
    high = x.astype(jnp.bfloat16)
    low = (x - high.astype(jnp.float32)).astype(jnp.bfloat16)
    return high, low


def exchange_order(wide):
    far = list(range(wide // 2, wide, 2))
    near = [k for top in (wide // 4, wide // 8) for k in range(top, 2 * top, 2) if top > 1]
    near += [k for k in range(wide // 2 - 2, 0, -2) if k not in near]
    pairs = []
    for i, k in enumerate(far):
        pairs += [k] + near[i : i + 1] * (i < len(near) - 1)
    pairs += near[-1:]
    return [0] + [k + j for k in pairs for j in range(2)] + [1]


def block_of(ref, k, wide):
    rows = ref.shape[0] // wide
    start = (lax.axis_index("wide") ^ k) * rows
    return ref.at[pl.ds(pl.multiple_of(start, rows), rows)]


def tables_kernel(spect, narrow, re_ref, im_ref, order_ref, pair_ref, angle_ref, gate_ref, half_ref, turn_ref):
    size = turn_ref.shape[2]
    row = lax.broadcasted_iota(jnp.int32, (size, LOW), 0)
    lane = lax.broadcasted_iota(jnp.int32, (size, LOW), 1)
    r = lax.axis_index("wide") * (spect // narrow) + row // narrow
    turn_ref[0, 0] = jnp.ones((size, LOW), jnp.float32)
    turn_ref[0, 1] = jnp.zeros((size, LOW), jnp.float32)
    for layer in range(LAYERS):
        b = lax.axis_index("narrow") if layer % 2 == 0 else row % narrow
        u = ((r * narrow + b) * LOW + lane) & (2**PHASE_BITS - 1)
        phase = jnp.zeros((size, LOW), jnp.float32)
        for gate in range(PHASES):
            first = u >> jnp.full((size, LOW), pair_ref[layer, 0, gate], jnp.int32)
            second = u >> jnp.full((size, LOW), pair_ref[layer, 1, gate], jnp.int32)
            phase = phase + jnp.where((first & second & 1) == 1, angle_ref[layer, gate], 0.0)
        turn_ref[layer + 1, 0] = jnp.cos(phase)
        turn_ref[layer + 1, 1] = jnp.sin(phase)

    t = lax.broadcasted_iota(jnp.int32, (8, GATE), 1)
    position = lax.broadcasted_iota(jnp.int32, (LOW // 8, 8, GATE), 0) * 8
    position = position + lax.broadcasted_iota(jnp.int32, (LOW // 8, 8, GATE), 1)
    contract = (((1,), (1,)), ((), ()))
    for layer in range(LAYERS):
        source = jnp.zeros((8, GATE), jnp.int32)
        for bit in range(LOW_BITS - 1):
            source = source + (((t >> bit) & 1) << jnp.full((8, GATE), order_ref[layer, bit], jnp.int32))
        half = jnp.int32(1) << order_ref[layer, LOW_BITS - 1]
        half_ref[layer] = jnp.full((8, GATE), half, jnp.int32)
        hot = jnp.where((position & ~half) == source[None], 1.0, 0.0).reshape(LOW, GATE).astype(jnp.bfloat16)
        for part, ref in enumerate((re_ref, im_ref)):
            for which, piece in enumerate(split(ref[layer])):
                moved = lax.dot_general(hot, piece, contract, preferred_element_type=jnp.float32)
                gate_ref[layer, which, :, part * GATE : (part + 1) * GATE] = moved.astype(jnp.bfloat16)


def exchange_modes(rows, span):
    count = len(rows)
    group = lax.broadcasted_iota(jnp.int32, rows[0].shape, 1) // span
    rows = [pltpu.roll(row, m * span, 1) if m else row for m, row in enumerate(rows)]
    step = 1
    while step < count:
        taken = (group & step) != 0
        rows = [jnp.where(taken, rows[(y + step) % count], rows[y]) for y in range(count)]
        step *= 2
    return [pltpu.roll(rows[-r % count], LANES - r * span, 1) if r else rows[0] for r in range(count)]


def place_kernel(wide, *rest):
    blocks, out_hbm, sem = rest[:wide], rest[wide], rest[wide + 1]
    copies = [
        pltpu.make_async_copy(blocks[i], block_of(out_hbm, k, wide), sem.at[i])
        for i, k in enumerate(exchange_order(wide))
    ]
    for copy in copies:
        copy.start()
    for copy in copies:
        copy.wait()


def layers_kernel(wide, spect, x, gate, half_bit, turn, *rest):
    outs = rest[:wide]
    state, left_high, left_low, spread = rest[wide:]
    me = lax.axis_index("wide")
    count = wide * spect
    span = LOW // wide
    half = wide // 2
    rows_at_once = min(spect, PACKED)
    joined = PACKED // rows_at_once
    tile = min(TILE, count // 2)

    for part in range(2):
        for lanes in range(2):
            state[0, part, :, lanes * LANES : (lanes + 1) * LANES] = x[pl.ds(2 * lanes + part, count, stride=4), :]
    def turned(slot, entry, first, size, offset, lanes):
        rows, lanes = pl.ds(first + offset, size), slice(lanes * LANES, (lanes + 1) * LANES)
        real, imag = state[slot, 0, rows, lanes], state[slot, 1, rows, lanes]
        cosine, sine = turn[entry, 0, :, lanes], turn[entry, 1, :, lanes]
        return real * cosine - imag * sine, real * sine + imag * cosine

    def one_layer(layer, slot):
        position = lax.broadcasted_iota(jnp.int32, (LOW // 8, 8, GATE), 0) * 8
        position = position + lax.broadcasted_iota(jnp.int32, (LOW // 8, 8, GATE), 1)
        kept = jnp.where((position & half_bit[layer][None]) == 0, 1.0, 0.0).reshape(LOW, GATE).astype(jnp.bfloat16)
        for which in range(2):
            for part in range(2):
                piece = gate[layer, which, :, part * GATE : (part + 1) * GATE]
                first = piece * kept
                both = jnp.concatenate([first, piece - first], axis=1)
                spread[which, part] = both
                if part:
                    spread[which, 2] = -both
        factors = [[[spread[which, 0], spread[which, 2]], [spread[which, 1], spread[which, 0]]] for which in range(2)]

        def load(lanes, top, offset):
            pieces = [turned(slot, layer, (top * half + m) * spect, rows_at_once, offset, lanes) for m in range(half)]
            for part in range(2):
                rows = exchange_modes([piece[part] for piece in pieces], span)
                column = part * LOW + top * LANES
                for g in range(0, half, joined):
                    at = (lanes * half + g) * spect + offset
                    high, low = split(jnp.concatenate(rows[g : g + joined], axis=0))
                    left_high[at : at + PACKED, column : column + LANES] = high
                    left_low[at : at + PACKED, column : column + LANES] = low

        def multiply(first, part):
            rows = slice(first, first + tile)
            terms = jnp.concatenate([left_high[rows], left_low[rows], left_high[rows]], axis=1)
            square = jnp.concatenate(factors[0][part] + factors[0][part] + factors[1][part], axis=0)
            state[1 - slot, part, rows] = jnp.dot(terms, square, preferred_element_type=jnp.float32)

        loads = [[(lanes, top, offset) for offset in range(0, spect, rows_at_once) for top in range(2)] for lanes in range(2)]
        products = [(first, part) for first in range(0, count, tile) for part in range(2)]
        middle = len(products) // 2
        for args in loads[0]:
            load(*args)
        for i in range(max(middle, len(loads[1]))):
            if i < middle:
                multiply(*products[i])
            if i < len(loads[1]):
                load(*loads[1][i])
        for args in products[middle:]:
            multiply(*args)

    def two_layers(step, carry):
        one_layer(2 * step, 0)
        one_layer(2 * step + 1, 1)
        return carry

    lax.fori_loop(0, LAYERS // 2, two_layers, 0)

    for i, k in enumerate(exchange_order(wide)):
        first = pl.multiple_of((me ^ k) * spect, spect)
        for offset in range(0, spect, rows_at_once):
            for lanes in range(2):
                for part, piece in enumerate(turned(0, LAYERS, first, rows_at_once, offset, lanes)):
                    outs[i][pl.ds(4 * offset + 2 * lanes + part, rows_at_once, stride=4), :] = piece


def local(state, gate_re, gate_im, bit_orders, phase_pairs, phase_angles):
    wide = lax.axis_size("wide")
    narrow = lax.axis_size("narrow")
    amps = state.shape[1]
    spect = amps // (wide * LOW)
    count = wide * spect

    view = with_layout_constraint(state.reshape(2, amps // LANES, LANES), PAIRED)
    rows = view.transpose(1, 0, 2).reshape(2 * amps // LANES, LANES)
    gathered = lax.all_to_all(rows, "wide", split_axis=0, concat_axis=0, tiled=True)

    in_hbm = pl.BlockSpec(memory_space=pltpu.HBM)
    in_vmem = pl.BlockSpec(memory_space=pltpu.VMEM)
    in_smem = pl.BlockSpec(memory_space=pltpu.SMEM)
    piece = jax.ShapeDtypeStruct((4 * spect, LANES), jnp.float32)
    part_of_vmem = pltpu.CompilerParams(vmem_limit_bytes=24 * 2**20)
    order = exchange_order(wide)

    turns = (LAYERS + 1, 2, min(spect, 2 ** (PHASE_BITS - LOW_BITS)), LOW)
    tables = pl.pallas_call(
        partial(tables_kernel, spect, narrow),
        in_specs=[in_vmem, in_vmem, in_smem, in_smem, in_smem],
        out_specs=[in_vmem] * 3,
        out_shape=[
            jax.ShapeDtypeStruct((LAYERS, 2, LOW, 2 * GATE), jnp.bfloat16),
            jax.ShapeDtypeStruct((LAYERS, 8, GATE), jnp.int32),
            jax.ShapeDtypeStruct(turns, jnp.float32),
        ],
        compiler_params=part_of_vmem,
        cost_estimate=pl.CostEstimate(flops=10**9, bytes_accessed=8 * 10**6, transcendentals=10**5),
        name="tables",
    )(gate_re, gate_im, bit_orders, phase_pairs.transpose(0, 2, 1), phase_angles)

    def swap(blocks, ks):
        return [
            lax.ppermute(block, "wide", [(i, i ^ k) for i in range(wide)]) if k else block
            for block, k in zip(blocks, ks)
        ]

    done = pl.pallas_call(
        partial(layers_kernel, wide, spect),
        in_specs=[in_vmem] * 4,
        out_specs=[in_vmem] * wide,
        out_shape=[piece] * wide,
        scratch_shapes=[
            pltpu.VMEM((2, 2, count, LOW), jnp.float32),
            pltpu.VMEM((count, 2 * LOW), jnp.bfloat16),
            pltpu.VMEM((count, 2 * LOW), jnp.bfloat16),
            pltpu.VMEM((2, 3, LOW, LOW), jnp.bfloat16),
        ],
        compiler_params=part_of_vmem,
        cost_estimate=pl.CostEstimate(flops=5 * 10**9, bytes_accessed=10**7, transcendentals=0),
        name="layers",
    )(gathered, *tables)

    back = pl.pallas_call(
        partial(place_kernel, wide),
        in_specs=[in_vmem] * wide,
        out_specs=in_hbm,
        out_shape=jax.ShapeDtypeStruct(rows.shape, jnp.float32),
        scratch_shapes=[pltpu.SemaphoreType.DMA((wide,))],
        compiler_params=part_of_vmem,
        name="place",
    )(*swap(done, order))
    view = with_layout_constraint(back.reshape(amps // LANES, 2, LANES).transpose(1, 0, 2), PAIRED)
    return view.reshape(2, amps)


def solution(mesh):
    return jax.shard_map(
        local,
        mesh=mesh,
        in_specs=(P(None, ("wide", "narrow")), P(), P(), P(), P(), P()),
        out_specs=P(None, ("wide", "narrow")),
        check_vma=False,
    )
```

```python
from functools import partial

import jax
import jax.numpy as jnp
from jax import lax
from jax.experimental import pallas as pl
from jax.experimental.layout import Layout, with_layout_constraint
from jax.experimental.pallas import tpu as pltpu
from jax.sharding import PartitionSpec as P

LAYERS = 6
GATE = 128
LOW = 256
LOW_BITS = 8
PHASES = 16
PHASE_BITS = 12
LANES = 128
PACKED = 16
TILE = 256
PAIRED = Layout(major_to_minor=(1, 0, 2))


def split(x):
    high = x.astype(jnp.bfloat16)
    low = (x - high.astype(jnp.float32)).astype(jnp.bfloat16)
    return high, low


def exchange_order(wide):
    far = list(range(wide // 2, wide, 2))
    near = [k for top in (wide // 4, wide // 8) for k in range(top, 2 * top, 2) if top > 1]
    near += [k for k in range(wide // 2 - 2, 0, -2) if k not in near]
    pairs = []
    for i, k in enumerate(far):
        pairs += [k] + near[i : i + 1] * (i < len(near) - 1)
    pairs += near[-1:]
    return [0] + [k + j for k in pairs for j in range(2)] + [1]


def block_of(ref, k, wide):
    rows = ref.shape[0] // wide
    start = (lax.axis_index("wide") ^ k) * rows
    return ref.at[pl.ds(pl.multiple_of(start, rows), rows)]


def gates_kernel(re_ref, im_ref, order_ref, gate_ref, half_ref):
    t = lax.broadcasted_iota(jnp.int32, (8, GATE), 1)
    position = lax.broadcasted_iota(jnp.int32, (LOW // 8, 8, GATE), 0) * 8
    position = position + lax.broadcasted_iota(jnp.int32, (LOW // 8, 8, GATE), 1)
    contract = (((1,), (1,)), ((), ()))
    for layer in range(LAYERS):
        source = jnp.zeros((8, GATE), jnp.int32)
        for bit in range(LOW_BITS - 1):
            source = source + (((t >> bit) & 1) << jnp.full((8, GATE), order_ref[layer, bit], jnp.int32))
        half = jnp.int32(1) << order_ref[layer, LOW_BITS - 1]
        half_ref[layer] = jnp.full((8, GATE), half, jnp.int32)
        hot = jnp.where((position & ~half) == source[None], 1.0, 0.0).reshape(LOW, GATE).astype(jnp.bfloat16)
        for part, ref in enumerate((re_ref, im_ref)):
            for which, piece in enumerate(split(ref[layer])):
                moved = lax.dot_general(hot, piece, contract, preferred_element_type=jnp.float32)
                gate_ref[layer, which, :, part * GATE : (part + 1) * GATE] = moved.astype(jnp.bfloat16)


def phases_kernel(spect, narrow, pair_ref, angle_ref, half_ref, turn_ref):
    size = turn_ref.shape[2]
    row = lax.broadcasted_iota(jnp.int32, (size, LOW), 0)
    lane = lax.broadcasted_iota(jnp.int32, (size, LOW), 1)
    r = lax.axis_index("wide") * (spect // narrow) + row // narrow
    turn_ref[0, 0] = jnp.ones((size, LOW), jnp.float32)
    turn_ref[0, 1] = jnp.zeros((size, LOW), jnp.float32)
    for layer in range(LAYERS):
        b = lax.axis_index("narrow") if layer % 2 == 0 else row % narrow
        u = ((r * narrow + b) * LOW + lane) & (2**PHASE_BITS - 1)
        phase = jnp.zeros((size, LOW), jnp.float32)
        for gate in range(PHASES):
            first = u >> jnp.full((size, LOW), pair_ref[layer, 0, gate], jnp.int32)
            second = u >> jnp.full((size, LOW), pair_ref[layer, 1, gate], jnp.int32)
            phase = phase + jnp.where((first & second & 1) == 1, angle_ref[layer, gate], 0.0)
        turn_ref[layer + 1, 0] = jnp.cos(phase)
        turn_ref[layer + 1, 1] = jnp.sin(phase)


def exchange_modes(rows, span):
    count = len(rows)
    group = lax.broadcasted_iota(jnp.int32, rows[0].shape, 1) // span
    rows = [pltpu.roll(row, m * span, 1) if m else row for m, row in enumerate(rows)]
    step = 1
    while step < count:
        taken = (group & step) != 0
        rows = [jnp.where(taken, rows[(y + step) % count], rows[y]) for y in range(count)]
        step *= 2
    return [pltpu.roll(rows[-r % count], LANES - r * span, 1) if r else rows[0] for r in range(count)]


def place_kernel(wide, *rest):
    blocks, out_hbm, sem = rest[:wide], rest[wide], rest[wide + 1]
    copies = [
        pltpu.make_async_copy(blocks[i], block_of(out_hbm, k, wide), sem.at[i])
        for i, k in enumerate(exchange_order(wide))
    ]
    for copy in copies:
        copy.start()
    for copy in copies:
        copy.wait()


def layers_kernel(wide, spect, x, gate, half_bit, turn, *rest):
    outs = rest[:wide]
    state, left_high, left_low, spread = rest[wide:]
    me = lax.axis_index("wide")
    count = wide * spect
    span = LOW // wide
    half = wide // 2
    rows_at_once = min(spect, PACKED)
    joined = PACKED // rows_at_once
    tile = min(TILE, count // 2)

    for part in range(2):
        for lanes in range(2):
            state[0, part, :, lanes * LANES : (lanes + 1) * LANES] = x[pl.ds(2 * lanes + part, count, stride=4), :]
    def turned(slot, entry, first, size, offset, lanes):
        rows, lanes = pl.ds(first + offset, size), slice(lanes * LANES, (lanes + 1) * LANES)
        real, imag = state[slot, 0, rows, lanes], state[slot, 1, rows, lanes]
        cosine, sine = turn[entry, 0, :, lanes], turn[entry, 1, :, lanes]
        return real * cosine - imag * sine, real * sine + imag * cosine

    def one_layer(layer, slot):
        position = lax.broadcasted_iota(jnp.int32, (LOW // 8, 8, GATE), 0) * 8
        position = position + lax.broadcasted_iota(jnp.int32, (LOW // 8, 8, GATE), 1)
        kept = jnp.where((position & half_bit[layer][None]) == 0, 1.0, 0.0).reshape(LOW, GATE).astype(jnp.bfloat16)
        for which in range(2):
            for part in range(2):
                piece = gate[layer, which, :, part * GATE : (part + 1) * GATE]
                first = piece * kept
                both = jnp.concatenate([first, piece - first], axis=1)
                spread[which, part] = both
                if part:
                    spread[which, 2] = -both
        factors = [[[spread[which, 0], spread[which, 2]], [spread[which, 1], spread[which, 0]]] for which in range(2)]

        def load(lanes, top, offset):
            pieces = [turned(slot, layer, (top * half + m) * spect, rows_at_once, offset, lanes) for m in range(half)]
            for part in range(2):
                rows = exchange_modes([piece[part] for piece in pieces], span)
                column = part * LOW + top * LANES
                for g in range(0, half, joined):
                    at = (lanes * half + g) * spect + offset
                    high, low = split(jnp.concatenate(rows[g : g + joined], axis=0))
                    left_high[at : at + PACKED, column : column + LANES] = high
                    left_low[at : at + PACKED, column : column + LANES] = low

        def multiply(first, part):
            rows = slice(first, first + tile)
            terms = jnp.concatenate([left_high[rows], left_low[rows], left_high[rows]], axis=1)
            square = jnp.concatenate(factors[0][part] + factors[0][part] + factors[1][part], axis=0)
            state[1 - slot, part, rows] = jnp.dot(terms, square, preferred_element_type=jnp.float32)

        loads = [[(lanes, top, offset) for offset in range(0, spect, rows_at_once) for top in range(2)] for lanes in range(2)]
        products = [(first, part) for first in range(0, count, tile) for part in range(2)]
        middle = len(products) // 2
        for args in loads[0]:
            load(*args)
        for i in range(max(middle, len(loads[1]))):
            if i < middle:
                multiply(*products[i])
            if i < len(loads[1]):
                load(*loads[1][i])
        for args in products[middle:]:
            multiply(*args)

    def two_layers(step, carry):
        one_layer(2 * step, 0)
        one_layer(2 * step + 1, 1)
        return carry

    lax.fori_loop(0, LAYERS // 2, two_layers, 0)

    for i, k in enumerate(exchange_order(wide)):
        first = pl.multiple_of((me ^ k) * spect, spect)
        for offset in range(0, spect, rows_at_once):
            for lanes in range(2):
                for part, piece in enumerate(turned(0, LAYERS, first, rows_at_once, offset, lanes)):
                    outs[i][pl.ds(4 * offset + 2 * lanes + part, rows_at_once, stride=4), :] = piece


def local(state, gate_re, gate_im, bit_orders, phase_pairs, phase_angles):
    wide = lax.axis_size("wide")
    narrow = lax.axis_size("narrow")
    amps = state.shape[1]
    spect = amps // (wide * LOW)
    count = wide * spect

    view = with_layout_constraint(state.reshape(2, amps // LANES, LANES), PAIRED)
    rows = view.transpose(1, 0, 2).reshape(2 * amps // LANES, LANES)
    gathered = lax.all_to_all(rows, "wide", split_axis=0, concat_axis=0, tiled=True)

    in_hbm = pl.BlockSpec(memory_space=pltpu.HBM)
    in_vmem = pl.BlockSpec(memory_space=pltpu.VMEM)
    in_smem = pl.BlockSpec(memory_space=pltpu.SMEM)
    piece = jax.ShapeDtypeStruct((4 * spect, LANES), jnp.float32)
    part_of_vmem = pltpu.CompilerParams(vmem_limit_bytes=24 * 2**20)
    order = exchange_order(wide)

    turns = (LAYERS + 1, 2, min(spect, 2 ** (PHASE_BITS - LOW_BITS)), LOW)
    gate, half_bit = pl.pallas_call(
        gates_kernel,
        in_specs=[in_vmem, in_vmem, in_smem],
        out_specs=[in_vmem] * 2,
        out_shape=[
            jax.ShapeDtypeStruct((LAYERS, 2, LOW, 2 * GATE), jnp.bfloat16),
            jax.ShapeDtypeStruct((LAYERS, 8, GATE), jnp.int32),
        ],
        compiler_params=part_of_vmem,
        cost_estimate=pl.CostEstimate(flops=10**9, bytes_accessed=4 * 10**6, transcendentals=0),
        name="gates",
    )(gate_re, gate_im, bit_orders)
    turn = pl.pallas_call(
        partial(phases_kernel, spect, narrow),
        in_specs=[in_smem, in_smem, in_vmem],
        out_specs=in_vmem,
        out_shape=jax.ShapeDtypeStruct(turns, jnp.float32),
        compiler_params=part_of_vmem,
        cost_estimate=pl.CostEstimate(flops=10**8, bytes_accessed=10**6, transcendentals=10**5),
        name="phases",
    )(phase_pairs.transpose(0, 2, 1), phase_angles, half_bit)

    def swap(blocks, ks):
        return [
            lax.ppermute(block, "wide", [(i, i ^ k) for i in range(wide)]) if k else block
            for block, k in zip(blocks, ks)
        ]

    done = pl.pallas_call(
        partial(layers_kernel, wide, spect),
        in_specs=[in_vmem] * 4,
        out_specs=[in_vmem] * wide,
        out_shape=[piece] * wide,
        scratch_shapes=[
            pltpu.VMEM((2, 2, count, LOW), jnp.float32),
            pltpu.VMEM((count, 2 * LOW), jnp.bfloat16),
            pltpu.VMEM((count, 2 * LOW), jnp.bfloat16),
            pltpu.VMEM((2, 3, LOW, LOW), jnp.bfloat16),
        ],
        compiler_params=part_of_vmem,
        cost_estimate=pl.CostEstimate(flops=5 * 10**9, bytes_accessed=10**7, transcendentals=0),
        name="layers",
    )(gathered, gate, half_bit, turn)

    back = pl.pallas_call(
        partial(place_kernel, wide),
        in_specs=[in_vmem] * wide,
        out_specs=in_hbm,
        out_shape=jax.ShapeDtypeStruct(rows.shape, jnp.float32),
        scratch_shapes=[pltpu.SemaphoreType.DMA((wide,))],
        compiler_params=part_of_vmem,
        name="place",
    )(*swap(done, order))
    view = with_layout_constraint(back.reshape(amps // LANES, 2, LANES).transpose(1, 0, 2), PAIRED)
    return view.reshape(2, amps)


def solution(mesh):
    return jax.shard_map(
        local,
        mesh=mesh,
        in_specs=(P(None, ("wide", "narrow")), P(), P(), P(), P(), P()),
        out_specs=P(None, ("wide", "narrow")),
        check_vma=False,
    )
```

```python
from functools import partial

import jax
import jax.numpy as jnp
from jax import lax
from jax.experimental import pallas as pl
from jax.experimental.layout import Layout, with_layout_constraint
from jax.experimental.pallas import tpu as pltpu
from jax.sharding import PartitionSpec as P

LAYERS = 6
GATE = 128
LOW = 256
LOW_BITS = 8
PHASES = 16
PHASE_BITS = 12
LANES = 128
PACKED = 16
TILE = 128
PAIRED = Layout(major_to_minor=(1, 0, 2))


def split(x):
    high = x.astype(jnp.bfloat16)
    low = (x - high.astype(jnp.float32)).astype(jnp.bfloat16)
    return high, low


def exchange_order(wide):
    far = list(range(wide // 2, wide, 2))
    near = [k for top in (wide // 4, wide // 8) for k in range(top, 2 * top, 2) if top > 1]
    near += [k for k in range(wide // 2 - 2, 0, -2) if k not in near]
    pairs = []
    for i, k in enumerate(far):
        pairs += [k] + near[i : i + 1] * (i < len(near) - 1)
    pairs += near[-1:]
    return [0] + [k + j for k in pairs for j in range(2)] + [1]


def block_of(ref, k, wide):
    rows = ref.shape[0] // wide
    start = (lax.axis_index("wide") ^ k) * rows
    return ref.at[pl.ds(pl.multiple_of(start, rows), rows)]


def gates_kernel(re_ref, im_ref, order_ref, gate_ref):
    j = lax.broadcasted_iota(jnp.int32, (8, GATE), 1)
    position = lax.broadcasted_iota(jnp.int32, (GATE // 8, 8, GATE), 0) * 8
    position = position + lax.broadcasted_iota(jnp.int32, (GATE // 8, 8, GATE), 1)
    contract = (((1,), (1,)), ((), ()))
    top = LOW_BITS - 1
    for layer in range(LAYERS):
        source = jnp.zeros((8, GATE), jnp.int32)
        for bit in range(top):
            place = order_ref[layer, bit]
            place = jnp.where(place == top, order_ref[layer, top], place)
            source = source + (((j >> bit) & 1) << jnp.full((8, GATE), place, jnp.int32))
        hot = jnp.where(position == source[None], 1.0, 0.0).reshape(GATE, GATE).astype(jnp.bfloat16)
        for part, ref in enumerate((re_ref, im_ref)):
            for which, piece in enumerate(split(ref[layer])):
                moved = lax.dot_general(hot, piece, contract, preferred_element_type=jnp.float32)
                gate_ref[layer, which, :, part * GATE : (part + 1) * GATE] = moved.astype(jnp.bfloat16)


def phases_kernel(spect, narrow, pair_ref, angle_ref, turn_ref):
    size = turn_ref.shape[2]
    row = lax.broadcasted_iota(jnp.int32, (size, LOW), 0)
    lane = lax.broadcasted_iota(jnp.int32, (size, LOW), 1)
    r = lax.axis_index("wide") * (spect // narrow) + row // narrow
    for layer in range(LAYERS):
        b = lax.axis_index("narrow") if layer % 2 == 0 else row % narrow
        u = ((r * narrow + b) * LOW + lane) & (2**PHASE_BITS - 1)
        phase = jnp.zeros((size, LOW), jnp.float32)
        for gate in range(PHASES):
            first = u >> jnp.full((size, LOW), pair_ref[layer, 0, gate], jnp.int32)
            second = u >> jnp.full((size, LOW), pair_ref[layer, 1, gate], jnp.int32)
            phase = phase + jnp.where((first & second & 1) == 1, angle_ref[layer, gate], 0.0)
        turn_ref[layer, 0] = jnp.cos(phase)
        turn_ref[layer, 1] = jnp.sin(phase)


def exchange_modes(rows, span):
    count = len(rows)
    group = lax.broadcasted_iota(jnp.int32, rows[0].shape, 1) // span
    rows = [pltpu.roll(row, m * span, 1) if m else row for m, row in enumerate(rows)]
    step = 1
    while step < count:
        taken = (group & step) != 0
        rows = [jnp.where(taken, rows[(y + step) % count], rows[y]) for y in range(count)]
        step *= 2
    return [pltpu.roll(rows[-r % count], LANES - r * span, 1) if r else rows[0] for r in range(count)]


def place_kernel(wide, *rest):
    blocks, out_hbm, sem = rest[:wide], rest[wide], rest[wide + 1]
    copies = [
        pltpu.make_async_copy(blocks[i], block_of(out_hbm, k, wide), sem.at[i])
        for i, k in enumerate(exchange_order(wide))
    ]
    for copy in copies:
        copy.start()
    for copy in copies:
        copy.wait()


def exchange_top(x0, x1, shift):
    at = lax.broadcasted_iota(jnp.int32, x0.shape, 1) & shift
    back = (LANES - shift) & (LANES - 1)
    forth = shift & (LANES - 1)
    return jnp.where(at != 0, pltpu.roll(x1, forth, 1), x0), jnp.where(at == forth, x1, pltpu.roll(x0, back, 1))


def layers_kernel(wide, spect, order_ref, x, gate, turn, *rest):
    outs = rest[:wide]
    state, left_high, left_low, factor = rest[wide:]
    me = lax.axis_index("wide")
    count = wide * spect
    span = LOW // wide
    half = wide // 2
    rows_at_once = min(spect, PACKED)
    joined = PACKED // rows_at_once
    tile = min(TILE, count)
    distinct = turn.shape[2]

    for part in range(2):
        for lanes in range(2):
            state[0, part, :, lanes * LANES : (lanes + 1) * LANES] = x[pl.ds(2 * lanes + part, count, stride=4), :]

    def one_layer(layer, slot):
        for which in range(2):
            factor[which, :GATE] = gate[layer, which]
            factor[which, GATE:, :GATE] = -gate[layer, which, :, GATE:]
            factor[which, GATE:, GATE:] = gate[layer, which, :, :GATE]

        shift = jnp.int32(1) << order_ref[layer, LOW_BITS - 1]
        for lanes in range(2):
            for part in range(2):
                for offset in range(0, spect, rows_at_once):
                    tops = []
                    for top in range(2):
                        first = top * half * spect + offset
                        pieces = [
                            state[
                                slot,
                                part,
                                first + m * spect : first + m * spect + rows_at_once,
                                lanes * LANES : (lanes + 1) * LANES,
                            ]
                            for m in range(half)
                        ]
                        tops.append(exchange_modes(pieces, span))
                    for g in range(0, half, joined):
                        at = (lanes * half + g) * spect + offset
                        ends = [jnp.concatenate(rows[g : g + joined], axis=0) for rows in tops]
                        for e, piece in enumerate(exchange_top(*ends, shift)):
                            high, low = split(piece)
                            left_high[e, at : at + PACKED, part * LANES : (part + 1) * LANES] = high
                            left_low[e, at : at + PACKED, part * LANES : (part + 1) * LANES] = low

        square = jnp.concatenate([factor[0], factor[0], factor[1]], axis=0)
        for first in range(0, count, tile):
            rows = slice(first, first + tile)
            for e in range(2):
                terms = jnp.concatenate([left_high[e, rows], left_low[e, rows], left_high[e, rows]], axis=1)
                gated = jnp.dot(terms, square, preferred_element_type=jnp.float32)
                real = gated[:, :LANES].reshape(tile // distinct, distinct, LANES)
                imag = gated[:, LANES:].reshape(tile // distinct, distinct, LANES)
                lanes = slice(e * LANES, (e + 1) * LANES)
                cosine, sine = turn[layer, 0, :, lanes][None], turn[layer, 1, :, lanes][None]
                state[1 - slot, 0, rows, lanes] = (real * cosine - imag * sine).reshape(tile, LANES)
                state[1 - slot, 1, rows, lanes] = (real * sine + imag * cosine).reshape(tile, LANES)

    def two_layers(step, carry):
        one_layer(2 * step, 0)
        one_layer(2 * step + 1, 1)
        return carry

    lax.fori_loop(0, LAYERS // 2, two_layers, 0)

    for i, k in enumerate(exchange_order(wide)):
        rows = pl.ds(pl.multiple_of((me ^ k) * spect, spect), spect)
        for part in range(2):
            for lanes in range(2):
                outs[i][pl.ds(2 * lanes + part, spect, stride=4), :] = state[
                    0, part, rows, lanes * LANES : (lanes + 1) * LANES
                ]


def local(state, gate_re, gate_im, bit_orders, phase_pairs, phase_angles):
    wide = lax.axis_size("wide")
    narrow = lax.axis_size("narrow")
    amps = state.shape[1]
    spect = amps // (wide * LOW)
    count = wide * spect

    view = with_layout_constraint(state.reshape(2, amps // LANES, LANES), PAIRED)
    rows = view.transpose(1, 0, 2).reshape(2 * amps // LANES, LANES)
    gathered = lax.all_to_all(rows, "wide", split_axis=0, concat_axis=0, tiled=True)

    in_hbm = pl.BlockSpec(memory_space=pltpu.HBM)
    in_vmem = pl.BlockSpec(memory_space=pltpu.VMEM)
    in_smem = pl.BlockSpec(memory_space=pltpu.SMEM)
    piece = jax.ShapeDtypeStruct((4 * spect, LANES), jnp.float32)
    part_of_vmem = pltpu.CompilerParams(vmem_limit_bytes=24 * 2**20)
    order = exchange_order(wide)

    turns = (LAYERS, 2, min(spect, 2 ** (PHASE_BITS - LOW_BITS)), LOW)
    gate = pl.pallas_call(
        gates_kernel,
        in_specs=[in_vmem, in_vmem, in_smem],
        out_specs=in_vmem,
        out_shape=jax.ShapeDtypeStruct((LAYERS, 2, GATE, 2 * GATE), jnp.bfloat16),
        compiler_params=part_of_vmem,
        cost_estimate=pl.CostEstimate(flops=10**9, bytes_accessed=4 * 10**6, transcendentals=0),
        name="gates",
    )(gate_re, gate_im, bit_orders)
    turn = pl.pallas_call(
        partial(phases_kernel, spect, narrow),
        in_specs=[in_smem, in_smem],
        out_specs=in_vmem,
        out_shape=jax.ShapeDtypeStruct(turns, jnp.float32),
        compiler_params=part_of_vmem,
        cost_estimate=pl.CostEstimate(flops=10**8, bytes_accessed=10**6, transcendentals=10**5),
        name="phases",
    )(phase_pairs.transpose(0, 2, 1), phase_angles)

    def swap(blocks, ks):
        return [
            lax.ppermute(block, "wide", [(i, i ^ k) for i in range(wide)]) if k else block
            for block, k in zip(blocks, ks)
        ]

    done = pl.pallas_call(
        partial(layers_kernel, wide, spect),
        in_specs=[in_smem] + [in_vmem] * 3,
        out_specs=[in_vmem] * wide,
        out_shape=[piece] * wide,
        scratch_shapes=[
            pltpu.VMEM((2, 2, count, LOW), jnp.float32),
            pltpu.VMEM((2, count, 2 * LANES), jnp.bfloat16),
            pltpu.VMEM((2, count, 2 * LANES), jnp.bfloat16),
            pltpu.VMEM((2, 2 * GATE, 2 * GATE), jnp.bfloat16),
        ],
        compiler_params=part_of_vmem,
        cost_estimate=pl.CostEstimate(flops=5 * 10**9, bytes_accessed=10**7, transcendentals=0),
        name="layers",
    )(bit_orders, gathered, gate, turn)

    back = pl.pallas_call(
        partial(place_kernel, wide),
        in_specs=[in_vmem] * wide,
        out_specs=in_hbm,
        out_shape=jax.ShapeDtypeStruct(rows.shape, jnp.float32),
        scratch_shapes=[pltpu.SemaphoreType.DMA((wide,))],
        compiler_params=part_of_vmem,
        name="place",
    )(*swap(done, order))
    view = with_layout_constraint(back.reshape(amps // LANES, 2, LANES).transpose(1, 0, 2), PAIRED)
    return view.reshape(2, amps)


def solution(mesh):
    return jax.shard_map(
        local,
        mesh=mesh,
        in_specs=(P(None, ("wide", "narrow")), P(), P(), P(), P(), P()),
        out_specs=P(None, ("wide", "narrow")),
        check_vma=False,
    )
```

```python
from functools import partial

import jax
import jax.numpy as jnp
from jax import lax
from jax.experimental import pallas as pl
from jax.experimental.layout import Layout, with_layout_constraint
from jax.experimental.pallas import tpu as pltpu
from jax.sharding import PartitionSpec as P

LAYERS = 6
GATE = 128
LOW = 256
LOW_BITS = 8
PHASES = 16
PHASE_BITS = 12
LANES = 128
PACKED = 16
TILE = 128
PAIRED = Layout(major_to_minor=(1, 0, 2))


def split(x):
    high = x.astype(jnp.bfloat16)
    low = (x - high.astype(jnp.float32)).astype(jnp.bfloat16)
    return high, low


def exchange_order(wide):
    far = list(range(wide // 2, wide, 2))
    near = [k for top in (wide // 4, wide // 8) for k in range(top, 2 * top, 2) if top > 1]
    near += [k for k in range(wide // 2 - 2, 0, -2) if k not in near]
    pairs = []
    for i, k in enumerate(far):
        pairs += [k] + near[i : i + 1] * (i < len(near) - 1)
    pairs += near[-1:]
    return [0] + [k + j for k in pairs for j in range(2)] + [1]


def block_of(ref, k, wide):
    rows = ref.shape[0] // wide
    start = (lax.axis_index("wide") ^ k) * rows
    return ref.at[pl.ds(pl.multiple_of(start, rows), rows)]


def gates_kernel(re_ref, im_ref, order_ref, gate_ref, half_ref):
    t = lax.broadcasted_iota(jnp.int32, (8, GATE), 1)
    position = lax.broadcasted_iota(jnp.int32, (LOW // 8, 8, GATE), 0) * 8
    position = position + lax.broadcasted_iota(jnp.int32, (LOW // 8, 8, GATE), 1)
    contract = (((1,), (1,)), ((), ()))
    for layer in range(LAYERS):
        source = jnp.zeros((8, GATE), jnp.int32)
        for bit in range(LOW_BITS - 1):
            source = source + (((t >> bit) & 1) << jnp.full((8, GATE), order_ref[layer, bit], jnp.int32))
        half = jnp.int32(1) << order_ref[layer, LOW_BITS - 1]
        half_ref[layer] = jnp.full((8, GATE), half, jnp.int32)
        hot = jnp.where((position & ~half) == source[None], 1.0, 0.0).reshape(LOW, GATE).astype(jnp.bfloat16)
        for part, ref in enumerate((re_ref, im_ref)):
            for which, piece in enumerate(split(ref[layer])):
                moved = lax.dot_general(hot, piece, contract, preferred_element_type=jnp.float32)
                gate_ref[layer, which, :, part * GATE : (part + 1) * GATE] = moved.astype(jnp.bfloat16)


def phases_kernel(spect, narrow, pair_ref, angle_ref, half_ref, turn_ref):
    size = turn_ref.shape[2]
    row = lax.broadcasted_iota(jnp.int32, (size, LOW), 0)
    lane = lax.broadcasted_iota(jnp.int32, (size, LOW), 1)
    r = lax.axis_index("wide") * (spect // narrow) + row // narrow
    turn_ref[0, 0] = jnp.ones((size, LOW), jnp.float32)
    turn_ref[0, 1] = jnp.zeros((size, LOW), jnp.float32)
    for layer in range(LAYERS):
        b = lax.axis_index("narrow") if layer % 2 == 0 else row % narrow
        u = ((r * narrow + b) * LOW + lane) & (2**PHASE_BITS - 1)
        phase = jnp.zeros((size, LOW), jnp.float32)
        for gate in range(PHASES):
            first = u >> jnp.full((size, LOW), pair_ref[layer, 0, gate], jnp.int32)
            second = u >> jnp.full((size, LOW), pair_ref[layer, 1, gate], jnp.int32)
            phase = phase + jnp.where((first & second & 1) == 1, angle_ref[layer, gate], 0.0)
        turn_ref[layer + 1, 0] = jnp.cos(phase)
        turn_ref[layer + 1, 1] = jnp.sin(phase)


def exchange_modes(rows, span):
    count = len(rows)
    group = lax.broadcasted_iota(jnp.int32, rows[0].shape, 1) // span
    rows = [pltpu.roll(row, m * span, 1) if m else row for m, row in enumerate(rows)]
    step = 1
    while step < count:
        taken = (group & step) != 0
        rows = [jnp.where(taken, rows[(y + step) % count], rows[y]) for y in range(count)]
        step *= 2
    return [pltpu.roll(rows[-r % count], LANES - r * span, 1) if r else rows[0] for r in range(count)]


def place_kernel(wide, *rest):
    blocks, out_hbm, sem = rest[:wide], rest[wide], rest[wide + 1]
    copies = [
        pltpu.make_async_copy(blocks[i], block_of(out_hbm, k, wide), sem.at[i])
        for i, k in enumerate(exchange_order(wide))
    ]
    for copy in copies:
        copy.start()
    for copy in copies:
        copy.wait()


def layers_kernel(wide, spect, x, gate, half_bit, turn, *rest):
    outs = rest[:wide]
    state, left_high, left_low, spread = rest[wide:]
    me = lax.axis_index("wide")
    count = wide * spect
    span = LOW // wide
    half = wide // 2
    rows_at_once = min(spect, PACKED)
    joined = PACKED // rows_at_once
    tile = min(TILE, count // 2)

    for part in range(2):
        for lanes in range(2):
            state[0, part, :, lanes * LANES : (lanes + 1) * LANES] = x[pl.ds(2 * lanes + part, count, stride=4), :]
    def turned(slot, entry, first, size, offset, lanes):
        rows, lanes = pl.ds(first + offset, size), slice(lanes * LANES, (lanes + 1) * LANES)
        real, imag = state[slot, 0, rows, lanes], state[slot, 1, rows, lanes]
        cosine, sine = turn[entry, 0, :, lanes], turn[entry, 1, :, lanes]
        return real * cosine - imag * sine, real * sine + imag * cosine

    def one_layer(layer, slot):
        position = lax.broadcasted_iota(jnp.int32, (LOW // 8, 8, GATE), 0) * 8
        position = position + lax.broadcasted_iota(jnp.int32, (LOW // 8, 8, GATE), 1)
        kept = jnp.where((position & half_bit[layer][None]) == 0, 1.0, 0.0).reshape(LOW, GATE).astype(jnp.bfloat16)
        parts = [[gate[layer, which, :, part * GATE : (part + 1) * GATE] for part in range(2)] for which in range(2)]
        total = parts[0][0].astype(jnp.float32) + parts[0][1].astype(jnp.float32)
        total = total + (parts[1][0].astype(jnp.float32) + parts[1][1].astype(jnp.float32))
        for which, piece in enumerate(split(total)):
            for i, values in enumerate(parts[which] + [piece]):
                first = values * kept
                spread[which, i] = jnp.concatenate([first, values - first], axis=1)

        def load(lanes, top, offset):
            pieces = [turned(slot, layer, (top * half + m) * spect, rows_at_once, offset, lanes) for m in range(half)]
            reals, imags = (exchange_modes([piece[part] for piece in pieces], span) for part in range(2))
            for g in range(0, half, joined):
                at = (lanes * half + g) * spect + offset
                real = jnp.concatenate(reals[g : g + joined], axis=0)
                imag = jnp.concatenate(imags[g : g + joined], axis=0)
                for i, values in enumerate((real, imag, real + imag)):
                    high, low = split(values)
                    left_high[i, at : at + PACKED, top * LANES : (top + 1) * LANES] = high
                    left_low[i, at : at + PACKED, top * LANES : (top + 1) * LANES] = low

        def product(i, rows):
            terms = jnp.concatenate([left_high[i, rows], left_low[i, rows], left_high[i, rows]], axis=1)
            square = jnp.concatenate([spread[0, i], spread[0, i], spread[1, i]], axis=0)
            return jnp.dot(terms, square, preferred_element_type=jnp.float32)

        def multiply(first):
            rows = slice(first, first + tile)
            real, imag = product(0, rows), product(1, rows)
            state[1 - slot, 0, rows] = real - imag
            state[1 - slot, 1, rows] = product(2, rows) - (real + imag)

        loads = [[(lanes, top, offset) for offset in range(0, spect, rows_at_once) for top in range(2)] for lanes in range(2)]
        products = [(first,) for first in range(0, count, tile)]
        middle = len(products) // 2
        for args in loads[0]:
            load(*args)
        for i in range(max(middle, len(loads[1]))):
            if i < middle:
                multiply(*products[i])
            if i < len(loads[1]):
                load(*loads[1][i])
        for args in products[middle:]:
            multiply(*args)

    def two_layers(step, carry):
        one_layer(2 * step, 0)
        one_layer(2 * step + 1, 1)
        return carry

    lax.fori_loop(0, LAYERS // 2, two_layers, 0)

    for i, k in enumerate(exchange_order(wide)):
        first = pl.multiple_of((me ^ k) * spect, spect)
        for offset in range(0, spect, rows_at_once):
            for lanes in range(2):
                for part, piece in enumerate(turned(0, LAYERS, first, rows_at_once, offset, lanes)):
                    outs[i][pl.ds(4 * offset + 2 * lanes + part, rows_at_once, stride=4), :] = piece


def local(state, gate_re, gate_im, bit_orders, phase_pairs, phase_angles):
    wide = lax.axis_size("wide")
    narrow = lax.axis_size("narrow")
    amps = state.shape[1]
    spect = amps // (wide * LOW)
    count = wide * spect

    view = with_layout_constraint(state.reshape(2, amps // LANES, LANES), PAIRED)
    rows = view.transpose(1, 0, 2).reshape(2 * amps // LANES, LANES)
    gathered = lax.all_to_all(rows, "wide", split_axis=0, concat_axis=0, tiled=True)

    in_hbm = pl.BlockSpec(memory_space=pltpu.HBM)
    in_vmem = pl.BlockSpec(memory_space=pltpu.VMEM)
    in_smem = pl.BlockSpec(memory_space=pltpu.SMEM)
    piece = jax.ShapeDtypeStruct((4 * spect, LANES), jnp.float32)
    part_of_vmem = pltpu.CompilerParams(vmem_limit_bytes=24 * 2**20)
    order = exchange_order(wide)

    turns = (LAYERS + 1, 2, min(spect, 2 ** (PHASE_BITS - LOW_BITS)), LOW)
    gate, half_bit = pl.pallas_call(
        gates_kernel,
        in_specs=[in_vmem, in_vmem, in_smem],
        out_specs=[in_vmem] * 2,
        out_shape=[
            jax.ShapeDtypeStruct((LAYERS, 2, LOW, 2 * GATE), jnp.bfloat16),
            jax.ShapeDtypeStruct((LAYERS, 8, GATE), jnp.int32),
        ],
        compiler_params=part_of_vmem,
        cost_estimate=pl.CostEstimate(flops=10**9, bytes_accessed=4 * 10**6, transcendentals=0),
        name="gates",
    )(gate_re, gate_im, bit_orders)
    turn = pl.pallas_call(
        partial(phases_kernel, spect, narrow),
        in_specs=[in_smem, in_smem, in_vmem],
        out_specs=in_vmem,
        out_shape=jax.ShapeDtypeStruct(turns, jnp.float32),
        compiler_params=part_of_vmem,
        cost_estimate=pl.CostEstimate(flops=10**8, bytes_accessed=10**6, transcendentals=10**5),
        name="phases",
    )(phase_pairs.transpose(0, 2, 1), phase_angles, half_bit)

    def swap(blocks, ks):
        return [
            lax.ppermute(block, "wide", [(i, i ^ k) for i in range(wide)]) if k else block
            for block, k in zip(blocks, ks)
        ]

    done = pl.pallas_call(
        partial(layers_kernel, wide, spect),
        in_specs=[in_vmem] * 4,
        out_specs=[in_vmem] * wide,
        out_shape=[piece] * wide,
        scratch_shapes=[
            pltpu.VMEM((2, 2, count, LOW), jnp.float32),
            pltpu.VMEM((3, count, LOW), jnp.bfloat16),
            pltpu.VMEM((3, count, LOW), jnp.bfloat16),
            pltpu.VMEM((2, 3, LOW, LOW), jnp.bfloat16),
        ],
        compiler_params=part_of_vmem,
        cost_estimate=pl.CostEstimate(flops=5 * 10**9, bytes_accessed=10**7, transcendentals=0),
        name="layers",
    )(gathered, gate, half_bit, turn)

    back = pl.pallas_call(
        partial(place_kernel, wide),
        in_specs=[in_vmem] * wide,
        out_specs=in_hbm,
        out_shape=jax.ShapeDtypeStruct(rows.shape, jnp.float32),
        scratch_shapes=[pltpu.SemaphoreType.DMA((wide,))],
        compiler_params=part_of_vmem,
        name="place",
    )(*swap(done, order))
    view = with_layout_constraint(back.reshape(amps // LANES, 2, LANES).transpose(1, 0, 2), PAIRED)
    return view.reshape(2, amps)


def solution(mesh):
    return jax.shard_map(
        local,
        mesh=mesh,
        in_specs=(P(None, ("wide", "narrow")), P(), P(), P(), P(), P()),
        out_specs=P(None, ("wide", "narrow")),
        check_vma=False,
    )
```

```python
from functools import partial

import jax
import jax.numpy as jnp
from jax import lax
from jax.experimental import pallas as pl
from jax.experimental.layout import Layout, with_layout_constraint
from jax.experimental.pallas import tpu as pltpu
from jax.sharding import PartitionSpec as P

LAYERS = 6
GATE = 128
LOW = 256
LOW_BITS = 8
PHASES = 16
PHASE_BITS = 12
LANES = 128
PACKED = 16
TILE = 128
PAIRED = Layout(major_to_minor=(1, 0, 2))


def split(x):
    high = x.astype(jnp.bfloat16)
    low = (x - high.astype(jnp.float32)).astype(jnp.bfloat16)
    return high, low


def exchange_order(wide):
    far = list(range(wide // 2, wide, 2))
    near = [k for low in (wide // 4, wide // 8) for k in range(low, 2 * low, 2) if low > 1]
    near += [k for k in range(wide // 2 - 2, 0, -2) if k not in near]
    pairs = []
    for i, k in enumerate(far):
        pairs += [k] + near[i : i + 1]
    return [0] + [k + j for k in pairs for j in range(2)] + [1]


def block_of(ref, k, wide):
    rows = ref.shape[0] // wide
    start = (lax.axis_index("wide") ^ k) * rows
    return ref.at[pl.ds(pl.multiple_of(start, rows), rows)]


def gates_kernel(re_ref, im_ref, order_ref, gate_ref, half_ref):
    t = lax.broadcasted_iota(jnp.int32, (8, GATE), 1)
    position = lax.broadcasted_iota(jnp.int32, (LOW // 8, 8, GATE), 0) * 8
    position = position + lax.broadcasted_iota(jnp.int32, (LOW // 8, 8, GATE), 1)
    contract = (((1,), (1,)), ((), ()))
    for layer in range(LAYERS):
        source = jnp.zeros((8, GATE), jnp.int32)
        for bit in range(LOW_BITS - 1):
            source = source + (((t >> bit) & 1) << jnp.full((8, GATE), order_ref[layer, bit], jnp.int32))
        half = jnp.int32(1) << order_ref[layer, LOW_BITS - 1]
        half_ref[layer] = jnp.full((8, GATE), half, jnp.int32)
        hot = jnp.where((position & ~half) == source[None], 1.0, 0.0).reshape(LOW, GATE).astype(jnp.bfloat16)
        for part, ref in enumerate((re_ref, im_ref)):
            for which, piece in enumerate(split(ref[layer])):
                moved = lax.dot_general(hot, piece, contract, preferred_element_type=jnp.float32)
                gate_ref[layer, which, :, part * GATE : (part + 1) * GATE] = moved.astype(jnp.bfloat16)


def phases_kernel(spect, narrow, pair_ref, angle_ref, half_ref, turn_ref):
    size = turn_ref.shape[2]
    row = lax.broadcasted_iota(jnp.int32, (size, LOW), 0)
    lane = lax.broadcasted_iota(jnp.int32, (size, LOW), 1)
    r = lax.axis_index("wide") * (spect // narrow) + row // narrow
    turn_ref[0, 0] = jnp.ones((size, LOW), jnp.float32)
    turn_ref[0, 1] = jnp.zeros((size, LOW), jnp.float32)
    for layer in range(LAYERS):
        b = lax.axis_index("narrow") if layer % 2 == 0 else row % narrow
        u = ((r * narrow + b) * LOW + lane) & (2**PHASE_BITS - 1)
        phase = jnp.zeros((size, LOW), jnp.float32)
        for gate in range(PHASES):
            first = u >> jnp.full((size, LOW), pair_ref[layer, 0, gate], jnp.int32)
            second = u >> jnp.full((size, LOW), pair_ref[layer, 1, gate], jnp.int32)
            phase = phase + jnp.where((first & second & 1) == 1, angle_ref[layer, gate], 0.0)
        turn_ref[layer + 1, 0] = jnp.cos(phase)
        turn_ref[layer + 1, 1] = jnp.sin(phase)


def exchange_modes(rows, span, taken):
    count = len(rows)
    rows = [pltpu.roll(row, m * span, 1) if m else row for m, row in enumerate(rows)]
    for i, mask in enumerate(taken):
        rows = [jnp.where(mask, rows[(y + (1 << i)) % count], rows[y]) for y in range(count)]
    return [pltpu.roll(rows[-r % count], LANES - r * span, 1) if r else rows[0] for r in range(count)]


def place_kernel(wide, *rest):
    blocks, out_hbm, sem = rest[:wide], rest[wide], rest[wide + 1]
    copies = [
        pltpu.make_async_copy(blocks[i], block_of(out_hbm, k, wide), sem.at[i])
        for i, k in enumerate(exchange_order(wide))
    ]
    for copy in copies:
        copy.start()
    for copy in copies:
        copy.wait()


def layers_kernel(wide, spect, x, gate, half_bit, turn, *rest):
    outs = rest[:wide]
    state, left_high, left_low, spread = rest[wide:]
    me = lax.axis_index("wide")
    count = wide * spect
    span = LOW // wide
    half = wide // 2
    rows_at_once = min(spect, PACKED)
    joined = PACKED // rows_at_once
    tile = min(TILE, count // 2)

    for part in range(2):
        for lanes in range(2):
            state[0, part, :, lanes * LANES : (lanes + 1) * LANES] = x[pl.ds(2 * lanes + part, count, stride=4), :]
    lane = lax.broadcasted_iota(jnp.int32, (rows_at_once, LANES), 1)
    taken = [(lane & (span << i)) != 0 for i in range(half.bit_length() - 1)]

    def turned(slot, entry, firsts, offset, lanes):
        lanes = slice(lanes * LANES, (lanes + 1) * LANES)
        cosine, sine = turn[entry, 0, :, lanes], turn[entry, 1, :, lanes]
        pieces = []
        for first in firsts:
            rows = pl.ds(first + offset, rows_at_once)
            real, imag = state[slot, 0, rows, lanes], state[slot, 1, rows, lanes]
            pieces.append((real * cosine - imag * sine, real * sine + imag * cosine))
        return pieces

    def one_layer(layer, slot):
        position = lax.broadcasted_iota(jnp.int32, (LOW // 8, 8, GATE), 0) * 8
        position = position + lax.broadcasted_iota(jnp.int32, (LOW // 8, 8, GATE), 1)
        kept = jnp.where((position & half_bit[layer][None]) == 0, 1.0, 0.0).reshape(LOW, GATE).astype(jnp.bfloat16)
        parts = [[gate[layer, which, :, part * GATE : (part + 1) * GATE] for part in range(2)] for which in range(2)]
        total = parts[0][0].astype(jnp.float32) + parts[0][1].astype(jnp.float32)
        total = total + (parts[1][0].astype(jnp.float32) + parts[1][1].astype(jnp.float32))
        for which, piece in enumerate(split(total)):
            for i, values in enumerate(parts[which] + [piece]):
                first = values * kept
                spread[which, i] = jnp.concatenate([first, values - first], axis=1)

        def load(lanes, top, offset):
            pieces = turned(slot, layer, [(top * half + m) * spect for m in range(half)], offset, lanes)
            reals, imags = (exchange_modes([piece[part] for piece in pieces], span, taken) for part in range(2))
            for g in range(0, half, joined):
                at = (lanes * half + g) * spect + offset
                real = jnp.concatenate(reals[g : g + joined], axis=0)
                imag = jnp.concatenate(imags[g : g + joined], axis=0)
                for i, values in enumerate((real, imag, real + imag)):
                    high, low = split(values)
                    left_high[i, at : at + PACKED, top * LANES : (top + 1) * LANES] = high
                    left_low[i, at : at + PACKED, top * LANES : (top + 1) * LANES] = low

        def product(i, rows):
            terms = jnp.concatenate([left_high[i, rows], left_low[i, rows], left_high[i, rows]], axis=1)
            square = jnp.concatenate([spread[0, i], spread[0, i], spread[1, i]], axis=0)
            return jnp.dot(terms, square, preferred_element_type=jnp.float32)

        def multiply(first):
            rows = slice(first, first + tile)
            real, imag = product(0, rows), product(1, rows)
            state[1 - slot, 0, rows] = real - imag
            state[1 - slot, 1, rows] = product(2, rows) - (real + imag)

        loads = [[(lanes, top, offset) for offset in range(0, spect, rows_at_once) for top in range(2)] for lanes in range(2)]
        products = [(first,) for first in range(0, count, tile)]
        middle = len(products) // 2
        for args in loads[0]:
            load(*args)
        for i in range(max(middle, len(loads[1]))):
            if i < middle:
                multiply(*products[i])
            if i < len(loads[1]):
                load(*loads[1][i])
        for args in products[middle:]:
            multiply(*args)

    def two_layers(step, carry):
        one_layer(2 * step, 0)
        one_layer(2 * step + 1, 1)
        return carry

    lax.fori_loop(0, LAYERS // 2, two_layers, 0)

    firsts = [pl.multiple_of((me ^ k) * spect, spect) for k in exchange_order(wide)]
    for offset in range(0, spect, rows_at_once):
        for lanes in range(2):
            for i, pieces in enumerate(turned(0, LAYERS, firsts, offset, lanes)):
                for part, piece in enumerate(pieces):
                    outs[i][pl.ds(4 * offset + 2 * lanes + part, rows_at_once, stride=4), :] = piece


def local(state, gate_re, gate_im, bit_orders, phase_pairs, phase_angles):
    wide = lax.axis_size("wide")
    narrow = lax.axis_size("narrow")
    amps = state.shape[1]
    spect = amps // (wide * LOW)
    count = wide * spect

    view = with_layout_constraint(state.reshape(2, amps // LANES, LANES), PAIRED)
    rows = view.transpose(1, 0, 2).reshape(2 * amps // LANES, LANES)
    gathered = lax.all_to_all(rows, "wide", split_axis=0, concat_axis=0, tiled=True)

    in_hbm = pl.BlockSpec(memory_space=pltpu.HBM)
    in_vmem = pl.BlockSpec(memory_space=pltpu.VMEM)
    in_smem = pl.BlockSpec(memory_space=pltpu.SMEM)
    piece = jax.ShapeDtypeStruct((4 * spect, LANES), jnp.float32)
    part_of_vmem = pltpu.CompilerParams(vmem_limit_bytes=24 * 2**20)
    order = exchange_order(wide)

    turns = (LAYERS + 1, 2, min(spect, 2 ** (PHASE_BITS - LOW_BITS)), LOW)
    gate, half_bit = pl.pallas_call(
        gates_kernel,
        in_specs=[in_vmem, in_vmem, in_smem],
        out_specs=[in_vmem] * 2,
        out_shape=[
            jax.ShapeDtypeStruct((LAYERS, 2, LOW, 2 * GATE), jnp.bfloat16),
            jax.ShapeDtypeStruct((LAYERS, 8, GATE), jnp.int32),
        ],
        compiler_params=part_of_vmem,
        cost_estimate=pl.CostEstimate(flops=10**9, bytes_accessed=4 * 10**6, transcendentals=0),
        name="gates",
    )(gate_re, gate_im, bit_orders)
    turn = pl.pallas_call(
        partial(phases_kernel, spect, narrow),
        in_specs=[in_smem, in_smem, in_vmem],
        out_specs=in_vmem,
        out_shape=jax.ShapeDtypeStruct(turns, jnp.float32),
        compiler_params=part_of_vmem,
        cost_estimate=pl.CostEstimate(flops=10**8, bytes_accessed=10**6, transcendentals=10**5),
        name="phases",
    )(phase_pairs.transpose(0, 2, 1), phase_angles, half_bit)

    def swap(blocks, ks):
        return [
            lax.ppermute(block, "wide", [(i, i ^ k) for i in range(wide)]) if k else block
            for block, k in zip(blocks, ks)
        ]

    done = pl.pallas_call(
        partial(layers_kernel, wide, spect),
        in_specs=[in_vmem] * 4,
        out_specs=[in_vmem] * wide,
        out_shape=[piece] * wide,
        scratch_shapes=[
            pltpu.VMEM((2, 2, count, LOW), jnp.float32),
            pltpu.VMEM((3, count, LOW), jnp.bfloat16),
            pltpu.VMEM((3, count, LOW), jnp.bfloat16),
            pltpu.VMEM((2, 3, LOW, LOW), jnp.bfloat16),
        ],
        compiler_params=part_of_vmem,
        cost_estimate=pl.CostEstimate(flops=5 * 10**9, bytes_accessed=10**7, transcendentals=0),
        name="layers",
    )(gathered, gate, half_bit, turn)

    back = pl.pallas_call(
        partial(place_kernel, wide),
        in_specs=[in_vmem] * wide,
        out_specs=in_hbm,
        out_shape=jax.ShapeDtypeStruct(rows.shape, jnp.float32),
        scratch_shapes=[pltpu.SemaphoreType.DMA((wide,))],
        compiler_params=part_of_vmem,
        name="place",
    )(*swap(done, order))
    view = with_layout_constraint(back.reshape(amps // LANES, 2, LANES).transpose(1, 0, 2), PAIRED)
    return view.reshape(2, amps)


def solution(mesh):
    return jax.shard_map(
        local,
        mesh=mesh,
        in_specs=(P(None, ("wide", "narrow")), P(), P(), P(), P(), P()),
        out_specs=P(None, ("wide", "narrow")),
        check_vma=False,
    )
```

```python
from functools import partial

import jax
import jax.numpy as jnp
from jax import lax
from jax.experimental import pallas as pl
from jax.experimental.layout import Layout, with_layout_constraint
from jax.experimental.pallas import tpu as pltpu
from jax.sharding import PartitionSpec as P

LAYERS = 6
GATE = 128
LOW = 256
LOW_BITS = 8
PHASES = 16
PHASE_BITS = 12
LANES = 128
PACKED = 16
TILE = 128
PAIRED = Layout(major_to_minor=(1, 0, 2))


def split(x):
    high = x.astype(jnp.bfloat16)
    low = (x - high.astype(jnp.float32)).astype(jnp.bfloat16)
    return high, low


def exchange_order(wide):
    far = list(range(wide // 2, wide, 2))
    near = [k for top in (wide // 4, wide // 8) for k in range(top, 2 * top, 2) if top > 1]
    near += [k for k in range(wide // 2 - 2, 0, -2) if k not in near]
    pairs = []
    for i, k in enumerate(far):
        pairs += [k] + near[i : i + 1] * (i < len(near) - 1)
    pairs += near[-1:]
    return [0] + [k + j for k in pairs for j in range(2)] + [1]


def block_of(ref, k, wide):
    rows = ref.shape[0] // wide
    start = (lax.axis_index("wide") ^ k) * rows
    return ref.at[pl.ds(pl.multiple_of(start, rows), rows)]


def gates_kernel(re_ref, im_ref, order_ref, gate_ref, half_ref):
    t = lax.broadcasted_iota(jnp.int32, (8, GATE), 1)
    position = lax.broadcasted_iota(jnp.int32, (LOW // 8, 8, GATE), 0) * 8
    position = position + lax.broadcasted_iota(jnp.int32, (LOW // 8, 8, GATE), 1)
    contract = (((1,), (1,)), ((), ()))
    for layer in range(LAYERS):
        source = jnp.zeros((8, GATE), jnp.int32)
        for bit in range(LOW_BITS - 1):
            source = source + (((t >> bit) & 1) << jnp.full((8, GATE), order_ref[layer, bit], jnp.int32))
        half = jnp.int32(1) << order_ref[layer, LOW_BITS - 1]
        half_ref[layer] = jnp.full((8, GATE), half, jnp.int32)
        hot = jnp.where((position & ~half) == source[None], 1.0, 0.0).reshape(LOW, GATE).astype(jnp.bfloat16)
        for part, ref in enumerate((re_ref, im_ref)):
            for which, piece in enumerate(split(ref[layer])):
                moved = lax.dot_general(hot, piece, contract, preferred_element_type=jnp.float32)
                gate_ref[layer, which, :, part * GATE : (part + 1) * GATE] = moved.astype(jnp.bfloat16)


def phases_kernel(spect, narrow, pair_ref, angle_ref, half_ref, turn_ref):
    size = turn_ref.shape[2]
    row = lax.broadcasted_iota(jnp.int32, (size, LOW), 0)
    lane = lax.broadcasted_iota(jnp.int32, (size, LOW), 1)
    r = lax.axis_index("wide") * (spect // narrow) + row // narrow
    turn_ref[0, 0] = jnp.ones((size, LOW), jnp.float32)
    turn_ref[0, 1] = jnp.zeros((size, LOW), jnp.float32)
    for layer in range(LAYERS):
        b = lax.axis_index("narrow") if layer % 2 == 0 else row % narrow
        u = ((r * narrow + b) * LOW + lane) & (2**PHASE_BITS - 1)
        phase = jnp.zeros((size, LOW), jnp.float32)
        for gate in range(PHASES):
            first = u >> jnp.full((size, LOW), pair_ref[layer, 0, gate], jnp.int32)
            second = u >> jnp.full((size, LOW), pair_ref[layer, 1, gate], jnp.int32)
            phase = phase + jnp.where((first & second & 1) == 1, angle_ref[layer, gate], 0.0)
        turn_ref[layer + 1, 0] = jnp.cos(phase)
        turn_ref[layer + 1, 1] = jnp.sin(phase)


def exchange_modes(rows, span, taken):
    count = len(rows)
    rows = [pltpu.roll(row, m * span, 1) if m else row for m, row in enumerate(rows)]
    for i, mask in enumerate(taken):
        rows = [jnp.where(mask, rows[(y + (1 << i)) % count], rows[y]) for y in range(count)]
    return [pltpu.roll(rows[-r % count], LANES - r * span, 1) if r else rows[0] for r in range(count)]


def place_kernel(wide, *rest):
    blocks, out_hbm, sem = rest[:wide], rest[wide], rest[wide + 1]
    copies = [
        pltpu.make_async_copy(blocks[i], block_of(out_hbm, k, wide), sem.at[i])
        for i, k in enumerate(exchange_order(wide))
    ]
    for copy in copies:
        copy.start()
    for copy in copies:
        copy.wait()


def layers_kernel(wide, spect, x, gate, half_bit, turn, *rest):
    outs = rest[:wide]
    state, left_high, left_low, spread = rest[wide:]
    me = lax.axis_index("wide")
    count = wide * spect
    span = LOW // wide
    half = wide // 2
    rows_at_once = min(spect, PACKED)
    joined = PACKED // rows_at_once
    tile = min(TILE, count // 2)

    for part in range(2):
        for lanes in range(2):
            state[0, part, :, lanes * LANES : (lanes + 1) * LANES] = x[pl.ds(2 * lanes + part, count, stride=4), :]
    lane = lax.broadcasted_iota(jnp.int32, (rows_at_once, LANES), 1)
    taken = [(lane & (span << i)) != 0 for i in range(half.bit_length() - 1)]

    def turned(slot, entry, firsts, offset, lanes):
        lanes = slice(lanes * LANES, (lanes + 1) * LANES)
        cosine, sine = turn[entry, 0, :, lanes], turn[entry, 1, :, lanes]
        pieces = []
        for first in firsts:
            rows = pl.ds(first + offset, rows_at_once)
            real, imag = state[slot, 0, rows, lanes], state[slot, 1, rows, lanes]
            pieces.append((real * cosine - imag * sine, real * sine + imag * cosine))
        return pieces

    def one_layer(layer, slot):
        position = lax.broadcasted_iota(jnp.int32, (LOW // 8, 8, GATE), 0) * 8
        position = position + lax.broadcasted_iota(jnp.int32, (LOW // 8, 8, GATE), 1)
        kept = jnp.where((position & half_bit[layer][None]) == 0, 1.0, 0.0).reshape(LOW, GATE).astype(jnp.bfloat16)
        parts = [[gate[layer, which, :, part * GATE : (part + 1) * GATE] for part in range(2)] for which in range(2)]
        total = parts[0][0].astype(jnp.float32) + parts[0][1].astype(jnp.float32)
        total = total + (parts[1][0].astype(jnp.float32) + parts[1][1].astype(jnp.float32))
        for which, piece in enumerate(split(total)):
            for i, values in enumerate(parts[which] + [piece]):
                first = values * kept
                spread[which, i] = jnp.concatenate([first, values - first], axis=1)

        def load(lanes, top, offset):
            pieces = turned(slot, layer, [(top * half + m) * spect for m in range(half)], offset, lanes)
            reals, imags = (exchange_modes([piece[part] for piece in pieces], span, taken) for part in range(2))
            for g in range(0, half, joined):
                at = (lanes * half + g) * spect + offset
                real = jnp.concatenate(reals[g : g + joined], axis=0)
                imag = jnp.concatenate(imags[g : g + joined], axis=0)
                for i, values in enumerate((real, imag, real + imag)):
                    high, low = split(values)
                    left_high[i, at : at + PACKED, top * LANES : (top + 1) * LANES] = high
                    left_low[i, at : at + PACKED, top * LANES : (top + 1) * LANES] = low

        def product(i, rows):
            terms = jnp.concatenate([left_high[i, rows], left_low[i, rows], left_high[i, rows]], axis=1)
            square = jnp.concatenate([spread[0, i], spread[0, i], spread[1, i]], axis=0)
            return jnp.dot(terms, square, preferred_element_type=jnp.float32)

        def multiply(first):
            rows = slice(first, first + tile)
            real, imag = product(0, rows), product(1, rows)
            state[1 - slot, 0, rows] = real - imag
            state[1 - slot, 1, rows] = product(2, rows) - (real + imag)

        loads = [[(lanes, top, offset) for offset in range(0, spect, rows_at_once) for top in range(2)] for lanes in range(2)]
        products = [(first,) for first in range(0, count, tile)]
        middle = len(products) // 2
        for args in loads[0]:
            load(*args)
        for i in range(max(middle, len(loads[1]))):
            if i < middle:
                multiply(*products[i])
            if i < len(loads[1]):
                load(*loads[1][i])
        for args in products[middle:]:
            multiply(*args)

    def step(layer, carry):
        one_layer(layer, layer & 1)
        return carry

    lax.fori_loop(0, LAYERS, step, 0)

    firsts = [pl.multiple_of((me ^ k) * spect, spect) for k in exchange_order(wide)]
    for offset in range(0, spect, rows_at_once):
        for lanes in range(2):
            for i, pieces in enumerate(turned(0, LAYERS, firsts, offset, lanes)):
                for part, piece in enumerate(pieces):
                    outs[i][pl.ds(4 * offset + 2 * lanes + part, rows_at_once, stride=4), :] = piece


def local(state, gate_re, gate_im, bit_orders, phase_pairs, phase_angles):
    wide = lax.axis_size("wide")
    narrow = lax.axis_size("narrow")
    amps = state.shape[1]
    spect = amps // (wide * LOW)
    count = wide * spect

    view = with_layout_constraint(state.reshape(2, amps // LANES, LANES), PAIRED)
    rows = view.transpose(1, 0, 2).reshape(2 * amps // LANES, LANES)
    gathered = lax.all_to_all(rows, "wide", split_axis=0, concat_axis=0, tiled=True)

    in_hbm = pl.BlockSpec(memory_space=pltpu.HBM)
    in_vmem = pl.BlockSpec(memory_space=pltpu.VMEM)
    in_smem = pl.BlockSpec(memory_space=pltpu.SMEM)
    piece = jax.ShapeDtypeStruct((4 * spect, LANES), jnp.float32)
    part_of_vmem = pltpu.CompilerParams(vmem_limit_bytes=24 * 2**20)
    order = exchange_order(wide)

    turns = (LAYERS + 1, 2, min(spect, 2 ** (PHASE_BITS - LOW_BITS)), LOW)
    gate, half_bit = pl.pallas_call(
        gates_kernel,
        in_specs=[in_vmem, in_vmem, in_smem],
        out_specs=[in_vmem] * 2,
        out_shape=[
            jax.ShapeDtypeStruct((LAYERS, 2, LOW, 2 * GATE), jnp.bfloat16),
            jax.ShapeDtypeStruct((LAYERS, 8, GATE), jnp.int32),
        ],
        compiler_params=part_of_vmem,
        cost_estimate=pl.CostEstimate(flops=10**9, bytes_accessed=4 * 10**6, transcendentals=0),
        name="gates",
    )(gate_re, gate_im, bit_orders)
    turn = pl.pallas_call(
        partial(phases_kernel, spect, narrow),
        in_specs=[in_smem, in_smem, in_vmem],
        out_specs=in_vmem,
        out_shape=jax.ShapeDtypeStruct(turns, jnp.float32),
        compiler_params=part_of_vmem,
        cost_estimate=pl.CostEstimate(flops=10**8, bytes_accessed=10**6, transcendentals=10**5),
        name="phases",
    )(phase_pairs.transpose(0, 2, 1), phase_angles, half_bit)

    def swap(blocks, ks):
        return [
            lax.ppermute(block, "wide", [(i, i ^ k) for i in range(wide)]) if k else block
            for block, k in zip(blocks, ks)
        ]

    done = pl.pallas_call(
        partial(layers_kernel, wide, spect),
        in_specs=[in_vmem] * 4,
        out_specs=[in_vmem] * wide,
        out_shape=[piece] * wide,
        scratch_shapes=[
            pltpu.VMEM((2, 2, count, LOW), jnp.float32),
            pltpu.VMEM((3, count, LOW), jnp.bfloat16),
            pltpu.VMEM((3, count, LOW), jnp.bfloat16),
            pltpu.VMEM((2, 3, LOW, LOW), jnp.bfloat16),
        ],
        compiler_params=part_of_vmem,
        cost_estimate=pl.CostEstimate(flops=5 * 10**9, bytes_accessed=10**7, transcendentals=0),
        name="layers",
    )(gathered, gate, half_bit, turn)

    back = pl.pallas_call(
        partial(place_kernel, wide),
        in_specs=[in_vmem] * wide,
        out_specs=in_hbm,
        out_shape=jax.ShapeDtypeStruct(rows.shape, jnp.float32),
        scratch_shapes=[pltpu.SemaphoreType.DMA((wide,))],
        compiler_params=part_of_vmem,
        name="place",
    )(*swap(done, order))
    view = with_layout_constraint(back.reshape(amps // LANES, 2, LANES).transpose(1, 0, 2), PAIRED)
    return view.reshape(2, amps)


def solution(mesh):
    return jax.shard_map(
        local,
        mesh=mesh,
        in_specs=(P(None, ("wide", "narrow")), P(), P(), P(), P(), P()),
        out_specs=P(None, ("wide", "narrow")),
        check_vma=False,
    )
```

```python
from functools import partial

import jax
import jax.numpy as jnp
from jax import lax
from jax.experimental import pallas as pl
from jax.experimental.layout import Layout, with_layout_constraint
from jax.experimental.pallas import tpu as pltpu
from jax.sharding import PartitionSpec as P

LAYERS = 6
GATE = 128
LOW = 256
LOW_BITS = 8
PHASES = 16
PHASE_BITS = 12
LANES = 128
PACKED = 16
TILE = 128
PAIRED = Layout(major_to_minor=(1, 0, 2))


def split(x):
    high = x.astype(jnp.bfloat16)
    low = (x - high.astype(jnp.float32)).astype(jnp.bfloat16)
    return high, low


def exchange_order(wide):
    far = list(range(wide // 2, wide, 2))
    near = [k for top in (wide // 4, wide // 8) for k in range(top, 2 * top, 2) if top > 1]
    near += [k for k in range(wide // 2 - 2, 0, -2) if k not in near]
    pairs = []
    for i, k in enumerate(far):
        pairs += [k] + near[i : i + 1] * (i < len(near) - 1)
    pairs += near[-1:]
    return [0] + [k + j for k in pairs for j in range(2)] + [1]


def block_of(ref, k, wide):
    rows = ref.shape[0] // wide
    start = (lax.axis_index("wide") ^ k) * rows
    return ref.at[pl.ds(pl.multiple_of(start, rows), rows)]


def gates_kernel(re_ref, im_ref, order_ref, gate_ref, half_ref):
    t = lax.broadcasted_iota(jnp.int32, (8, GATE), 1)
    position = lax.broadcasted_iota(jnp.int32, (LOW // 8, 8, GATE), 0) * 8
    position = position + lax.broadcasted_iota(jnp.int32, (LOW // 8, 8, GATE), 1)
    contract = (((1,), (1,)), ((), ()))
    for layer in range(LAYERS):
        source = jnp.zeros((8, GATE), jnp.int32)
        for bit in range(LOW_BITS - 1):
            source = source + (((t >> bit) & 1) << jnp.full((8, GATE), order_ref[layer, bit], jnp.int32))
        half = jnp.int32(1) << order_ref[layer, LOW_BITS - 1]
        half_ref[layer] = jnp.full((8, GATE), half, jnp.int32)
        hot = jnp.where((position & ~half) == source[None], 1.0, 0.0).reshape(LOW, GATE).astype(jnp.bfloat16)
        for part, ref in enumerate((re_ref, im_ref)):
            for which, piece in enumerate(split(ref[layer])):
                moved = lax.dot_general(hot, piece, contract, preferred_element_type=jnp.float32)
                gate_ref[layer, which, :, part * GATE : (part + 1) * GATE] = moved.astype(jnp.bfloat16)


def phases_kernel(spect, narrow, pair_ref, angle_ref, half_ref, turn_ref):
    size = turn_ref.shape[2]
    row = lax.broadcasted_iota(jnp.int32, (size, LOW), 0)
    lane = lax.broadcasted_iota(jnp.int32, (size, LOW), 1)
    r = lax.axis_index("wide") * (spect // narrow) + row // narrow
    turn_ref[0, 0] = jnp.ones((size, LOW), jnp.float32)
    turn_ref[0, 1] = jnp.zeros((size, LOW), jnp.float32)
    for layer in range(LAYERS):
        b = lax.axis_index("narrow") if layer % 2 == 0 else row % narrow
        u = ((r * narrow + b) * LOW + lane) & (2**PHASE_BITS - 1)
        phase = jnp.zeros((size, LOW), jnp.float32)
        for gate in range(PHASES):
            first = u >> jnp.full((size, LOW), pair_ref[layer, 0, gate], jnp.int32)
            second = u >> jnp.full((size, LOW), pair_ref[layer, 1, gate], jnp.int32)
            phase = phase + jnp.where((first & second & 1) == 1, angle_ref[layer, gate], 0.0)
        turn_ref[layer + 1, 0] = jnp.cos(phase)
        turn_ref[layer + 1, 1] = jnp.sin(phase)


def exchange_modes(rows, span, taken):
    count = len(rows)
    rows = [pltpu.roll(row, m * span, 1) if m else row for m, row in enumerate(rows)]
    for i, mask in enumerate(taken):
        rows = [jnp.where(mask, rows[(y + (1 << i)) % count], rows[y]) for y in range(count)]
    return [pltpu.roll(rows[-r % count], LANES - r * span, 1) if r else rows[0] for r in range(count)]


def place_kernel(wide, *rest):
    blocks, out_hbm, sem = rest[:wide], rest[wide], rest[wide + 1]
    copies = [
        pltpu.make_async_copy(blocks[i], block_of(out_hbm, k, wide), sem.at[i])
        for i, k in enumerate(exchange_order(wide))
    ]
    for copy in copies:
        copy.start()
    for copy in copies:
        copy.wait()


def layers_kernel(wide, spect, x, gate, half_bit, turn, *rest):
    outs = rest[:wide]
    state, left_high, left_low, spread = rest[wide:]
    me = lax.axis_index("wide")
    count = wide * spect
    span = LOW // wide
    half = wide // 2
    rows_at_once = min(spect, PACKED)
    joined = PACKED // rows_at_once
    tile = min(TILE, count // 2)

    for part in range(2):
        for lanes in range(2):
            state[0, part, :, lanes * LANES : (lanes + 1) * LANES] = x[pl.ds(2 * lanes + part, count, stride=4), :]
    lane = lax.broadcasted_iota(jnp.int32, (rows_at_once, LANES), 1)
    taken = [(lane & (span << i)) != 0 for i in range(half.bit_length() - 1)]

    def turned(slot, entry, firsts, offset, lanes):
        lanes = slice(lanes * LANES, (lanes + 1) * LANES)
        cosine, sine = turn[entry, 0, :, lanes], turn[entry, 1, :, lanes]
        pieces = []
        for first in firsts:
            rows = pl.ds(first + offset, rows_at_once)
            real, imag = state[slot, 0, rows, lanes], state[slot, 1, rows, lanes]
            pieces.append((real * cosine - imag * sine, real * sine + imag * cosine))
        return pieces

    position = lax.broadcasted_iota(jnp.int32, (LOW // 8, 8, GATE), 0) * 8
    position = position + lax.broadcasted_iota(jnp.int32, (LOW // 8, 8, GATE), 1)

    def prepare(layer):
        kept = jnp.where((position & half_bit[layer][None]) == 0, 1.0, 0.0).reshape(LOW, GATE).astype(jnp.bfloat16)
        parts = [[gate[layer, which, :, part * GATE : (part + 1) * GATE] for part in range(2)] for which in range(2)]
        total = parts[0][0].astype(jnp.float32) + parts[0][1].astype(jnp.float32)
        total = total + (parts[1][0].astype(jnp.float32) + parts[1][1].astype(jnp.float32))
        for which, piece in enumerate(split(total)):
            for i, values in enumerate(parts[which] + [piece]):
                first = values * kept
                spread[layer % 2, which, i] = jnp.concatenate([first, values - first], axis=1)

    def load(layer, lanes, top, offset):
        slot = layer % 2
        pieces = turned(slot, layer, [(top * half + m) * spect for m in range(half)], offset, lanes)
        reals, imags = (exchange_modes([piece[part] for piece in pieces], span, taken) for part in range(2))
        for g in range(0, half, joined):
            at = (lanes * half + g) * spect + offset
            real = jnp.concatenate(reals[g : g + joined], axis=0)
            imag = jnp.concatenate(imags[g : g + joined], axis=0)
            for i, values in enumerate((real, imag, real + imag)):
                high, low = split(values)
                left_high[slot, i, at : at + PACKED, top * LANES : (top + 1) * LANES] = high
                left_low[slot, i, at : at + PACKED, top * LANES : (top + 1) * LANES] = low

    def product(layer, i, rows):
        slot = layer % 2
        high, low = left_high[slot, i, rows], left_low[slot, i, rows]
        square = jnp.concatenate([spread[slot, 0, i], spread[slot, 0, i], spread[slot, 1, i]], axis=0)
        return jnp.dot(jnp.concatenate([high, low, high], axis=1), square, preferred_element_type=jnp.float32)

    def multiply(layer, first):
        rows = slice(first, first + tile)
        real, imag = product(layer, 0, rows), product(layer, 1, rows)
        state[1 - layer % 2, 0, rows] = real - imag
        state[1 - layer % 2, 1, rows] = product(layer, 2, rows) - (real + imag)

    def in_turn(products, loads):
        for i, args in enumerate(products):
            multiply(*args)
            for more in loads[i * len(loads) // len(products) : (i + 1) * len(loads) // len(products)]:
                load(*more)

    offsets = range(0, spect, rows_at_once)
    tiles = range(0, count, tile)
    prepare(0)
    for args in [(0, lanes, 0, offset) for lanes in range(2) for offset in offsets]:
        load(*args)
    for layer in range(LAYERS):
        for offset in offsets:
            load(layer, 0, 1, offset)
        in_turn([(layer, first) for first in tiles if first < count // 2], [(layer, 1, 1, offset) for offset in offsets])
        ahead = []
        if layer + 1 < LAYERS:
            prepare(layer + 1)
            ahead = [(layer + 1, lanes, 0, offset) for lanes in range(2) for offset in offsets]
        in_turn([(layer, first) for first in tiles if first >= count // 2], ahead)

    firsts = [pl.multiple_of((me ^ k) * spect, spect) for k in exchange_order(wide)]
    for offset in range(0, spect, rows_at_once):
        for lanes in range(2):
            for i, pieces in enumerate(turned(0, LAYERS, firsts, offset, lanes)):
                for part, piece in enumerate(pieces):
                    outs[i][pl.ds(4 * offset + 2 * lanes + part, rows_at_once, stride=4), :] = piece


def local(state, gate_re, gate_im, bit_orders, phase_pairs, phase_angles):
    wide = lax.axis_size("wide")
    narrow = lax.axis_size("narrow")
    amps = state.shape[1]
    spect = amps // (wide * LOW)
    count = wide * spect

    view = with_layout_constraint(state.reshape(2, amps // LANES, LANES), PAIRED)
    rows = view.transpose(1, 0, 2).reshape(2 * amps // LANES, LANES)
    gathered = lax.all_to_all(rows, "wide", split_axis=0, concat_axis=0, tiled=True)

    in_hbm = pl.BlockSpec(memory_space=pltpu.HBM)
    in_vmem = pl.BlockSpec(memory_space=pltpu.VMEM)
    in_smem = pl.BlockSpec(memory_space=pltpu.SMEM)
    piece = jax.ShapeDtypeStruct((4 * spect, LANES), jnp.float32)
    part_of_vmem = pltpu.CompilerParams(vmem_limit_bytes=24 * 2**20)
    order = exchange_order(wide)

    turns = (LAYERS + 1, 2, min(spect, 2 ** (PHASE_BITS - LOW_BITS)), LOW)
    gate, half_bit = pl.pallas_call(
        gates_kernel,
        in_specs=[in_vmem, in_vmem, in_smem],
        out_specs=[in_vmem] * 2,
        out_shape=[
            jax.ShapeDtypeStruct((LAYERS, 2, LOW, 2 * GATE), jnp.bfloat16),
            jax.ShapeDtypeStruct((LAYERS, 8, GATE), jnp.int32),
        ],
        compiler_params=part_of_vmem,
        cost_estimate=pl.CostEstimate(flops=10**9, bytes_accessed=4 * 10**6, transcendentals=0),
        name="gates",
    )(gate_re, gate_im, bit_orders)
    turn = pl.pallas_call(
        partial(phases_kernel, spect, narrow),
        in_specs=[in_smem, in_smem, in_vmem],
        out_specs=in_vmem,
        out_shape=jax.ShapeDtypeStruct(turns, jnp.float32),
        compiler_params=part_of_vmem,
        cost_estimate=pl.CostEstimate(flops=10**8, bytes_accessed=10**6, transcendentals=10**5),
        name="phases",
    )(phase_pairs.transpose(0, 2, 1), phase_angles, half_bit)

    def swap(blocks, ks):
        return [
            lax.ppermute(block, "wide", [(i, i ^ k) for i in range(wide)]) if k else block
            for block, k in zip(blocks, ks)
        ]

    done = pl.pallas_call(
        partial(layers_kernel, wide, spect),
        in_specs=[in_vmem] * 4,
        out_specs=[in_vmem] * wide,
        out_shape=[piece] * wide,
        scratch_shapes=[
            pltpu.VMEM((2, 2, count, LOW), jnp.float32),
            pltpu.VMEM((2, 3, count, LOW), jnp.bfloat16),
            pltpu.VMEM((2, 3, count, LOW), jnp.bfloat16),
            pltpu.VMEM((2, 2, 3, LOW, LOW), jnp.bfloat16),
        ],
        compiler_params=part_of_vmem,
        cost_estimate=pl.CostEstimate(flops=5 * 10**9, bytes_accessed=10**7, transcendentals=0),
        name="layers",
    )(gathered, gate, half_bit, turn)

    back = pl.pallas_call(
        partial(place_kernel, wide),
        in_specs=[in_vmem] * wide,
        out_specs=in_hbm,
        out_shape=jax.ShapeDtypeStruct(rows.shape, jnp.float32),
        scratch_shapes=[pltpu.SemaphoreType.DMA((wide,))],
        compiler_params=part_of_vmem,
        name="place",
    )(*swap(done, order))
    view = with_layout_constraint(back.reshape(amps // LANES, 2, LANES).transpose(1, 0, 2), PAIRED)
    return view.reshape(2, amps)


def solution(mesh):
    return jax.shard_map(
        local,
        mesh=mesh,
        in_specs=(P(None, ("wide", "narrow")), P(), P(), P(), P(), P()),
        out_specs=P(None, ("wide", "narrow")),
        check_vma=False,
    )
```

```python
from functools import partial

import jax
import jax.numpy as jnp
from jax import lax
from jax.experimental import pallas as pl
from jax.experimental.layout import Layout, with_layout_constraint
from jax.experimental.pallas import tpu as pltpu
from jax.sharding import PartitionSpec as P

LAYERS = 6
GATE = 128
LOW = 256
LOW_BITS = 8
PHASES = 16
PHASE_BITS = 12
LANES = 128
PACKED = 16
TILE = 128
PAIRED = Layout(major_to_minor=(1, 0, 2))


def split(x):
    high = x.astype(jnp.bfloat16)
    low = (x - high.astype(jnp.float32)).astype(jnp.bfloat16)
    return high, low


def exchange_order(wide):
    far = list(range(wide // 2, wide, 2))
    near = [k for top in (wide // 4, wide // 8) for k in range(top, 2 * top, 2) if top > 1]
    near += [k for k in range(wide // 2 - 2, 0, -2) if k not in near]
    pairs = []
    for i, k in enumerate(far):
        pairs += [k] + near[i : i + 1] * (i < len(near) - 1)
    pairs += near[-1:]
    return [0] + [k + j for k in pairs for j in range(2)] + [1]


def block_of(ref, k, wide):
    rows = ref.shape[0] // wide
    start = (lax.axis_index("wide") ^ k) * rows
    return ref.at[pl.ds(pl.multiple_of(start, rows), rows)]


def gates_kernel(re_ref, im_ref, order_ref, gate_ref, half_ref):
    t = lax.broadcasted_iota(jnp.int32, (8, GATE), 1)
    position = lax.broadcasted_iota(jnp.int32, (LOW // 8, 8, GATE), 0) * 8
    position = position + lax.broadcasted_iota(jnp.int32, (LOW // 8, 8, GATE), 1)
    contract = (((1,), (1,)), ((), ()))
    for layer in range(LAYERS):
        source = jnp.zeros((8, GATE), jnp.int32)
        for bit in range(LOW_BITS - 1):
            source = source + (((t >> bit) & 1) << jnp.full((8, GATE), order_ref[layer, bit], jnp.int32))
        half = jnp.int32(1) << order_ref[layer, LOW_BITS - 1]
        half_ref[layer] = jnp.full((8, GATE), half, jnp.int32)
        hot = jnp.where((position & ~half) == source[None], 1.0, 0.0).reshape(LOW, GATE).astype(jnp.bfloat16)
        for part, ref in enumerate((re_ref, im_ref)):
            for which, piece in enumerate(split(ref[layer])):
                moved = lax.dot_general(hot, piece, contract, preferred_element_type=jnp.float32)
                gate_ref[layer, which, :, part * GATE : (part + 1) * GATE] = moved.astype(jnp.bfloat16)


def phases_kernel(spect, narrow, pair_ref, angle_ref, half_ref, turn_ref):
    size = turn_ref.shape[2]
    row = lax.broadcasted_iota(jnp.int32, (size, LOW), 0)
    lane = lax.broadcasted_iota(jnp.int32, (size, LOW), 1)
    r = lax.axis_index("wide") * (spect // narrow) + row // narrow
    turn_ref[0, 0] = jnp.ones((size, LOW), jnp.float32)
    turn_ref[0, 1] = jnp.zeros((size, LOW), jnp.float32)
    for layer in range(LAYERS):
        b = lax.axis_index("narrow") if layer % 2 == 0 else row % narrow
        u = ((r * narrow + b) * LOW + lane) & (2**PHASE_BITS - 1)
        phase = jnp.zeros((size, LOW), jnp.float32)
        for gate in range(PHASES):
            first = u >> jnp.full((size, LOW), pair_ref[layer, 0, gate], jnp.int32)
            second = u >> jnp.full((size, LOW), pair_ref[layer, 1, gate], jnp.int32)
            phase = phase + jnp.where((first & second & 1) == 1, angle_ref[layer, gate], 0.0)
        turn_ref[layer + 1, 0] = jnp.cos(phase)
        turn_ref[layer + 1, 1] = jnp.sin(phase)


def exchange_modes(rows, span, taken):
    count = len(rows)
    rows = [pltpu.roll(row, m * span, 1) if m else row for m, row in enumerate(rows)]
    for i, mask in enumerate(taken):
        rows = [jnp.where(mask, rows[(y + (1 << i)) % count], rows[y]) for y in range(count)]
    return [pltpu.roll(rows[-r % count], LANES - r * span, 1) if r else rows[0] for r in range(count)]


def place_kernel(wide, *rest):
    blocks, out_hbm, sem = rest[:wide], rest[wide], rest[wide + 1]
    copies = [
        pltpu.make_async_copy(blocks[i], block_of(out_hbm, k, wide), sem.at[i])
        for i, k in enumerate(exchange_order(wide))
    ]
    for copy in copies:
        copy.start()
    for copy in copies:
        copy.wait()


def layers_kernel(wide, spect, x, gate, half_bit, turn, *rest):
    outs = rest[:wide]
    state, left_high, left_low, spread = rest[wide:]
    me = lax.axis_index("wide")
    count = wide * spect
    span = LOW // wide
    half = wide // 2
    rows_at_once = min(spect, PACKED)
    joined = PACKED // rows_at_once
    tile = min(TILE, count // 2)

    lane = lax.broadcasted_iota(jnp.int32, (rows_at_once, LANES), 1)
    taken = [(lane & (span << i)) != 0 for i in range(half.bit_length() - 1)]

    def turned(slot, entry, firsts, offset, lanes):
        lanes = slice(lanes * LANES, (lanes + 1) * LANES)
        cosine, sine = turn[entry, 0, :, lanes], turn[entry, 1, :, lanes]
        pieces = []
        for first in firsts:
            rows = pl.ds(first + offset, rows_at_once)
            real, imag = state[slot, 0, rows, lanes], state[slot, 1, rows, lanes]
            pieces.append((real * cosine - imag * sine, real * sine + imag * cosine))
        return pieces

    position = lax.broadcasted_iota(jnp.int32, (LOW // 8, 8, GATE), 0) * 8
    position = position + lax.broadcasted_iota(jnp.int32, (LOW // 8, 8, GATE), 1)

    def prepare(layer):
        kept = jnp.where((position & half_bit[layer][None]) == 0, 1.0, 0.0).reshape(LOW, GATE).astype(jnp.bfloat16)
        parts = [[gate[layer, which, :, part * GATE : (part + 1) * GATE] for part in range(2)] for which in range(2)]
        total = parts[0][0].astype(jnp.float32) + parts[0][1].astype(jnp.float32)
        total = total + (parts[1][0].astype(jnp.float32) + parts[1][1].astype(jnp.float32))
        for which, piece in enumerate(split(total)):
            for i, values in enumerate(parts[which] + [piece]):
                first = values * kept
                spread[layer % 2, which, i] = jnp.concatenate([first, values - first], axis=1)

    def load(layer, lanes, top, offset):
        slot = layer % 2
        firsts = [(top * half + m) * spect for m in range(half)]
        if layer:
            pieces = turned(slot, layer, firsts, offset, lanes)
        else:
            starts = [4 * (first + offset) + 2 * lanes for first in firsts]
            pieces = [[x[pl.ds(start + part, rows_at_once, stride=4), :] for part in range(2)] for start in starts]
        reals, imags = (exchange_modes([piece[part] for piece in pieces], span, taken) for part in range(2))
        for g in range(0, half, joined):
            at = (lanes * half + g) * spect + offset
            real = jnp.concatenate(reals[g : g + joined], axis=0)
            imag = jnp.concatenate(imags[g : g + joined], axis=0)
            for i, values in enumerate((real, imag, real + imag)):
                high, low = split(values)
                left_high[slot, i, at : at + PACKED, top * LANES : (top + 1) * LANES] = high
                left_low[slot, i, at : at + PACKED, top * LANES : (top + 1) * LANES] = low

    def product(layer, i, rows):
        slot = layer % 2
        high, low = left_high[slot, i, rows], left_low[slot, i, rows]
        square = jnp.concatenate([spread[slot, 0, i], spread[slot, 0, i], spread[slot, 1, i]], axis=0)
        return jnp.dot(jnp.concatenate([high, low, high], axis=1), square, preferred_element_type=jnp.float32)

    def multiply(layer, first):
        rows = slice(first, first + tile)
        real, imag = product(layer, 0, rows), product(layer, 1, rows)
        state[1 - layer % 2, 0, rows] = real - imag
        state[1 - layer % 2, 1, rows] = product(layer, 2, rows) - (real + imag)

    def in_turn(products, loads):
        for i, args in enumerate(products):
            multiply(*args)
            for more in loads[i * len(loads) // len(products) : (i + 1) * len(loads) // len(products)]:
                load(*more)

    offsets = range(0, spect, rows_at_once)
    tiles = range(0, count, tile)
    prepare(0)
    for args in [(0, lanes, 0, offset) for lanes in range(2) for offset in offsets]:
        load(*args)
    for layer in range(LAYERS):
        for offset in offsets:
            load(layer, 0, 1, offset)
        in_turn([(layer, first) for first in tiles if first < count // 2], [(layer, 1, 1, offset) for offset in offsets])
        ahead = []
        if layer + 1 < LAYERS:
            prepare(layer + 1)
            ahead = [(layer + 1, lanes, 0, offset) for lanes in range(2) for offset in offsets]
        in_turn([(layer, first) for first in tiles if first >= count // 2], ahead)

    firsts = [pl.multiple_of((me ^ k) * spect, spect) for k in exchange_order(wide)]
    for offset in range(0, spect, rows_at_once):
        for lanes in range(2):
            for i, pieces in enumerate(turned(0, LAYERS, firsts, offset, lanes)):
                for part, piece in enumerate(pieces):
                    outs[i][pl.ds(4 * offset + 2 * lanes + part, rows_at_once, stride=4), :] = piece


def local(state, gate_re, gate_im, bit_orders, phase_pairs, phase_angles):
    wide = lax.axis_size("wide")
    narrow = lax.axis_size("narrow")
    amps = state.shape[1]
    spect = amps // (wide * LOW)
    count = wide * spect

    view = with_layout_constraint(state.reshape(2, amps // LANES, LANES), PAIRED)
    rows = view.transpose(1, 0, 2).reshape(2 * amps // LANES, LANES)
    gathered = lax.all_to_all(rows, "wide", split_axis=0, concat_axis=0, tiled=True)

    in_hbm = pl.BlockSpec(memory_space=pltpu.HBM)
    in_vmem = pl.BlockSpec(memory_space=pltpu.VMEM)
    in_smem = pl.BlockSpec(memory_space=pltpu.SMEM)
    piece = jax.ShapeDtypeStruct((4 * spect, LANES), jnp.float32)
    part_of_vmem = pltpu.CompilerParams(vmem_limit_bytes=24 * 2**20)
    order = exchange_order(wide)

    turns = (LAYERS + 1, 2, min(spect, 2 ** (PHASE_BITS - LOW_BITS)), LOW)
    gate, half_bit = pl.pallas_call(
        gates_kernel,
        in_specs=[in_vmem, in_vmem, in_smem],
        out_specs=[in_vmem] * 2,
        out_shape=[
            jax.ShapeDtypeStruct((LAYERS, 2, LOW, 2 * GATE), jnp.bfloat16),
            jax.ShapeDtypeStruct((LAYERS, 8, GATE), jnp.int32),
        ],
        compiler_params=part_of_vmem,
        cost_estimate=pl.CostEstimate(flops=10**9, bytes_accessed=4 * 10**6, transcendentals=0),
        name="gates",
    )(gate_re, gate_im, bit_orders)
    turn = pl.pallas_call(
        partial(phases_kernel, spect, narrow),
        in_specs=[in_smem, in_smem, in_vmem],
        out_specs=in_vmem,
        out_shape=jax.ShapeDtypeStruct(turns, jnp.float32),
        compiler_params=part_of_vmem,
        cost_estimate=pl.CostEstimate(flops=10**8, bytes_accessed=10**6, transcendentals=10**5),
        name="phases",
    )(phase_pairs.transpose(0, 2, 1), phase_angles, half_bit)

    def swap(blocks, ks):
        return [
            lax.ppermute(block, "wide", [(i, i ^ k) for i in range(wide)]) if k else block
            for block, k in zip(blocks, ks)
        ]

    done = pl.pallas_call(
        partial(layers_kernel, wide, spect),
        in_specs=[in_vmem] * 4,
        out_specs=[in_vmem] * wide,
        out_shape=[piece] * wide,
        scratch_shapes=[
            pltpu.VMEM((2, 2, count, LOW), jnp.float32),
            pltpu.VMEM((2, 3, count, LOW), jnp.bfloat16),
            pltpu.VMEM((2, 3, count, LOW), jnp.bfloat16),
            pltpu.VMEM((2, 2, 3, LOW, LOW), jnp.bfloat16),
        ],
        compiler_params=part_of_vmem,
        cost_estimate=pl.CostEstimate(flops=5 * 10**9, bytes_accessed=10**7, transcendentals=0),
        name="layers",
    )(gathered, gate, half_bit, turn)

    back = pl.pallas_call(
        partial(place_kernel, wide),
        in_specs=[in_vmem] * wide,
        out_specs=in_hbm,
        out_shape=jax.ShapeDtypeStruct(rows.shape, jnp.float32),
        scratch_shapes=[pltpu.SemaphoreType.DMA((wide,))],
        compiler_params=part_of_vmem,
        name="place",
    )(*swap(done, order))
    view = with_layout_constraint(back.reshape(amps // LANES, 2, LANES).transpose(1, 0, 2), PAIRED)
    return view.reshape(2, amps)


def solution(mesh):
    return jax.shard_map(
        local,
        mesh=mesh,
        in_specs=(P(None, ("wide", "narrow")), P(), P(), P(), P(), P()),
        out_specs=P(None, ("wide", "narrow")),
        check_vma=False,
    )
```
